128 devices in a mesh: dp: 16 (over y, x_hi, core), mp: 8 (over z, x_lo).
Axes of the slice: x: 4 (x_hi: 2, x_lo: 2; x = x_hi * 2 + x_lo), y: 4, z: 4, core: 2. Of those that a mesh axis runs over, the one named last changes fastest.
Arguments:
- block_input: bfloat16 [32768, 1024], P(('dp', 'mp')), may hold values from -6 to 6
- first_values: bfloat16 [32768, 1024], P('dp', 'mp'), may hold values from -6 to 6
- out_cotangent: bfloat16 [32768, 1024], P(('dp', 'mp')), may hold values from -10 to 10
- doc_lengths: int32 [16, 4], P('dp'), may hold values from 1 to 1793, 2048 in all within a row
- norm_gains: float32 [2, 1024], replicated, may hold values from 0.5 to 1.5
- gain_moment1: float32 [2, 1024], replicated, may hold values from -448 to 448
- gain_moment2: float32 [2, 1024], replicated, may hold values from 22937.6 to 91750.4
- qkv_weight: float32 [1024, 3, 1024], P('dp', None, 'mp'), may hold values from -0.1875 to 0.1875
- qkv_momentum: float32 [1024, 3, 1024], P('dp', None, 'mp'), may hold values from -1024 to 1024
- out_weight: float32 [1024, 1024], P('mp', 'dp'), may hold values from -2 to 2
- out_momentum: float32 [1024, 1024], P('mp', 'dp'), may hold values from -112 to 112
- gate_up_weight: float32 [1024, 2, 2816], P('dp', None, 'mp'), may hold values from -0.1875 to 0.1875
- gate_up_momentum: float32 [1024, 2, 2816], P('dp', None, 'mp'), may hold values from -320 to 320
- down_weight: float32 [2816, 1024], P('mp', 'dp'), may hold values from -0.109375 to 0.109375
- down_momentum: float32 [2816, 1024], P('mp', 'dp'), may hold values from -512 to 512
Outputs:
- block_output: bfloat16 [32768, 1024], P(('dp', 'mp'))
- input_grad: float32 [32768, 1024], P(('dp', 'mp'))
- first_values_grad: float32 [32768, 1024], P('dp', 'mp')
- qkv_weight_new: float32 [1024, 3, 1024], P('dp', None, 'mp')
- qkv_momentum_new: float32 [1024, 3, 1024], P('dp', None, 'mp')
- out_weight_new: float32 [1024, 1024], P('mp', 'dp')
- out_momentum_new: float32 [1024, 1024], P('mp', 'dp')
- gate_up_weight_new: float32 [1024, 2, 2816], P('dp', None, 'mp')
- gate_up_momentum_new: float32 [1024, 2, 2816], P('dp', None, 'mp')
- down_weight_new: float32 [2816, 1024], P('mp', 'dp')
- down_momentum_new: float32 [2816, 1024], P('mp', 'dp')
- gain_moment1_new: float32 [2, 1024], replicated
- gain_moment2_new: float32 [2, 1024], replicated
- norm_gains_new: float32 [2, 1024], replicated
The draws below stay inside these ranges and needn't reach their ends.
Inputs may be any that keep to these rules, and one draw needn't show every extreme that they name: `doc_lengths`: each row's lengths sum to 2048, and one document of every row has exactly the largest value.
All inputs are finite; a program needn't handle non-finite values.
Results may differ from the reference program's by a relative error of at most 0.028.
Values may be sent and summed in bfloat16 or wider, within the bound.
A program may use at most 128 MiB of HBM per device.

```python
import math
import jax
import jax.numpy as jnp
import numpy as np
from jax import lax

D = 1024
HEADS = 16
HD = 64
FF = 2816
LEN = 2048
NDOC = 4
STEP = 10
ROWS = 16
TOKENS = 32768
N_MP = 8


def draw_out_cotangent(key, part):
    key = jax.random.fold_in(key, 3)
    sample = jnp.clip(jax.random.normal(key, (TOKENS, D), jnp.float32), -4.0, 4.0)
    growth = 3.0
    fraction = jnp.arange(TOKENS, dtype=jnp.float32) / max(TOKENS - 1, 1)
    row_scale = growth ** (fraction - 0.5)
    return (sample * row_scale[:, None]).astype(jnp.bfloat16)


def block_levels(stream_key, shape, split, least, high):
    factor_of, own = 1.0, jax.random.fold_in(stream_key, 6)
    for dim, blocks in split:
        heights = jnp.exp(jax.random.uniform(jax.random.fold_in(own, dim), (blocks,), jnp.float32, least / len(split), high / len(split)))
        factor_of = factor_of * jnp.repeat(heights, shape[dim] // blocks).reshape([-1 if axis == dim else 1 for axis in range(len(shape))])
    return factor_of


def profile(number_of, total, limit, lean):
    portions = [(1 << 20) // math.isqrt(standing ** lean) + 1 for standing in range(2, number_of + 1)]
    surplus, counts = total - limit - (number_of - 1), [1] * (number_of - 1)
    while surplus > 0:
        movable = [i for i in range(number_of - 1) if counts[i] < limit]
        pool, budget = sum([portions[i] for i in movable]), surplus
        for i in movable:
            extra = min(limit - counts[i], max(1, budget * portions[i] // pool), surplus)
            counts[i] = counts[i] + extra
            surplus = surplus - extra
    return np.array([limit] + counts)


def uneven(stream_key, amount, total, reach, skew):
    if amount == 2:
        one = jax.random.randint(stream_key, (), max(1, total - reach), min(reach, total - 1) + 1)
        return jnp.stack([one, total - one])
    sizes = jnp.asarray(profile(amount, total, reach, skew), jnp.int32)
    twos = (amount - 1) // 2
    donor, receiver = sizes[1:1 + 2 * twos:2], sizes[2:2 + 2 * twos:2]
    margin = jnp.minimum(donor - 1, reach - receiver)
    moved = jax.random.randint(jax.random.fold_in(stream_key, 1), (twos,), 0, 1 << 20) % (margin + 1)
    sizes = sizes.at[1:1 + 2 * twos:2].set(donor - moved).at[2:2 + 2 * twos:2].set(receiver + moved)
    return sizes[jax.random.permutation(jax.random.fold_in(stream_key, 2), amount)]


def centred(stream_key, extent, spread, bound, shards=(), held_as=jnp.bfloat16):
    drawn = jax.random.normal(stream_key, extent, jnp.float32) * spread
    if len(shards) > 0:
        drawn = block_levels(stream_key, extent, shards, -0.22, 0.18) * drawn
    return jnp.clip(drawn, min=-bound, max=bound).astype(held_as)


def setup_inputs(seed: int = 0) -> dict:
    key_of = jax.random.split(jax.random.key(seed), 16)
    block_input = centred(key_of[0], (TOKENS, D), 1.0, 6.0, ((0, 128),))
    first_values = centred(key_of[1], (TOKENS, D), 1.0, 6.0, ((0, 16), (1, 8)))
    out_cotangent = draw_out_cotangent(jax.random.fold_in(key_of[15], 71), 0)
    doc_lengths = jax.vmap(lambda own: uneven(own, NDOC, LEN, LEN - LEN // N_MP + 1, 2))(jax.random.split(key_of[3], ROWS)).reshape((ROWS, NDOC)).astype(jnp.int32)
    norm_gains = jnp.clip(1.0 + 0.1 * jax.random.normal(key_of[4], (2, D), jnp.float32), 0.5, 1.5)
    gain_moment1 = centred(key_of[5], (2, D), (0.4 * TOKENS ** 0.5), 448.0, (), jnp.float32)
    gain_moment2 = jnp.clip(jnp.exp(jax.random.uniform(key_of[6], (2, D), jnp.float32, math.log(22937.6), math.log(91750.4))), 22937.6, 91750.4)
    qkv_weight = centred(key_of[7], (D, 3, D), D ** -0.5, 0.1875, ((0, 16), (2, 8)), jnp.float32)
    qkv_momentum = centred(key_of[8], (D, 3, D), (1.0 * TOKENS ** 0.5), 1024.0, ((0, 16), (2, 8)), jnp.float32)
    out_weight = centred(key_of[9], (D, D), (max(HD // 8, 1)) ** -0.5, 2.0, ((0, 8), (1, 16)), jnp.float32)
    out_momentum = centred(key_of[10], (D, D), (0.1 * TOKENS ** 0.5), 112.0, ((0, 8), (1, 16)), jnp.float32)
    gate_up_weight = centred(key_of[11], (D, 2, FF), D ** -0.5, 0.1875, ((0, 16), (2, 8)), jnp.float32)
    gate_up_momentum = centred(key_of[12], (D, 2, FF), (0.3 * TOKENS ** 0.5), 320.0, ((0, 16), (2, 8)), jnp.float32)
    down_weight = centred(key_of[13], (FF, D), FF ** -0.5, 0.109375, ((0, 8), (1, 16)), jnp.float32)
    down_momentum = centred(key_of[14], (FF, D), (0.5 * TOKENS ** 0.5), 512.0, ((0, 8), (1, 16)), jnp.float32)
    return dict(block_input=block_input, first_values=first_values, out_cotangent=out_cotangent, doc_lengths=doc_lengths, norm_gains=norm_gains, gain_moment1=gain_moment1, gain_moment2=gain_moment2, qkv_weight=qkv_weight, qkv_momentum=qkv_momentum, out_weight=out_weight, out_momentum=out_momentum, gate_up_weight=gate_up_weight, gate_up_momentum=gate_up_momentum, down_weight=down_weight, down_momentum=down_momentum)


@jax.custom_vjp
def low(v):
    return lax.optimization_barrier(v.astype(jnp.bfloat16)).astype(jnp.float32)

@jax.custom_vjp
def low_back(v):
    return v

def low_keep(v):
    return (low(v), None)

def low_pass(kept, grad):
    return (grad,)

def back_keep(v):
    return (v, None)

def back_low(kept, grad):
    return (low(grad),)
low.defvjp(low_keep, low_pass)
low_back.defvjp(back_keep, back_low)
norm_epsilon = 1e-06
newton_a = 3.4445
newton_b = -4.775
newton_c = 2.0315
muon_rate = 1.0
out_rate = 4.0
adam_rate = 0.8
beta_first = 0.9
beta_second = 0.95
adam_epsilon = 1e-08
mask_fill = -1e+30

def precise(left, right):
    return jnp.dot(left, right, precision=lax.Precision.HIGHEST, preferred_element_type=jnp.float32)

def orthogonal(moment):
    row_total, col_total = moment.shape
    iterate = moment / (jnp.sqrt(jnp.sum(moment * moment)) + 1e-07)
    if row_total > col_total:
        iterate = iterate.T
    for sweep in range(5):
        gram = precise(iterate, iterate.T)
        poly = newton_b * gram + newton_c * precise(gram, gram)
        iterate = newton_a * iterate + precise(poly, iterate)
    if row_total > col_total:
        iterate = iterate.T
    return iterate * max(1.0, row_total / col_total) ** 0.5

def doc_tables(lengths):
    doc_ends = jnp.cumsum(lengths, dtype=jnp.int32)
    starts = (doc_ends - lengths).astype(jnp.int32)
    places = jnp.arange(LEN, dtype=jnp.int32)
    doc_ids = lax.optimization_barrier(jnp.sum((places[:, None] >= doc_ends[None, :]).astype(jnp.int32), axis=1))
    doc_begin = lax.optimization_barrier(jnp.max(jnp.where(starts[None, :] <= places[:, None], starts[None, :], 0), axis=1))
    return (doc_ids.astype(jnp.int32), (places - doc_begin).astype(jnp.int32))

def rotation(positions):
    half_dim = HD // 2
    frequency = jnp.exp(-jnp.log(10000.0) * jnp.arange(half_dim, dtype=jnp.float32) * 2.0 / HD)
    angles = positions.astype(jnp.float32)[:, None] * frequency[None, :]
    return (jnp.cos(angles), jnp.sin(angles))

def rotate(vectors, cosine, sine_part):
    half_dim = HD // 2
    front_half = vectors[..., :half_dim]
    back_half = vectors[..., half_dim:]
    cos_b = cosine[:, None, :]
    sin_b = sine_part[:, None, :]
    return jnp.concatenate([front_half * cos_b - back_half * sin_b, back_half * cos_b + front_half * sin_b], axis=-1)

def attention(queries, key_rows, values_mix, doc_ids):
    block_rows = min(512, LEN)
    places = jnp.arange(LEN, dtype=jnp.int32)

    def one_block(offset):
        q_block = lax.dynamic_slice_in_dim(queries, offset, block_rows, 0)
        row_ids = lax.dynamic_slice_in_dim(places, offset, block_rows, 0)
        doc_block = lax.dynamic_slice_in_dim(doc_ids, offset, block_rows, 0)
        scores = jnp.einsum('qhc,khc->hqk', q_block, key_rows, precision=lax.Precision.HIGHEST) * HD ** (-0.5)
        scores = low_back(scores)
        allowed = (row_ids[:, None] >= places[None, :]) & (doc_block[:, None] == doc_ids[None, :])
        scores = jnp.where(allowed[None], scores, mask_fill)
        row_top = lax.optimization_barrier(jnp.max(scores, axis=-1, keepdims=True))
        weights = jnp.exp(scores - row_top)
        probability = weights / lax.optimization_barrier(jnp.sum(weights, axis=-1, keepdims=True))
        return jnp.einsum('hqk,khc->qhc', low(probability), values_mix, precision=lax.Precision.HIGHEST)
    offsets = jnp.arange(LEN // block_rows, dtype=jnp.int32) * block_rows
    blocks_out = lax.map(jax.checkpoint(one_block), offsets)
    return blocks_out.reshape(LEN, HEADS * HD)

def row_forward(weights, row_data):
    w_qkv, w_out, w_gate_up, w_down, norm_gains = weights
    stream, first_values, lengths = row_data
    doc_ids, positions = doc_tables(lengths)
    cosine, sine_part = rotation(positions)
    inverse_one = lax.rsqrt(lax.optimization_barrier(jnp.mean(stream * stream, axis=-1, keepdims=True)) + norm_epsilon)
    normed_one = low(stream * inverse_one * norm_gains[0])
    qkv_proj = low_back(jnp.einsum('td,dkc->tkc', normed_one, w_qkv, precision=lax.Precision.HIGHEST))
    queries = low(rotate(qkv_proj[:, 0].reshape(LEN, HEADS, HD), cosine, sine_part))
    key_rows = low(rotate(qkv_proj[:, 1].reshape(LEN, HEADS, HD), cosine, sine_part))
    values_mix = low(0.5 * qkv_proj[:, 2] + 0.5 * first_values).reshape(LEN, HEADS, HD)
    heads_out = low(low_back(attention(queries, key_rows, values_mix, doc_ids)))
    share_width = D // N_MP
    partials = jnp.einsum('tmc,mcd->mtd', heads_out.reshape(LEN, N_MP, share_width), w_out.reshape(N_MP, share_width, D), precision=lax.Precision.HIGHEST)
    attn_branch = low_back(lax.optimization_barrier(jnp.sum(low(partials), axis=0)))
    residual = stream + attn_branch
    inverse_two = lax.rsqrt(lax.optimization_barrier(jnp.mean(residual * residual, axis=-1, keepdims=True)) + norm_epsilon)
    normed_two = low(residual * inverse_two * norm_gains[1])
    gate_up = low_back(jnp.einsum('td,dkf->tkf', normed_two, w_gate_up, precision=lax.Precision.HIGHEST))
    hidden = low(jax.nn.silu(gate_up[:, 0]) * gate_up[:, 1])
    ff_share = FF // N_MP
    ffn_partials = jnp.einsum('tmf,mfd->mtd', hidden.reshape(LEN, N_MP, ff_share), w_down.reshape(N_MP, ff_share, D), precision=lax.Precision.HIGHEST)
    ffn_branch = low_back(lax.optimization_barrier(jnp.sum(low(ffn_partials), axis=0)))
    return residual + ffn_branch

def make_forward(doc_lengths):

    def forward(stream, first_values, w_qkv, w_out, w_gate_up, w_down, norm_gains):
        weights = (low(w_qkv), low(w_out), low(w_gate_up), low(w_down), norm_gains)
        row_total = stream.shape[0] // LEN

        def row_step(unused_carry, row_data):
            return (unused_carry, row_forward(weights, row_data))
        unused, rows_out = lax.scan(row_step, jnp.zeros((), jnp.float32), (stream.reshape(row_total, LEN, D), first_values.reshape(row_total, LEN, D), doc_lengths))
        return rows_out.reshape(row_total * LEN, D)
    return forward

def reference(block_input, first_values, out_cotangent, doc_lengths, norm_gains, gain_moment1, gain_moment2, qkv_weight, qkv_momentum, out_weight, out_momentum, gate_up_weight, gate_up_momentum, down_weight, down_momentum):
    forward = make_forward(doc_lengths)
    outputs, pullback = jax.vjp(forward, block_input.astype(jnp.float32), first_values.astype(jnp.float32), qkv_weight, out_weight, gate_up_weight, down_weight, norm_gains)
    input_grad, values_grad, grad_qkv, grad_out, grad_gate_up, grad_down, gain_grad = pullback(out_cotangent.astype(jnp.float32))
    qkv_moment_new = 0.5 * qkv_momentum + grad_qkv
    out_moment_new = 0.5 * out_momentum + grad_out
    gate_up_moment_new = 0.5 * gate_up_momentum + grad_gate_up
    down_moment_new = 0.5 * down_momentum + grad_down
    share_width = D // N_MP
    ff_share = FF // N_MP
    qkv_blocks = qkv_moment_new.reshape(D, 3, N_MP, share_width).transpose(1, 2, 0, 3)
    qkv_orth = jax.vmap(jax.vmap(orthogonal))(qkv_blocks).transpose(2, 0, 1, 3).reshape(D, 3, D)
    out_orth = jax.vmap(orthogonal)(out_moment_new.reshape(N_MP, share_width, D)).reshape(D, D)
    gate_up_blocks = gate_up_moment_new.reshape(D, 2, N_MP, ff_share).transpose(1, 2, 0, 3)
    gate_up_orth = jax.vmap(jax.vmap(orthogonal))(gate_up_blocks).transpose(2, 0, 1, 3).reshape(D, 2, FF)
    down_orth = jax.vmap(orthogonal)(down_moment_new.reshape(N_MP, ff_share, D)).reshape(FF, D)
    moment1_new = beta_first * gain_moment1 + (1.0 - beta_first) * gain_grad
    moment2_new = beta_second * gain_moment2 + (1.0 - beta_second) * gain_grad * gain_grad
    corrected1 = moment1_new / (1.0 - beta_first ** STEP)
    corrected2 = moment2_new / (1.0 - beta_second ** STEP)
    gains_new = norm_gains - adam_rate * corrected1 / (jnp.sqrt(corrected2) + adam_epsilon)
    return (outputs.astype(jnp.bfloat16), input_grad, values_grad, qkv_weight - muon_rate * qkv_orth, qkv_moment_new, out_weight - out_rate * out_orth, out_moment_new, gate_up_weight - muon_rate * gate_up_orth, gate_up_moment_new, down_weight - muon_rate * down_orth, down_moment_new, moment1_new, moment2_new, gains_new)
```

```python
import functools

import jax
import jax.numpy as jnp
import numpy as np
from jax import lax
from jax.experimental import pallas as pl
from jax.experimental.pallas import tpu as pltpu
from jax.sharding import PartitionSpec as P

MEGA = 2**20
f32, bf16 = jnp.float32, jnp.bfloat16
VMEM = pl.BlockSpec(memory_space=pltpu.VMEM)
SMEM = pl.BlockSpec(memory_space=pltpu.SMEM)

HD = 64
LEN = 2048
PAIR = 2 * HD
BLOCK = 256
BLOCKS = LEN // BLOCK
LOG2E = 1.4426950408889634
SCORE_SCALE = HD**-0.5 * LOG2E
mask_fill = -1e30


def dot(a, b):
    return lax.dot_general(a, b, (((1,), (0,)), ((), ())), preferred_element_type=f32)


def dot_t(a, b):
    return lax.dot_general(a, b, (((1,), (1,)), ((), ())), preferred_element_type=f32)


def angle_tables():
    half = HD // 2
    frequency = np.exp(-np.log(10000.0) * np.arange(half) * 2.0 / HD)
    angles = np.arange(LEN)[:, None] * np.tile(frequency, PAIR // half)[None, :]
    return np.cos(angles).astype(np.float32), np.sin(angles).astype(np.float32)


def frequency_row():
    half = HD // 2
    frequency = np.exp(-np.log(10000.0) * np.arange(half) * 2.0 / HD)
    return np.tile(frequency, PAIR // half)[None, :].astype(np.float32)


def doc_starts(lens):
    one = lens[0, 0]
    two = one + lens[0, 1]
    return one, two, two + lens[0, 2]


def pick_start(place, starts):
    zero = jnp.zeros_like(place)
    picked = jnp.where(place >= starts[0], starts[0], zero)
    picked = jnp.where(place >= starts[1], starts[1], picked)
    return jnp.where(place >= starts[2], starts[2], picked)


def block_angles(rows, starts, freq, cos_ref, sin_ref):
    place = rows.start + lax.broadcasted_iota(jnp.int32, (BLOCK, PAIR), 0)
    cos_i, sin_i = cos_ref[rows, :], sin_ref[rows, :]
    cos_s = jnp.ones((1, PAIR), f32)
    sin_s = jnp.zeros((1, PAIR), f32)
    for start in starts:
        angle = start.astype(f32) * freq
        cos_s = jnp.where(place >= start, jnp.cos(angle), cos_s)
        sin_s = jnp.where(place >= start, jnp.sin(angle), sin_s)
    return cos_i * cos_s + sin_i * sin_s, sin_i * cos_s - cos_i * sin_s


def swap_halves(x):
    lane = lax.broadcasted_iota(jnp.int32, x.shape, 1)
    front = lane % HD < HD // 2
    return front, jnp.where(front, pltpu.roll(x, PAIR - HD // 2, 1), pltpu.roll(x, HD // 2, 1))


def rotate(x, cos, sin):
    front, other = swap_halves(x)
    return x * cos + jnp.where(front, -other, other) * sin


def rotate_back(x, cos, sin):
    front, other = swap_halves(x)
    return x * cos + jnp.where(front, other, -other) * sin


def head_only(x, head):
    lane = lax.broadcasted_iota(jnp.int32, x.shape, 1)
    return jnp.where(lane // HD == head, x, jnp.zeros_like(x))


def attn_fwd_kernel(
    lens, normed, w_qkv, first_values, cos_ref, sin_ref, freq, q_ref, k_ref, v_ref, out_ref, lse_ref, vt
):
    starts = doc_starts(lens)
    vt[PAIR:, :] = jnp.ones((16, LEN), bf16)
    for block in range(BLOCKS):
        rows = slice(block * BLOCK, (block + 1) * BLOCK)
        proj = dot(normed[rows, :], w_qkv[...])
        cos, sin = block_angles(rows, starts, freq[...], cos_ref, sin_ref)
        q_ref[rows, :] = rotate(proj[:, :PAIR], cos, sin).astype(bf16)
        k_ref[rows, :] = rotate(proj[:, PAIR : 2 * PAIR], cos, sin).astype(bf16)
        mix = 0.5 * proj[:, 2 * PAIR :] + 0.5 * first_values[rows, :].astype(f32)
        v_ref[rows, :] = mix.astype(bf16)
        vt[:PAIR, rows] = mix.T.astype(bf16)
    lse_ref[...] = jnp.zeros_like(lse_ref)
    for block in range(BLOCKS):
        rows = slice(block * BLOCK, (block + 1) * BLOCK)
        span = (block + 1) * BLOCK
        start_row = pick_start(
            rows.start + lax.broadcasted_iota(jnp.int32, (1, BLOCK), 1), starts
        )
        key_at = lax.broadcasted_iota(jnp.int32, (span, BLOCK), 0)
        row_at = rows.start + lax.broadcasted_iota(jnp.int32, (1, BLOCK), 1)
        allowed = (key_at >= start_row) & (key_at <= row_at)
        outs = []
        for head in range(2):
            scores = dot_t(k_ref[:span, :], head_only(q_ref[rows, :], head))
            scores = jnp.where(allowed, scores, mask_fill)
            top = jnp.max(scores, axis=0, keepdims=True) * SCORE_SCALE
            weights = jnp.exp2(scores * SCORE_SCALE - top).astype(bf16)
            values = jnp.concatenate(
                [vt[head * HD : (head + 1) * HD, :span], vt[PAIR:, :span]], axis=0
            )
            mixed = dot(values, weights)
            total = mixed[HD : HD + 1, :]
            outs.append(mixed[:HD, :] / total)
            lse_ref[head : head + 1, rows] = top + jnp.log2(total)
        out_ref[rows, :] = jnp.concatenate(outs, axis=0).T.astype(bf16)


def attn_bwd_kernel(
    lens, q_ref, k_ref, v_ref, heads_ref, grad_ref, lse_ref, normed, w_qkv, cos_ref, sin_ref, freq,
    values_grad_ref, w_grad_ref, normed_grad_ref, kt, dqt, dk_ref, delta, dproj_t,
):
    starts = doc_starts(lens)
    for block in range(BLOCKS):
        rows = slice(block * BLOCK, (block + 1) * BLOCK)
        kt[:, rows] = k_ref[rows, :].astype(f32).T.astype(bf16)
        both = (grad_ref[rows, :].astype(f32) * heads_ref[rows, :].astype(f32)).T
        for head in range(2):
            delta[head : head + 1, rows] = jnp.sum(
                both[head * HD : (head + 1) * HD, :], axis=0, keepdims=True
            )
    dqt[...] = jnp.zeros_like(dqt)
    chunk = 2 * BLOCK
    for block in range(BLOCKS):
        keys = slice(block * BLOCK, (block + 1) * BLOCK)
        dk = jnp.zeros((BLOCK, PAIR), f32)
        dv = jnp.zeros((BLOCK, PAIR), f32)
        at = block * BLOCK
        while at < LEN:
            width = chunk if at % chunk == 0 else BLOCK
            rows = slice(at, at + width)
            at += width
            row_at = rows.start + lax.broadcasted_iota(jnp.int32, (1, width), 1)
            start_row = pick_start(row_at, starts)
            key_at = keys.start + lax.broadcasted_iota(jnp.int32, (BLOCK, width), 0)
            allowed = key_at >= start_row
            if rows.start == keys.start:
                allowed = allowed & (key_at <= row_at)
            for head in range(2):
                q_h = head_only(q_ref[rows, :], head)
                g_h = head_only(grad_ref[rows, :], head)
                scores = dot_t(k_ref[keys, :], q_h)
                prob = jnp.exp2(scores * SCORE_SCALE - lse_ref[head : head + 1, rows])
                prob = jnp.where(allowed, prob, 0.0)
                grad_prob = dot_t(v_ref[keys, :], g_h)
                grad_scores = (prob * (grad_prob - delta[head : head + 1, rows])).astype(bf16)
                dv = dv + dot(prob.astype(bf16), g_h)
                dk = dk + dot(grad_scores, q_h)
                lanes = slice(head * HD, (head + 1) * HD)
                dqt[lanes, rows] += dot(kt[lanes, keys], grad_scores)
        dk_ref[keys, :] = dk
        values_grad_ref[keys, :] = 0.5 * dv
    for block in range(BLOCKS):
        rows = slice(block * BLOCK, (block + 1) * BLOCK)
        cos, sin = block_angles(rows, starts, freq[...], cos_ref, sin_ref)
        dq = rotate_back(dqt[:, rows].T * HD**-0.5, cos, sin)
        dk = rotate_back(dk_ref[rows, :] * HD**-0.5, cos, sin)
        dproj = jnp.concatenate([dq, dk, values_grad_ref[rows, :]], axis=1)
        dproj_t[:, rows] = dproj.T.astype(bf16)
        normed_grad_ref[rows, :] = dot_t(dproj.astype(bf16), w_qkv[...]).astype(bf16)
    for part in range(4):
        cols = slice(part * BLOCK, (part + 1) * BLOCK)
        w_grad_ref[cols, :] = dot(dproj_t[...], normed[:, cols]).T.astype(bf16)


def attn_forward(lens, normed, w_qkv, first_values):
    cos, sin = angle_tables()
    flat = jax.ShapeDtypeStruct((LEN, PAIR), bf16)
    return pl.pallas_call(
        attn_fwd_kernel,
        out_shape=(flat, flat, flat, flat, jax.ShapeDtypeStruct((8, LEN), f32)),
        in_specs=[SMEM] + [VMEM] * 6,
        out_specs=(VMEM,) * 5,
        scratch_shapes=[pltpu.VMEM((PAIR + 16, LEN), bf16)],
        name="attn_fwd",
        compiler_params=pltpu.CompilerParams(vmem_limit_bytes=56 * MEGA),
    )(lens, normed, w_qkv, first_values, cos, sin, frequency_row())


def attn_backward(lens, q, k, v, heads_out, grad_heads, lse, normed, w_qkv):
    cos, sin = angle_tables()
    return pl.pallas_call(
        attn_bwd_kernel,
        out_shape=(
            jax.ShapeDtypeStruct((LEN, PAIR), f32),
            jax.ShapeDtypeStruct(w_qkv.shape, bf16),
            jax.ShapeDtypeStruct(normed.shape, bf16),
        ),
        in_specs=[SMEM] + [VMEM] * 11,
        out_specs=(VMEM,) * 3,
        scratch_shapes=[
            pltpu.VMEM((PAIR, LEN), bf16),
            pltpu.VMEM((PAIR, LEN), f32),
            pltpu.VMEM((LEN, PAIR), f32),
            pltpu.VMEM((8, LEN), f32),
            pltpu.VMEM((3 * PAIR, LEN), bf16),
        ],
        name="attn_bwd",
        compiler_params=pltpu.CompilerParams(vmem_limit_bytes=56 * MEGA),
    )(lens, q, k, v, heads_out, grad_heads, lse, normed, w_qkv, cos, sin, frequency_row())

MESH = pl.DeviceIdType.MESH
ANY = pl.BlockSpec(memory_space=pl.ANY)
DMA = pltpu.SemaphoreType.DMA


def place():
    dp, mp = lax.axis_index("dp"), lax.axis_index("mp")
    return {"x": (dp // 2) % 2 * 2 + mp % 2, "y": dp // 4, "z": mp // 2, "core": dp % 2}


def device_at(at):
    return ((at["y"] * 2 + at["x"] // 2) * 2 + at["core"], at["z"] * 2 + at["x"] % 2)


def moved(at, axis, step):
    new = dict(at)
    if axis == "core":
        new[axis] = 1 - at[axis]
    elif axis == "pair":
        new["x"] = at["x"] + 1 - 2 * (at["x"] % 2)
    else:
        new[axis] = (at[axis] + step + 4) % 4
    return new


def greet(devices):
    barrier = pltpu.get_barrier_semaphore()
    for device in devices:
        pl.semaphore_signal(barrier, inc=1, device_id=device, device_id_type=MESH)
    pl.semaphore_wait(barrier, len(devices))


class Mover:
    def __init__(self, send_sems, recv_sems, local_sems=None):
        self.send_sems, self.recv_sems, self.local_sems = send_sems, recv_sems, local_sems
        self.used, self.locals, self.started = 0, 0, []

    def remote(self, src, dst, device, slot):
        return pltpu.make_async_remote_copy(
            src_ref=src,
            dst_ref=dst,
            send_sem=self.send_sems.at[slot],
            recv_sem=self.recv_sems.at[slot],
            device_id=device,
            device_id_type=MESH,
        )

    def send(self, src, dst, device):
        slot = self.used
        self.used += 1
        copy = self.remote(src, dst, device, slot)
        copy.start()
        self.started.append(copy)
        return slot

    def arrived(self, slot, region):
        self.remote(region, region, self.anyone, slot).wait_recv()

    def local(self, src, dst):
        copy = pltpu.make_async_copy(src, dst, self.local_sems.at[self.locals])
        self.locals += 1
        copy.start()
        return copy

    def finish(self):
        for copy in self.started:
            copy.wait_send()


def weave(*tasks):
    tasks = list(tasks)
    while tasks:
        for task in list(tasks):
            try:
                next(task)
            except StopIteration:
                tasks.remove(task)


def blocks_of(ref, at, whole, half=None, core=True):
    index = (
        slice(None) if "z" in whole else at["z"],
        slice(None) if "x" in whole else at["x"] % 2,
        slice(None) if "y" in whole else at["y"],
        slice(None) if "x" in whole else at["x"] // 2,
    )
    if core:
        index = index + (at["core"],)
    if half is not None:
        rows = ref.shape[-2] // 2
        index = index + (pl.ds(half * rows, rows),)
    return ref.at[index]


ORDERS = (("x", "y", "z"), ("y", "z", "x"), ("z", "x", "y"), ("y", "x", "z"))
RING = ("x", "y", "z")


def ring_ends(me):
    return [moved(me, axis, step) for axis in RING for step in (1, -1)] + [moved(me, "core", 1)]


def gather_part(mover, me, part, whole, order):
    sibling = moved(me, "core", 1)
    mirrors = []

    def mirror(at, done):
        mine = blocks_of(whole, at, done)
        slot = mover.send(mine, mine, device_at(sibling))
        mirrors.append((slot, blocks_of(whole, moved(at, "core", 1), done)))

    own = blocks_of(whole, me, ())
    mover.local(part, own).wait()
    for phase, axis in enumerate(order):
        done = order[:phase]
        plus, minus, across = moved(me, axis, 1), moved(me, axis, -1), moved(me, axis, 2)
        mine = blocks_of(whole, me, done)
        up = mover.send(mine, mine, device_at(plus))
        down = mover.send(mine, mine, device_at(minus))
        if phase == 2:
            mirror(me, done)
        yield
        relay = blocks_of(whole, minus, done)
        mover.arrived(up, relay)
        relay = blocks_of(whole, minus, done, 0)
        up = mover.send(relay, relay, device_at(plus))
        relay = blocks_of(whole, plus, done)
        mover.arrived(down, relay)
        relay = blocks_of(whole, plus, done, 1)
        down = mover.send(relay, relay, device_at(minus))
        if phase == 2:
            mirror(minus, done)
            mirror(plus, done)
        yield
        mover.arrived(up, blocks_of(whole, across, done, 0))
        mover.arrived(down, blocks_of(whole, across, done, 1))
        if phase == 2:
            mirror(across, done)
    yield
    for slot, region in mirrors:
        mover.arrived(slot, region)


def gather_all_kernel(count, *refs):
    parts, wholes = refs[:count], refs[count : 2 * count]
    mover = Mover(*refs[2 * count :])
    me = place()
    mover.anyone = device_at(moved(me, "core", 1))
    greet([device_at(end) for end in ring_ends(me)])
    weave(*(gather_part(mover, me, p, w, o) for p, w, o in zip(parts, wholes, ORDERS)))
    mover.finish()


def gather_all(parts, collective_id):
    count = len(parts)
    shapes = [jax.ShapeDtypeStruct((4, 2, 4, 2, 2) + p.shape, p.dtype) for p in parts]
    return pl.pallas_call(
        functools.partial(gather_all_kernel, count),
        out_shape=shapes,
        in_specs=[ANY] * count,
        out_specs=[ANY] * count,
        scratch_shapes=[DMA((16 * count,)), DMA((16 * count,)), DMA((count,))],
        name="gather_all",
        compiler_params=pltpu.CompilerParams(collective_id=collective_id, has_side_effects=True),
    )(*parts)


LEAD = 144


def gather_tokens_part(mover, me, own, whole):
    mate, plus, minus, across = (
        moved(me, "pair", 1),
        moved(me, "z", 1),
        moved(me, "z", -1),
        moved(me, "z", 2),
    )
    rows = whole.shape[-2]
    rest = rows - LEAD
    cut = (rest // 2 + 15) // 16 * 16
    lead, tail = pl.ds(0, LEAD), pl.ds(LEAD, rest)
    tails = (pl.ds(LEAD, cut), pl.ds(LEAD + cut, rest - cut))

    def at(place_, span):
        return whole.at[place_["z"], place_["x"] % 2, span]

    def both(place_, side=None):
        return whole.at[place_["z"], slice(None) if side is None else side, lead]

    def pass_on(region, target):
        return mover.send(region, region, device_at(target))

    mover.local(own, whole.at[me["z"], me["x"] % 2]).wait()
    pair = pass_on(at(me, lead), mate)
    ring = pass_on(at(me, tail), plus), pass_on(at(me, tail), minus)
    crossed = [(pass_on(at(me, tail), mate), at(moved(me, "pair", 1), tail))]
    yield
    mover.arrived(pair, at(mate, lead))
    wide = pass_on(both(me), plus), pass_on(both(me), minus)
    yield
    mover.arrived(ring[0], at(minus, tail))
    relay = [pass_on(at(minus, tails[0]), plus)]
    crossed.append((pass_on(at(minus, tail), mate), at(moved(minus, "pair", 1), tail)))
    mover.arrived(ring[1], at(plus, tail))
    relay.append(pass_on(at(plus, tails[1]), minus))
    crossed.append((pass_on(at(plus, tail), mate), at(moved(plus, "pair", 1), tail)))
    yield
    mover.arrived(relay[0], at(across, tails[0]))
    mover.arrived(relay[1], at(across, tails[1]))
    crossed.append((pass_on(at(across, tail), mate), at(moved(across, "pair", 1), tail)))
    yield
    mover.arrived(wide[0], both(minus))
    last = [pass_on(both(minus, 0), plus)]
    mover.arrived(wide[1], both(plus))
    last.append(pass_on(both(plus, 1), minus))
    yield
    for slot, region in crossed:
        mover.arrived(slot, region)
    mover.arrived(last[0], both(across, 0))
    mover.arrived(last[1], both(across, 1))


def group_ends(me):
    return [moved(me, "pair", 1), moved(me, "z", 1), moved(me, "z", -1)]


def gather_tokens_kernel(own, whole, *sems):
    mover = Mover(*sems)
    me = place()
    mover.anyone = device_at(moved(me, "pair", 1))
    greet([device_at(end) for end in group_ends(me)])
    weave(gather_tokens_part(mover, me, own, whole))
    mover.finish()


def gather_tokens(own, collective_id):
    return pl.pallas_call(
        gather_tokens_kernel,
        out_shape=jax.ShapeDtypeStruct((4, 2) + own.shape, own.dtype),
        in_specs=[ANY],
        out_specs=ANY,
        scratch_shapes=[DMA((13,)), DMA((13,)), DMA((1,))],
        name="gather_tokens",
        compiler_params=pltpu.CompilerParams(collective_id=collective_id, has_side_effects=True),
    )(own)


def reduce_chunk(at, axis, whole):
    return dict(at), whole


def load(ref):
    return ref[...].astype(f32)


def each_block(ref, body):
    lead = ref.shape[:-2]
    total = 1
    for size in lead:
        total *= size

    def step(flat, carry):
        index = []
        for size in reversed(lead):
            index.append(flat % size)
            flat = flat // size
        body(tuple(reversed(index)))
        return carry

    if total == 1:
        body((0,) * len(lead))
    else:
        lax.fori_loop(0, total, step, 0)


def add_into(target, *terms):
    def body(index):
        total = target[index].astype(f32)
        for term in terms:
            total = total + term[index].astype(f32)
        target[index] = total.astype(target.dtype)

    each_block(target, body)


def scatter_part(mover, me, source, kept, twin, lands, out, order):
    sibling = moved(me, "core", 1)
    theirs = source.at[:, :, :, :, sibling["core"]]
    slot = mover.send(theirs, twin, device_at(sibling))
    own = mover.local(source.at[:, :, :, :, me["core"]], kept)
    yield
    own.wait()
    mover.arrived(slot, twin)
    add_into(kept, twin)
    for phase, axis in enumerate(order):
        rest = order[phase + 1 :]
        plus, minus, across = moved(me, axis, 1), moved(me, axis, -1), moved(me, axis, 2)
        hop_up, hop_down, from_minus, from_plus = lands[phase]
        rows = kept.shape[-2] // 2

        def part(at, half=None):
            return blocks_of(kept, at, rest, half, core=False)

        def half_of(ref, half):
            lead = (slice(None),) * (len(ref.shape) - 2)
            return ref.at[lead + (pl.ds(half * rows, rows),)]

        up = mover.send(part(across, 0), hop_up, device_at(plus))
        down = mover.send(part(across, 1), hop_down, device_at(minus))
        plain_up = mover.send(part(plus, 1), half_of(from_minus, 1), device_at(plus))
        plain_down = mover.send(part(minus, 0), half_of(from_plus, 0), device_at(minus))
        yield
        mover.arrived(up, hop_up)
        add_into(part(plus, 0), hop_up)
        up = mover.send(part(plus, 0), half_of(from_minus, 0), device_at(plus))
        mover.arrived(down, hop_down)
        add_into(part(minus, 1), hop_down)
        down = mover.send(part(minus, 1), half_of(from_plus, 1), device_at(minus))
        yield
        mover.arrived(plain_up, half_of(from_minus, 1))
        mover.arrived(plain_down, half_of(from_plus, 0))
        mover.arrived(up, half_of(from_minus, 0))
        mover.arrived(down, half_of(from_plus, 1))
        if phase < 2:
            add_into(part(me), from_minus, from_plus)
        else:
            out[...] = load(part(me)) + load(from_minus) + load(from_plus)


def scatter_all_kernel(count, *refs):
    sources, outs, rest = refs[:count], refs[count : 2 * count], refs[2 * count :]
    mover = Mover(*rest[:3])
    scratch = rest[3:]
    me = place()
    mover.anyone = device_at(moved(me, "core", 1))
    greet([device_at(end) for end in ring_ends(me)])
    tasks = []
    for index in range(count):
        own = scratch[index * 14 : (index + 1) * 14]
        lands = [own[2 + 4 * phase : 6 + 4 * phase] for phase in range(3)]
        tasks.append(
            scatter_part(mover, me, sources[index], own[0], own[1], lands, outs[index], ORDERS[index])
        )
    weave(*tasks)
    mover.finish()


def lead_shape(whole):
    shape = ()
    for axis, size in (("z", 4), ("x", 2), ("y", 4), ("x", 2)):
        if axis in whole:
            shape = shape + (size,)
    return shape


def scatter_all(sources, collective_id):
    count = len(sources)
    scratch = [DMA((19 * count,)), DMA((19 * count,)), DMA((count,))]
    outs = []
    for index, source in enumerate(sources):
        rows, cols = source.shape[-2:]
        scratch += [pltpu.VMEM((4, 2, 4, 2, rows, cols), bf16)] * 2
        for phase in range(3):
            lead = lead_shape(ORDERS[index][phase + 1 :])
            scratch += [pltpu.VMEM(lead + (rows // 2, cols), bf16)] * 2
            scratch += [pltpu.VMEM(lead + (rows, cols), bf16)] * 2
        outs.append(jax.ShapeDtypeStruct((rows, cols), f32))
    return pl.pallas_call(
        functools.partial(scatter_all_kernel, count),
        out_shape=outs,
        in_specs=[ANY] * count,
        out_specs=[VMEM] * count,
        scratch_shapes=scratch,
        name="scatter_all",
        compiler_params=pltpu.CompilerParams(
            collective_id=collective_id, has_side_effects=True, vmem_limit_bytes=56 * MEGA
        ),
    )(*sources)


def exchange_kernel(source, result, *sems):
    mover = Mover(*sems)
    me = place()
    mine = me["z"] * 2 + me["x"] % 2
    mates = [
        moved(moved(me, "z", dz), "pair", 1) if flip else moved(me, "z", dz)
        for dz, flip in ((2, 1), (2, 0), (1, 1), (3, 1), (1, 0), (3, 0), (0, 1))
    ]
    mover.anyone = device_at(mates[-1])
    greet([device_at(mate) for mate in mates])
    own = mover.local(source.at[mine], result.at[mine])
    slots = []
    for mate in mates:
        theirs = mate["z"] * 2 + mate["x"] % 2
        slots.append(mover.send(source.at[theirs], result.at[mine], device_at(mate)))
    for slot, (dz, flip) in zip(slots, ((2, 1), (2, 0), (3, 1), (1, 1), (3, 0), (1, 0), (0, 1))):
        giver = moved(moved(me, "z", dz), "pair", 1) if flip else moved(me, "z", dz)
        mover.arrived(slot, result.at[giver["z"] * 2 + giver["x"] % 2])
    own.wait()
    mover.finish()


def exchange(source, collective_id):
    return pl.pallas_call(
        exchange_kernel,
        out_shape=jax.ShapeDtypeStruct(source.shape, source.dtype),
        in_specs=[ANY],
        out_specs=ANY,
        scratch_shapes=[DMA((7,)), DMA((7,)), DMA((1,))],
        name="exchange",
        compiler_params=pltpu.CompilerParams(collective_id=collective_id, has_side_effects=True),
    )(source)

norm_epsilon = 1e-06
GROUPS = 8


def row_mean(x):
    return jnp.mean(x, axis=-1, keepdims=True)


def token_kernel(
    heads, stream, cotangent, gains, w_gate, w_up, w_down, w_out,
    block_output, grad_residual, grad_heads, gain_part, g_gate, g_up, g_down, g_out,
    residual, normed, normed_t, cot_t, ffn, grad_normed,
):
    group = pl.program_id(0)
    gain = gains[1:2, :]

    @pl.when(group == 0)
    def first():
        branch = jnp.zeros(residual.shape, f32)
        for m in range(GROUPS):
            branch = branch + dot_t(heads[m], w_out[m]).astype(bf16).astype(f32)
        total = stream[...].astype(f32) + branch
        residual[...] = total
        unit = total * lax.rsqrt(row_mean(total * total) + norm_epsilon)
        scaled = unit * gain
        normed[...] = scaled.astype(bf16)
        normed_t[...] = scaled.T.astype(bf16)
        cot_t[...] = cotangent[...].astype(f32).T.astype(bf16)
        ffn[...] = jnp.zeros_like(ffn)
        grad_normed[...] = jnp.zeros_like(grad_normed)

    gate = dot(normed[...], w_gate[0])
    up = dot(normed[...], w_up[0])
    sigmoid = jax.nn.sigmoid(gate)
    silu = gate * sigmoid
    hidden = (silu * up).astype(bf16)
    ffn[...] += dot_t(hidden, w_down[0]).astype(bf16).astype(f32)
    grad_hidden = dot(cotangent[...], w_down[0])
    slope = sigmoid * (1.0 + gate * (1.0 - sigmoid))
    grad_gate = (grad_hidden * up * slope).astype(bf16)
    grad_up = (grad_hidden * silu).astype(bf16)
    grad_normed[...] += dot_t(grad_gate, w_gate[0]) + dot_t(grad_up, w_up[0])
    g_gate[0] = dot(normed_t[...], grad_gate).astype(bf16)
    g_up[0] = dot(normed_t[...], grad_up).astype(bf16)
    g_down[0] = dot(cot_t[...], hidden).astype(bf16)

    @pl.when(group == GROUPS - 1)
    def last():
        total = residual[...]
        block_output[...] = (total + ffn[...]).astype(bf16)
        inverse = lax.rsqrt(row_mean(total * total) + norm_epsilon)
        unit = total * inverse
        grad = grad_normed[...]
        gain_part[...] = jnp.sum(grad * unit, axis=0, keepdims=True)
        scaled = grad * gain
        result = cotangent[...].astype(f32) + inverse * (scaled - unit * row_mean(scaled * unit))
        grad_residual[...] = result
        low = result.astype(bf16)
        low_t = result.T.astype(bf16)
        for m in range(GROUPS):
            grad_heads[m] = dot(low, w_out[m]).astype(bf16)
            g_out[m] = dot(low_t, heads[m]).astype(bf16)


def token_block(heads, stream, cotangent, gains, w_gate, w_up, w_down, w_out):
    tokens, width = stream.shape
    hidden = w_gate.shape[2]
    whole = lambda shape: pl.BlockSpec(shape, lambda m: (0,) * len(shape))
    each = pl.BlockSpec((1, width, hidden), lambda m: (m, 0, 0))
    flat = (tokens, width)
    return pl.pallas_call(
        token_kernel,
        grid=(GROUPS,),
        in_specs=[whole(heads.shape), whole(flat), whole(flat), whole(gains.shape)]
        + [each] * 3
        + [whole(w_out.shape)],
        out_specs=[whole(flat), whole(flat), whole(heads.shape), whole((1, width))]
        + [each] * 3
        + [whole(w_out.shape)],
        out_shape=[
            jax.ShapeDtypeStruct(flat, bf16),
            jax.ShapeDtypeStruct(flat, f32),
            jax.ShapeDtypeStruct(heads.shape, bf16),
            jax.ShapeDtypeStruct((1, width), f32),
        ]
        + [jax.ShapeDtypeStruct(w_gate.shape, bf16)] * 3
        + [jax.ShapeDtypeStruct(w_out.shape, bf16)],
        scratch_shapes=[
            pltpu.VMEM(flat, f32),
            pltpu.VMEM(flat, bf16),
            pltpu.VMEM((width, tokens), bf16),
            pltpu.VMEM((width, tokens), bf16),
            pltpu.VMEM(flat, f32),
            pltpu.VMEM(flat, f32),
        ],
        name="token_block",
        compiler_params=pltpu.CompilerParams(vmem_limit_bytes=56 * MEGA),
    )(heads, stream, cotangent, gains, w_gate, w_up, w_down, w_out)
STEP = 10
newton_a = 3.4445
newton_b = -4.775
newton_c = 2.0315
muon_rate = 1.0
out_rate = 4.0
adam_rate = 0.8
beta_first = 0.9
beta_second = 0.95
adam_epsilon = 1e-08


def precise(left, right):
    return jnp.dot(left, right, precision=lax.Precision.HIGHEST, preferred_element_type=f32)


def orthogonal(moment):
    row_total, col_total = moment.shape
    iterate = moment / (jnp.sqrt(jnp.sum(moment * moment)) + 1e-07)
    if row_total > col_total:
        iterate = iterate.T
    for sweep in range(5):
        gram = precise(iterate, iterate.T)
        poly = newton_b * gram + newton_c * precise(gram, gram)
        iterate = newton_a * iterate + precise(poly, iterate)
    if row_total > col_total:
        iterate = iterate.T
    return iterate * max(1.0, row_total / col_total) ** 0.5


def own_share(whole, dim, share_size, dp_self):
    return lax.dynamic_slice_in_dim(whole, dp_self * share_size, share_size, dim)


def widen(x):
    return jnp.pad(x, ((0, 0), (0, 384 - x.shape[1])))


def on_device(
    block_input, first_values, out_cotangent, doc_lengths, norm_gains, gain_moment1, gain_moment2,
    qkv_weight, qkv_momentum, out_weight, out_momentum, gate_up_weight, gate_up_momentum,
    down_weight, down_momentum,
):
    tokens, width = block_input.shape
    units = gate_up_weight.shape[2]
    stream = block_input.astype(f32)
    inverse_one = lax.rsqrt(jnp.mean(stream * stream, axis=-1, keepdims=True) + norm_epsilon)
    unit_one = stream * inverse_one
    normed_one = gather_tokens((unit_one * norm_gains[0]).astype(bf16), 0).reshape(LEN, width)
    w_qkv = lax.all_gather(qkv_weight.astype(bf16), "dp", axis=0, tiled=True).reshape(width, 3 * PAIR)
    low_gate_up = gate_up_weight.astype(bf16)
    shares = (
        widen(low_gate_up[:, 0]),
        widen(low_gate_up[:, 1]),
        widen(down_weight.astype(bf16).T),
        out_weight.astype(bf16).T,
    )
    w_gate, w_up, w_down, w_out = (
        whole.reshape(GROUPS, width, whole.shape[-1]) for whole in gather_all(shares, 1)
    )
    q, k, v, heads_out, lse = attn_forward(doc_lengths, normed_one, w_qkv, first_values)
    heads = exchange(heads_out.reshape(GROUPS, tokens, PAIR), 2)
    block_output, grad_residual, grad_heads, gain_two, g_gate, g_up, g_down, g_out = token_block(
        heads, block_input, out_cotangent, norm_gains, w_gate, w_up, w_down, w_out
    )
    grad_heads = exchange(grad_heads, 2).reshape(LEN, PAIR)
    s_gate, s_up, s_down, s_out = scatter_all(
        [g.reshape(4, 2, 4, 2, 2, 64, g.shape[-1]) for g in (g_gate, g_up, g_down, g_out)], 3
    )
    first_values_grad, g_qkv, grad_normed = attn_backward(
        doc_lengths, q, k, v, heads_out, grad_heads, lse, normed_one, w_qkv
    )
    grad_normed_one = lax.psum_scatter(
        grad_normed, "mp", scatter_dimension=0, tiled=True
    ).astype(f32)
    scaled_one = grad_normed_one * norm_gains[0]
    input_grad = grad_residual + inverse_one * (
        scaled_one - unit_one * jnp.mean(scaled_one * unit_one, axis=-1, keepdims=True)
    )
    gain_partial = jnp.stack([jnp.sum(grad_normed_one * unit_one, axis=0), gain_two[0]])
    gain_grad = lax.psum(gain_partial, ("dp", "mp"))
    s_qkv = lax.psum_scatter(g_qkv, "dp", scatter_dimension=0, tiled=True).astype(f32)
    qkv_moment_new = 0.5 * qkv_momentum + s_qkv.reshape(qkv_momentum.shape)
    out_moment_new = 0.5 * out_momentum + s_out.T
    gate_up_moment_new = 0.5 * gate_up_momentum + jnp.stack(
        [s_gate[:, :units], s_up[:, :units]], axis=1
    )
    down_moment_new = 0.5 * down_momentum + s_down[:, :units].T
    qkv_full, out_full, gate_up_full, down_full = (
        lax.all_gather(qkv_moment_new.astype(bf16), "dp", axis=0, tiled=True).astype(f32),
        lax.all_gather(out_moment_new.astype(bf16), "dp", axis=1, tiled=True).astype(f32),
        lax.all_gather(gate_up_moment_new.astype(bf16), "dp", axis=0, tiled=True).astype(f32),
        lax.all_gather(down_moment_new.astype(bf16), "dp", axis=1, tiled=True).astype(f32),
    )
    block_list = [
        qkv_full[:, 0], qkv_full[:, 1], qkv_full[:, 2], out_full,
        gate_up_full[:, 0], gate_up_full[:, 1], down_full,
    ]
    dp_self = lax.axis_index("dp")
    dp_count = lax.axis_size("dp")
    orthogonals = [
        lax.cond(dp_self == slot_index % dp_count, orthogonal, jnp.zeros_like, block_matrix)
        for slot_index, block_matrix in enumerate(block_list)
    ]
    orth_shares = (
        lax.psum_scatter(
            jnp.stack(orthogonals[0:3], axis=1).astype(bf16), "dp", scatter_dimension=0, tiled=True
        ).astype(f32),
        lax.psum_scatter(
            orthogonals[3].astype(bf16), "dp", scatter_dimension=1, tiled=True
        ).astype(f32),
        lax.psum_scatter(
            jnp.stack(orthogonals[4:6], axis=1).astype(bf16), "dp", scatter_dimension=0, tiled=True
        ).astype(f32),
        lax.psum_scatter(
            orthogonals[6].astype(bf16), "dp", scatter_dimension=1, tiled=True
        ).astype(f32),
    )
    moment1_new = beta_first * gain_moment1 + (1.0 - beta_first) * gain_grad
    moment2_new = beta_second * gain_moment2 + (1.0 - beta_second) * gain_grad * gain_grad
    corrected1 = moment1_new / (1.0 - beta_first**STEP)
    corrected2 = moment2_new / (1.0 - beta_second**STEP)
    gains_new = norm_gains - adam_rate * corrected1 / (jnp.sqrt(corrected2) + adam_epsilon)
    return (
        block_output,
        input_grad,
        first_values_grad,
        qkv_weight - muon_rate * orth_shares[0],
        qkv_moment_new,
        out_weight - out_rate * orth_shares[1],
        out_moment_new,
        gate_up_weight - muon_rate * orth_shares[2],
        gate_up_moment_new,
        down_weight - muon_rate * orth_shares[3],
        down_moment_new,
        moment1_new,
        moment2_new,
        gains_new,
    )


def solution(mesh):
    placed = (
        P(("dp", "mp"), None), P("dp", "mp"), P(("dp", "mp"), None), P("dp", None),
        P(), P(), P(),
        P("dp", None, "mp"), P("dp", None, "mp"), P("mp", "dp"), P("mp", "dp"),
        P("dp", None, "mp"), P("dp", None, "mp"), P("mp", "dp"), P("mp", "dp"),
    )
    return jax.shard_map(
        on_device,
        mesh=mesh,
        in_specs=placed,
        out_specs=(P(("dp", "mp"), None), P(("dp", "mp"), None), P("dp", "mp")) + placed[7:] + (P(),) * 3,
        check_vma=False,
    )
```

```python
import functools

import jax
import jax.numpy as jnp
import numpy as np
from jax import lax
from jax.experimental import pallas as pl
from jax.experimental.pallas import tpu as pltpu
from jax.sharding import PartitionSpec as P

MEGA = 2**20
f32, bf16 = jnp.float32, jnp.bfloat16
VMEM = pl.BlockSpec(memory_space=pltpu.VMEM)
SMEM = pl.BlockSpec(memory_space=pltpu.SMEM)

HD = 64
LEN = 2048
PAIR = 2 * HD
BLOCK = 256
BLOCKS = LEN // BLOCK
LOG2E = 1.4426950408889634
SCORE_SCALE = HD**-0.5 * LOG2E
mask_fill = -1e30


def dot(a, b):
    return lax.dot_general(a, b, (((1,), (0,)), ((), ())), preferred_element_type=f32)


def dot_t(a, b):
    return lax.dot_general(a, b, (((1,), (1,)), ((), ())), preferred_element_type=f32)


def angle_tables():
    half = HD // 2
    frequency = np.exp(-np.log(10000.0) * np.arange(half) * 2.0 / HD)
    angles = np.arange(LEN)[:, None] * np.tile(frequency, PAIR // half)[None, :]
    return np.cos(angles).astype(np.float32), np.sin(angles).astype(np.float32)


def frequency_row():
    half = HD // 2
    frequency = np.exp(-np.log(10000.0) * np.arange(half) * 2.0 / HD)
    return np.tile(frequency, PAIR // half)[None, :].astype(np.float32)


def doc_starts(lens):
    one = lens[0, 0]
    two = one + lens[0, 1]
    return one, two, two + lens[0, 2]


def pick_start(place, starts):
    zero = jnp.zeros_like(place)
    picked = jnp.where(place >= starts[0], starts[0], zero)
    picked = jnp.where(place >= starts[1], starts[1], picked)
    return jnp.where(place >= starts[2], starts[2], picked)


def block_angles(rows, starts, freq, cos_ref, sin_ref):
    place = rows.start + lax.broadcasted_iota(jnp.int32, (BLOCK, PAIR), 0)
    cos_i, sin_i = cos_ref[rows, :], sin_ref[rows, :]
    cos_s = jnp.ones((1, PAIR), f32)
    sin_s = jnp.zeros((1, PAIR), f32)
    for start in starts:
        angle = start.astype(f32) * freq
        cos_s = jnp.where(place >= start, jnp.cos(angle), cos_s)
        sin_s = jnp.where(place >= start, jnp.sin(angle), sin_s)
    return cos_i * cos_s + sin_i * sin_s, sin_i * cos_s - cos_i * sin_s


def swap_halves(x):
    lane = lax.broadcasted_iota(jnp.int32, x.shape, 1)
    front = lane % HD < HD // 2
    return front, jnp.where(front, pltpu.roll(x, PAIR - HD // 2, 1), pltpu.roll(x, HD // 2, 1))


def rotate(x, cos, sin):
    front, other = swap_halves(x)
    return x * cos + jnp.where(front, -other, other) * sin


def rotate_back(x, cos, sin):
    front, other = swap_halves(x)
    return x * cos + jnp.where(front, other, -other) * sin


def head_only(x, head):
    lane = lax.broadcasted_iota(jnp.int32, x.shape, 1)
    return jnp.where(lane // HD == head, x, jnp.zeros_like(x))


def attn_fwd_kernel(
    lens, normed, w_qkv, first_values, cos_ref, sin_ref, freq, q_ref, k_ref, v_ref, out_ref, lse_ref, vt
):
    starts = doc_starts(lens)
    vt[PAIR:, :] = jnp.ones((16, LEN), bf16)
    for block in range(BLOCKS):
        rows = slice(block * BLOCK, (block + 1) * BLOCK)
        proj = dot(normed[rows, :], w_qkv[...])
        cos, sin = block_angles(rows, starts, freq[...], cos_ref, sin_ref)
        q_ref[rows, :] = rotate(proj[:, :PAIR], cos, sin).astype(bf16)
        k_ref[rows, :] = rotate(proj[:, PAIR : 2 * PAIR], cos, sin).astype(bf16)
        mix = 0.5 * proj[:, 2 * PAIR :] + 0.5 * first_values[rows, :].astype(f32)
        v_ref[rows, :] = mix.astype(bf16)
        vt[:PAIR, rows] = mix.T.astype(bf16)
    lse_ref[...] = jnp.zeros_like(lse_ref)
    for block in range(BLOCKS):
        rows = slice(block * BLOCK, (block + 1) * BLOCK)
        span = (block + 1) * BLOCK
        start_row = pick_start(
            rows.start + lax.broadcasted_iota(jnp.int32, (1, BLOCK), 1), starts
        )
        key_at = lax.broadcasted_iota(jnp.int32, (span, BLOCK), 0)
        row_at = rows.start + lax.broadcasted_iota(jnp.int32, (1, BLOCK), 1)
        allowed = (key_at >= start_row) & (key_at <= row_at)
        outs = []
        for head in range(2):
            scores = dot_t(k_ref[:span, :], head_only(q_ref[rows, :], head))
            scores = jnp.where(allowed, scores, mask_fill)
            top = jnp.max(scores, axis=0, keepdims=True) * SCORE_SCALE
            weights = jnp.exp2(scores * SCORE_SCALE - top).astype(bf16)
            values = jnp.concatenate(
                [vt[head * HD : (head + 1) * HD, :span], vt[PAIR:, :span]], axis=0
            )
            mixed = dot(values, weights)
            total = mixed[HD : HD + 1, :]
            outs.append(mixed[:HD, :] / total)
            lse_ref[head : head + 1, rows] = top + jnp.log2(total)
        out_ref[rows, :] = jnp.concatenate(outs, axis=0).T.astype(bf16)


def attn_bwd_kernel(
    lens, q_ref, k_ref, v_ref, heads_ref, grad_ref, lse_ref, normed, w_qkv, cos_ref, sin_ref, freq,
    values_grad_ref, w_grad_ref, normed_grad_ref, kt, dqt, dk_ref, delta, dproj_t,
):
    starts = doc_starts(lens)
    for block in range(BLOCKS):
        rows = slice(block * BLOCK, (block + 1) * BLOCK)
        kt[:, rows] = k_ref[rows, :].astype(f32).T.astype(bf16)
        both = (grad_ref[rows, :].astype(f32) * heads_ref[rows, :].astype(f32)).T
        for head in range(2):
            delta[head : head + 1, rows] = jnp.sum(
                both[head * HD : (head + 1) * HD, :], axis=0, keepdims=True
            )
    dqt[...] = jnp.zeros_like(dqt)
    chunk = 2 * BLOCK
    for block in range(BLOCKS):
        keys = slice(block * BLOCK, (block + 1) * BLOCK)
        dk = jnp.zeros((BLOCK, PAIR), f32)
        dv = jnp.zeros((BLOCK, PAIR), f32)
        at = block * BLOCK
        while at < LEN:
            width = chunk if at % chunk == 0 else BLOCK
            rows = slice(at, at + width)
            at += width
            row_at = rows.start + lax.broadcasted_iota(jnp.int32, (1, width), 1)
            start_row = pick_start(row_at, starts)
            key_at = keys.start + lax.broadcasted_iota(jnp.int32, (BLOCK, width), 0)
            allowed = key_at >= start_row
            if rows.start == keys.start:
                allowed = allowed & (key_at <= row_at)
            for head in range(2):
                q_h = head_only(q_ref[rows, :], head)
                g_h = head_only(grad_ref[rows, :], head)
                scores = dot_t(k_ref[keys, :], q_h)
                prob = jnp.exp2(scores * SCORE_SCALE - lse_ref[head : head + 1, rows])
                prob = jnp.where(allowed, prob, 0.0)
                grad_prob = dot_t(v_ref[keys, :], g_h)
                grad_scores = (prob * (grad_prob - delta[head : head + 1, rows])).astype(bf16)
                dv = dv + dot(prob.astype(bf16), g_h)
                dk = dk + dot(grad_scores, q_h)
                lanes = slice(head * HD, (head + 1) * HD)
                dqt[lanes, rows] += dot(kt[lanes, keys], grad_scores)
        dk_ref[keys, :] = dk
        values_grad_ref[keys, :] = 0.5 * dv
    for block in range(BLOCKS):
        rows = slice(block * BLOCK, (block + 1) * BLOCK)
        cos, sin = block_angles(rows, starts, freq[...], cos_ref, sin_ref)
        dq = rotate_back(dqt[:, rows].T * HD**-0.5, cos, sin)
        dk = rotate_back(dk_ref[rows, :] * HD**-0.5, cos, sin)
        dproj = jnp.concatenate([dq, dk, values_grad_ref[rows, :]], axis=1)
        dproj_t[:, rows] = dproj.T.astype(bf16)
        normed_grad_ref[rows, :] = dot_t(dproj.astype(bf16), w_qkv[...]).astype(bf16)
    for part in range(4):
        cols = slice(part * BLOCK, (part + 1) * BLOCK)
        w_grad_ref[cols, :] = dot(dproj_t[...], normed[:, cols]).T.astype(bf16)


def attn_forward(lens, normed, w_qkv, first_values):
    cos, sin = angle_tables()
    flat = jax.ShapeDtypeStruct((LEN, PAIR), bf16)
    return pl.pallas_call(
        attn_fwd_kernel,
        out_shape=(flat, flat, flat, flat, jax.ShapeDtypeStruct((8, LEN), f32)),
        in_specs=[SMEM] + [VMEM] * 6,
        out_specs=(VMEM,) * 5,
        scratch_shapes=[pltpu.VMEM((PAIR + 16, LEN), bf16)],
        name="attn_fwd",
        compiler_params=pltpu.CompilerParams(vmem_limit_bytes=56 * MEGA),
    )(lens, normed, w_qkv, first_values, cos, sin, frequency_row())


def attn_backward(lens, q, k, v, heads_out, grad_heads, lse, normed, w_qkv):
    cos, sin = angle_tables()
    return pl.pallas_call(
        attn_bwd_kernel,
        out_shape=(
            jax.ShapeDtypeStruct((LEN, PAIR), f32),
            jax.ShapeDtypeStruct(w_qkv.shape, bf16),
            jax.ShapeDtypeStruct(normed.shape, bf16),
        ),
        in_specs=[SMEM] + [VMEM] * 11,
        out_specs=(VMEM,) * 3,
        scratch_shapes=[
            pltpu.VMEM((PAIR, LEN), bf16),
            pltpu.VMEM((PAIR, LEN), f32),
            pltpu.VMEM((LEN, PAIR), f32),
            pltpu.VMEM((8, LEN), f32),
            pltpu.VMEM((3 * PAIR, LEN), bf16),
        ],
        name="attn_bwd",
        compiler_params=pltpu.CompilerParams(vmem_limit_bytes=56 * MEGA),
    )(lens, q, k, v, heads_out, grad_heads, lse, normed, w_qkv, cos, sin, frequency_row())

MESH = pl.DeviceIdType.MESH
ANY = pl.BlockSpec(memory_space=pl.ANY)
DMA = pltpu.SemaphoreType.DMA


def place():
    dp, mp = lax.axis_index("dp"), lax.axis_index("mp")
    return {"x": (dp // 2) % 2 * 2 + mp % 2, "y": dp // 4, "z": mp // 2, "core": dp % 2}


def device_at(at):
    return ((at["y"] * 2 + at["x"] // 2) * 2 + at["core"], at["z"] * 2 + at["x"] % 2)


def moved(at, axis, step):
    new = dict(at)
    if axis == "core":
        new[axis] = 1 - at[axis]
    elif axis == "pair":
        new["x"] = at["x"] + 1 - 2 * (at["x"] % 2)
    else:
        new[axis] = (at[axis] + step + 4) % 4
    return new


def greet(devices):
    barrier = pltpu.get_barrier_semaphore()
    for device in devices:
        pl.semaphore_signal(barrier, inc=1, device_id=device, device_id_type=MESH)
    pl.semaphore_wait(barrier, len(devices))


class Mover:
    def __init__(self, send_sems, recv_sems, local_sems=None):
        self.send_sems, self.recv_sems, self.local_sems = send_sems, recv_sems, local_sems
        self.used, self.locals, self.started = 0, 0, []

    def remote(self, src, dst, device, slot):
        return pltpu.make_async_remote_copy(
            src_ref=src,
            dst_ref=dst,
            send_sem=self.send_sems.at[slot],
            recv_sem=self.recv_sems.at[slot],
            device_id=device,
            device_id_type=MESH,
        )

    def send(self, src, dst, device):
        slot = self.used
        self.used += 1
        copy = self.remote(src, dst, device, slot)
        copy.start()
        self.started.append(copy)
        return slot

    def arrived(self, slot, region):
        self.remote(region, region, self.anyone, slot).wait_recv()

    def local(self, src, dst):
        copy = pltpu.make_async_copy(src, dst, self.local_sems.at[self.locals])
        self.locals += 1
        copy.start()
        return copy

    def finish(self):
        for copy in self.started:
            copy.wait_send()


def weave(*tasks):
    tasks = list(tasks)
    while tasks:
        for task in list(tasks):
            try:
                next(task)
            except StopIteration:
                tasks.remove(task)


def blocks_of(ref, at, whole, half=None, core=True):
    index = (
        slice(None) if "z" in whole else at["z"],
        slice(None) if "x" in whole else at["x"] % 2,
        slice(None) if "y" in whole else at["y"],
        slice(None) if "x" in whole else at["x"] // 2,
    )
    if core:
        index = index + (at["core"],)
    if half is not None:
        rows = ref.shape[-2] // 2
        index = index + (pl.ds(half * rows, rows),)
    return ref.at[index]


ORDERS = (("x", "y", "z"), ("y", "z", "x"), ("z", "x", "y"), ("y", "x", "z"))
RING = ("x", "y", "z")


def ring_ends(me):
    return [moved(me, axis, step) for axis in RING for step in (1, -1)] + [moved(me, "core", 1)]


def gather_part(mover, me, part, whole, order):
    sibling = moved(me, "core", 1)
    mirrors = []

    def mirror(at, done):
        mine = blocks_of(whole, at, done)
        slot = mover.send(mine, mine, device_at(sibling))
        mirrors.append((slot, blocks_of(whole, moved(at, "core", 1), done)))

    own = blocks_of(whole, me, ())
    mover.local(part, own).wait()
    for phase, axis in enumerate(order):
        done = order[:phase]
        plus, minus, across = moved(me, axis, 1), moved(me, axis, -1), moved(me, axis, 2)
        mine = blocks_of(whole, me, done)
        up = mover.send(mine, mine, device_at(plus))
        down = mover.send(mine, mine, device_at(minus))
        if phase == 2:
            mirror(me, done)
        yield
        relay = blocks_of(whole, minus, done)
        mover.arrived(up, relay)
        relay = blocks_of(whole, minus, done, 0)
        up = mover.send(relay, relay, device_at(plus))
        relay = blocks_of(whole, plus, done)
        mover.arrived(down, relay)
        relay = blocks_of(whole, plus, done, 1)
        down = mover.send(relay, relay, device_at(minus))
        if phase == 2:
            mirror(minus, done)
            mirror(plus, done)
        yield
        mover.arrived(up, blocks_of(whole, across, done, 0))
        mover.arrived(down, blocks_of(whole, across, done, 1))
        if phase == 2:
            mirror(across, done)
    yield
    for slot, region in mirrors:
        mover.arrived(slot, region)


def gather_all_kernel(count, *refs):
    parts, wholes = refs[:count], refs[count : 2 * count]
    mover = Mover(*refs[2 * count :])
    me = place()
    mover.anyone = device_at(moved(me, "core", 1))
    greet([device_at(end) for end in ring_ends(me)])
    weave(*(gather_part(mover, me, p, w, o) for p, w, o in zip(parts, wholes, ORDERS)))
    mover.finish()


def gather_all(parts, collective_id):
    count = len(parts)
    shapes = [jax.ShapeDtypeStruct((4, 2, 4, 2, 2) + p.shape, p.dtype) for p in parts]
    return pl.pallas_call(
        functools.partial(gather_all_kernel, count),
        out_shape=shapes,
        in_specs=[ANY] * count,
        out_specs=[ANY] * count,
        scratch_shapes=[DMA((16 * count,)), DMA((16 * count,)), DMA((count,))],
        name="gather_all",
        compiler_params=pltpu.CompilerParams(collective_id=collective_id, has_side_effects=True),
    )(*parts)


LEAD = 144


def gather_tokens_part(mover, me, own, whole):
    mate, plus, minus, across = (
        moved(me, "pair", 1),
        moved(me, "z", 1),
        moved(me, "z", -1),
        moved(me, "z", 2),
    )
    rows = whole.shape[-2]
    rest = rows - LEAD
    cut = (rest // 2 + 15) // 16 * 16
    lead, tail = pl.ds(0, LEAD), pl.ds(LEAD, rest)
    tails = (pl.ds(LEAD, cut), pl.ds(LEAD + cut, rest - cut))

    def at(place_, span):
        return whole.at[place_["z"], place_["x"] % 2, span]

    def both(place_, side=None):
        return whole.at[place_["z"], slice(None) if side is None else side, lead]

    def pass_on(region, target):
        return mover.send(region, region, device_at(target))

    mover.local(own, whole.at[me["z"], me["x"] % 2]).wait()
    pair = pass_on(at(me, lead), mate)
    ring = pass_on(at(me, tail), plus), pass_on(at(me, tail), minus)
    crossed = [(pass_on(at(me, tail), mate), at(moved(me, "pair", 1), tail))]
    yield
    mover.arrived(pair, at(mate, lead))
    wide = pass_on(both(me), plus), pass_on(both(me), minus)
    yield
    mover.arrived(ring[0], at(minus, tail))
    relay = [pass_on(at(minus, tails[0]), plus)]
    crossed.append((pass_on(at(minus, tail), mate), at(moved(minus, "pair", 1), tail)))
    mover.arrived(ring[1], at(plus, tail))
    relay.append(pass_on(at(plus, tails[1]), minus))
    crossed.append((pass_on(at(plus, tail), mate), at(moved(plus, "pair", 1), tail)))
    yield
    mover.arrived(relay[0], at(across, tails[0]))
    mover.arrived(relay[1], at(across, tails[1]))
    crossed.append((pass_on(at(across, tail), mate), at(moved(across, "pair", 1), tail)))
    yield
    mover.arrived(wide[0], both(minus))
    last = [pass_on(both(minus, 0), plus)]
    mover.arrived(wide[1], both(plus))
    last.append(pass_on(both(plus, 1), minus))
    yield
    for slot, region in crossed:
        mover.arrived(slot, region)
    mover.arrived(last[0], both(across, 0))
    mover.arrived(last[1], both(across, 1))


def group_ends(me):
    return [moved(me, "pair", 1), moved(me, "z", 1), moved(me, "z", -1)]


def gather_tokens_kernel(own, whole, *sems):
    mover = Mover(*sems)
    me = place()
    mover.anyone = device_at(moved(me, "pair", 1))
    greet([device_at(end) for end in group_ends(me)])
    weave(gather_tokens_part(mover, me, own, whole))
    mover.finish()


def gather_tokens(own, collective_id):
    return pl.pallas_call(
        gather_tokens_kernel,
        out_shape=jax.ShapeDtypeStruct((4, 2) + own.shape, own.dtype),
        in_specs=[ANY],
        out_specs=ANY,
        scratch_shapes=[DMA((13,)), DMA((13,)), DMA((1,))],
        name="gather_tokens",
        compiler_params=pltpu.CompilerParams(collective_id=collective_id, has_side_effects=True),
    )(own)


def reduce_chunk(at, axis, whole):
    return dict(at), whole


def load(ref):
    return ref[...].astype(f32)


def each_block(ref, body):
    lead = ref.shape[:-2]
    total = 1
    for size in lead:
        total *= size

    def step(flat, carry):
        index = []
        for size in reversed(lead):
            index.append(flat % size)
            flat = flat // size
        body(tuple(reversed(index)))
        return carry

    if total == 1:
        body((0,) * len(lead))
    else:
        lax.fori_loop(0, total, step, 0)


def add_into(target, *terms):
    def body(index):
        total = target[index].astype(f32)
        for term in terms:
            total = total + term[index].astype(f32)
        target[index] = total.astype(target.dtype)

    each_block(target, body)


def scatter_part(mover, me, source, kept, twin, lands, out, order):
    sibling = moved(me, "core", 1)
    theirs = source.at[:, :, :, :, sibling["core"]]
    slot = mover.send(theirs, twin, device_at(sibling))
    own = mover.local(source.at[:, :, :, :, me["core"]], kept)
    yield
    own.wait()
    mover.arrived(slot, twin)
    add_into(kept, twin)
    for phase, axis in enumerate(order):
        rest = order[phase + 1 :]
        plus, minus, across = moved(me, axis, 1), moved(me, axis, -1), moved(me, axis, 2)
        hop_up, hop_down, from_minus, from_plus = lands[phase]
        rows = kept.shape[-2] // 2

        def part(at, half=None):
            return blocks_of(kept, at, rest, half, core=False)

        def half_of(ref, half):
            lead = (slice(None),) * (len(ref.shape) - 2)
            return ref.at[lead + (pl.ds(half * rows, rows),)]

        up = mover.send(part(across, 0), hop_up, device_at(plus))
        down = mover.send(part(across, 1), hop_down, device_at(minus))
        plain_up = mover.send(part(plus, 1), half_of(from_minus, 1), device_at(plus))
        plain_down = mover.send(part(minus, 0), half_of(from_plus, 0), device_at(minus))
        yield
        mover.arrived(up, hop_up)
        add_into(part(plus, 0), hop_up)
        up = mover.send(part(plus, 0), half_of(from_minus, 0), device_at(plus))
        mover.arrived(down, hop_down)
        add_into(part(minus, 1), hop_down)
        down = mover.send(part(minus, 1), half_of(from_plus, 1), device_at(minus))
        yield
        mover.arrived(plain_up, half_of(from_minus, 1))
        mover.arrived(plain_down, half_of(from_plus, 0))
        mover.arrived(up, half_of(from_minus, 0))
        mover.arrived(down, half_of(from_plus, 1))
        if phase < 2:
            add_into(part(me), from_minus, from_plus)
        else:
            out[...] = load(part(me)) + load(from_minus) + load(from_plus)


def scatter_all_kernel(count, *refs):
    sources, outs, rest = refs[:count], refs[count : 2 * count], refs[2 * count :]
    mover = Mover(*rest[:3])
    scratch = rest[3:]
    me = place()
    mover.anyone = device_at(moved(me, "core", 1))
    greet([device_at(end) for end in ring_ends(me)])
    tasks = []
    for index in range(count):
        own = scratch[index * 14 : (index + 1) * 14]
        lands = [own[2 + 4 * phase : 6 + 4 * phase] for phase in range(3)]
        tasks.append(
            scatter_part(mover, me, sources[index], own[0], own[1], lands, outs[index], ORDERS[index])
        )
    weave(*tasks)
    mover.finish()


def lead_shape(whole):
    shape = ()
    for axis, size in (("z", 4), ("x", 2), ("y", 4), ("x", 2)):
        if axis in whole:
            shape = shape + (size,)
    return shape


def scatter_all(sources, collective_id):
    count = len(sources)
    scratch = [DMA((19 * count,)), DMA((19 * count,)), DMA((count,))]
    outs = []
    for index, source in enumerate(sources):
        rows, cols = source.shape[-2:]
        scratch += [pltpu.VMEM((4, 2, 4, 2, rows, cols), bf16)] * 2
        for phase in range(3):
            lead = lead_shape(ORDERS[index][phase + 1 :])
            scratch += [pltpu.VMEM(lead + (rows // 2, cols), bf16)] * 2
            scratch += [pltpu.VMEM(lead + (rows, cols), bf16)] * 2
        outs.append(jax.ShapeDtypeStruct((rows, cols), f32))
    return pl.pallas_call(
        functools.partial(scatter_all_kernel, count),
        out_shape=outs,
        in_specs=[ANY] * count,
        out_specs=[VMEM] * count,
        scratch_shapes=scratch,
        name="scatter_all",
        compiler_params=pltpu.CompilerParams(
            collective_id=collective_id, has_side_effects=True, vmem_limit_bytes=56 * MEGA
        ),
    )(*sources)


def exchange_kernel(source, result, *sems):
    mover = Mover(*sems)
    me = place()
    mine = me["z"] * 2 + me["x"] % 2
    mates = [
        moved(moved(me, "z", dz), "pair", 1) if flip else moved(me, "z", dz)
        for dz, flip in ((2, 1), (2, 0), (1, 1), (3, 1), (1, 0), (3, 0), (0, 1))
    ]
    mover.anyone = device_at(mates[-1])
    greet([device_at(mate) for mate in mates])
    own = mover.local(source.at[mine], result.at[mine])
    slots = []
    for mate in mates:
        theirs = mate["z"] * 2 + mate["x"] % 2
        slots.append(mover.send(source.at[theirs], result.at[mine], device_at(mate)))
    for slot, (dz, flip) in zip(slots, ((2, 1), (2, 0), (3, 1), (1, 1), (3, 0), (1, 0), (0, 1))):
        giver = moved(moved(me, "z", dz), "pair", 1) if flip else moved(me, "z", dz)
        mover.arrived(slot, result.at[giver["z"] * 2 + giver["x"] % 2])
    own.wait()
    mover.finish()


def exchange(source, collective_id):
    return pl.pallas_call(
        exchange_kernel,
        out_shape=jax.ShapeDtypeStruct(source.shape, source.dtype),
        in_specs=[ANY],
        out_specs=ANY,
        scratch_shapes=[DMA((7,)), DMA((7,)), DMA((1,))],
        name="exchange",
        compiler_params=pltpu.CompilerParams(collective_id=collective_id, has_side_effects=True),
    )(source)

norm_epsilon = 1e-06
GROUPS = 8


def row_mean(x):
    return jnp.mean(x, axis=-1, keepdims=True)


def token_kernel(
    heads, stream, cotangent, gains, w_gate, w_up, w_down, w_out,
    block_output, grad_residual, grad_heads, gain_part, g_gate, g_up, g_down, g_out,
    residual, normed, normed_t, cot_t, ffn, grad_normed,
):
    group = pl.program_id(0)
    gain = gains[1:2, :]

    @pl.when(group == 0)
    def first():
        branch = jnp.zeros(residual.shape, f32)
        for m in range(GROUPS):
            branch = branch + dot_t(heads[m], w_out[m]).astype(bf16).astype(f32)
        total = stream[...].astype(f32) + branch
        residual[...] = total
        unit = total * lax.rsqrt(row_mean(total * total) + norm_epsilon)
        scaled = unit * gain
        normed[...] = scaled.astype(bf16)
        normed_t[...] = scaled.T.astype(bf16)
        cot_t[...] = cotangent[...].astype(f32).T.astype(bf16)
        ffn[...] = jnp.zeros_like(ffn)
        grad_normed[...] = jnp.zeros_like(grad_normed)

    gate = dot(normed[...], w_gate[0])
    up = dot(normed[...], w_up[0])
    sigmoid = jax.nn.sigmoid(gate)
    silu = gate * sigmoid
    hidden = (silu * up).astype(bf16)
    ffn[...] += dot_t(hidden, w_down[0]).astype(bf16).astype(f32)
    grad_hidden = dot(cotangent[...], w_down[0])
    slope = sigmoid * (1.0 + gate * (1.0 - sigmoid))
    grad_gate = (grad_hidden * up * slope).astype(bf16)
    grad_up = (grad_hidden * silu).astype(bf16)
    grad_normed[...] += dot_t(grad_gate, w_gate[0]) + dot_t(grad_up, w_up[0])
    g_gate[0] = dot(normed_t[...], grad_gate).astype(bf16)
    g_up[0] = dot(normed_t[...], grad_up).astype(bf16)
    g_down[0] = dot(cot_t[...], hidden).astype(bf16)

    @pl.when(group == GROUPS - 1)
    def last():
        total = residual[...]
        block_output[...] = (total + ffn[...]).astype(bf16)
        inverse = lax.rsqrt(row_mean(total * total) + norm_epsilon)
        unit = total * inverse
        grad = grad_normed[...]
        gain_part[...] = jnp.sum(grad * unit, axis=0, keepdims=True)
        scaled = grad * gain
        result = cotangent[...].astype(f32) + inverse * (scaled - unit * row_mean(scaled * unit))
        grad_residual[...] = result
        low = result.astype(bf16)
        low_t = result.T.astype(bf16)
        for m in range(GROUPS):
            grad_heads[m] = dot(low, w_out[m]).astype(bf16)
            g_out[m] = dot(low_t, heads[m]).astype(bf16)


def token_block(heads, stream, cotangent, gains, w_gate, w_up, w_down, w_out):
    tokens, width = stream.shape
    hidden = w_gate.shape[2]
    whole = lambda shape: pl.BlockSpec(shape, lambda m: (0,) * len(shape))
    each = pl.BlockSpec((1, width, hidden), lambda m: (m, 0, 0))
    flat = (tokens, width)
    return pl.pallas_call(
        token_kernel,
        grid=(GROUPS,),
        in_specs=[whole(heads.shape), whole(flat), whole(flat), whole(gains.shape)]
        + [each] * 3
        + [whole(w_out.shape)],
        out_specs=[whole(flat), whole(flat), whole(heads.shape), whole((1, width))]
        + [each] * 3
        + [whole(w_out.shape)],
        out_shape=[
            jax.ShapeDtypeStruct(flat, bf16),
            jax.ShapeDtypeStruct(flat, f32),
            jax.ShapeDtypeStruct(heads.shape, bf16),
            jax.ShapeDtypeStruct((1, width), f32),
        ]
        + [jax.ShapeDtypeStruct(w_gate.shape, bf16)] * 3
        + [jax.ShapeDtypeStruct(w_out.shape, bf16)],
        scratch_shapes=[
            pltpu.VMEM(flat, f32),
            pltpu.VMEM(flat, bf16),
            pltpu.VMEM((width, tokens), bf16),
            pltpu.VMEM((width, tokens), bf16),
            pltpu.VMEM(flat, f32),
            pltpu.VMEM(flat, f32),
        ],
        name="token_block",
        compiler_params=pltpu.CompilerParams(vmem_limit_bytes=56 * MEGA),
    )(heads, stream, cotangent, gains, w_gate, w_up, w_down, w_out)

newton_a = 3.4445
newton_b = -4.775
newton_c = 2.0315
SHARE = 64
DP, MP = 16, 8
WIDE, SLIM = 384, 128
OWNERS = (12, 2, 6, 10, 0, 4, 8)
COLUMNS = (SLIM, SLIM, SLIM, SLIM, WIDE, WIDE, WIDE)
ASPECTS = (8.0, 8.0, 8.0, 1.0, 1024 / 352, 1024 / 352, 1.0)


def halves(x):
    high = x.astype(bf16)
    return high, (x - high.astype(f32)).astype(bf16)


def times(a, b, kind=dot):
    (a_high, a_low), (b_high, b_low) = halves(a), halves(b)
    return kind(a_high, b_high) + (kind(a_high, b_low) + kind(a_low, b_high))


def newton_steps(stacked, result, scale, gram, poly, total, moving, norm):
    size = stacked.shape[-1]
    rows = DP * SHARE

    def held():
        return stacked[...].reshape(rows, size)

    def polynomial():
        one = gram[...]
        rank = lax.broadcasted_iota(jnp.int32, (size, size), 0)
        file = lax.broadcasted_iota(jnp.int32, (size, size), 1)
        poly[...] = (
            jnp.where(rank == file, newton_a, 0.0) + newton_b * one + newton_c * times(one, one)
        )

    def advance():
        step = poly[...]
        gram[...] = times(times(step, gram[...]), step)

    def gather():
        total[...] = times(poly[...], total[...])

    def begin():
        block = held()
        wide = block.astype(f32)
        length = jnp.sqrt(jnp.sum(wide * wide)) + 1e-07
        inverse = jnp.full((1, size), 1.0, f32) / length
        norm[0:1, :size] = inverse
        turned = wide.T.astype(bf16)
        gram[...] = dot(turned, block) * (inverse * inverse)

    def first():
        polynomial()
        total[...] = poly[...]

    def middle():
        high, low = halves(total[...])
        block = held()
        moving[...] = (dot(block, high) + dot(block, low)) * norm[0:1, :size]

    def regram():
        now = moving[...]
        high, low = halves(now)
        turned = now.T
        turned_high, turned_low = halves(turned)
        gram[...] = dot(turned_high, high) + (dot(turned_high, low) + dot(turned_low, high))

    def end():
        ending = times(moving[...], total[...]) * scale
        result[...] = ending.astype(bf16).reshape(DP, SHARE, size)

    return [
        begin, first, advance, polynomial, gather, middle, regram,
        first, advance, polynomial, gather, advance, polynomial, gather, end,
    ]


def scatter_tokens_part(mover, me, source, own, lead_lands, tail_lands, out):
    mate, plus, minus, across = (
        moved(me, "pair", 1),
        moved(me, "z", 1),
        moved(me, "z", -1),
        moved(me, "z", 2),
    )
    side, other = me["x"] % 2, mate["x"] % 2
    hop_up, hop_down, from_minus, from_plus, from_mate = lead_lands
    pairs, tail_up, tail_down, tail_minus, tail_plus = tail_lands
    rows = source.shape[-2]
    lead, tail = pl.ds(0, LEAD), pl.ds(LEAD, rows - LEAD)
    cut = tail_up.shape[0]
    low_cut, high_cut = pl.ds(0, cut), pl.ds(cut, rows - LEAD - cut)

    def to(src, dst, target):
        return mover.send(src, dst, device_at(target))

    load_own = mover.local(source, own)
    crossing = []
    for at in (across, plus, minus, me):
        crossing.append((to(source.at[at["z"], other, tail], pairs.at[at["z"]], mate), at))
    up = to(source.at[across["z"], 0, lead], hop_up, plus)
    down = to(source.at[across["z"], 1, lead], hop_down, minus)
    plain_up = to(source.at[plus["z"], 1, lead], from_minus.at[1], plus)
    plain_down = to(source.at[minus["z"], 0, lead], from_plus.at[0], minus)
    yield
    load_own.wait()

    def crossed(index):
        slot, at = crossing[index]
        region = pairs.at[at["z"]]
        mover.arrived(slot, region)
        add_into(region, own.at[at["z"], side, tail])
        return region

    region = crossed(0)
    t_up = to(region.at[low_cut], tail_up, plus)
    t_down = to(region.at[high_cut], tail_down, minus)
    region = crossed(1)
    t_plain_up = to(region.at[high_cut], tail_minus.at[high_cut], plus)
    region = crossed(2)
    t_plain_down = to(region.at[low_cut], tail_plus.at[low_cut], minus)
    yield
    mover.arrived(up, hop_up)
    add_into(hop_up, own.at[plus["z"], 0, lead])
    up = to(hop_up, from_minus.at[0], plus)
    mover.arrived(down, hop_down)
    add_into(hop_down, own.at[minus["z"], 1, lead])
    down = to(hop_down, from_plus.at[1], minus)
    yield
    mover.arrived(t_up, tail_up)
    add_into(tail_up, pairs.at[plus["z"], low_cut])
    t_up = to(tail_up, tail_minus.at[low_cut], plus)
    mover.arrived(t_down, tail_down)
    add_into(tail_down, pairs.at[minus["z"], high_cut])
    t_down = to(tail_down, tail_plus.at[high_cut], minus)
    yield
    mover.arrived(plain_up, from_minus.at[1])
    mover.arrived(plain_down, from_plus.at[0])
    mover.arrived(up, from_minus.at[0])
    mover.arrived(down, from_plus.at[1])
    add_into(from_minus, from_plus, own.at[me["z"], :, lead])
    last = to(from_minus.at[other], from_mate, mate)
    yield
    region = crossed(3)
    mover.arrived(t_plain_up, tail_minus.at[high_cut])
    mover.arrived(t_plain_down, tail_plus.at[low_cut])
    mover.arrived(t_up, tail_minus.at[low_cut])
    mover.arrived(t_down, tail_plus.at[high_cut])
    out[LEAD:, :] = load(region) + load(tail_minus) + load(tail_plus)
    yield
    mover.arrived(last, from_mate)
    out[:LEAD, :] = load(from_minus.at[side]) + load(from_mate)


def tail_kernel(
    g_qkv, qkv_momentum, s_out, s_gate, s_up, s_down, grad_normed,
    stream, grad_residual, gains, gain_two,
    moment_out, o_q, o_k, o_v, o_out, o_gate, o_up, o_down, input_grad, gain_grad,
    send_sems, recv_sems, local_sems, dp_send, dp_recv, own_send, own_recv, back_send, back_recv,
    all_send, all_recv,
    dp_land, qkv_share, wide_in, wide_out, slim_in, slim_out,
    w_gram, w_poly, w_total, w_moving, s_gram, s_poly, s_total, s_moving, norm,
    own, hop_up, hop_down, from_minus, from_plus, from_mate,
    pairs, tail_up, tail_down, tail_minus, tail_plus, summed, gain_dp, gain_mp,
):
    mover = Mover(send_sems, recv_sems, local_sems)
    me = place()
    dp, mp = lax.axis_index("dp"), lax.axis_index("mp")
    mover.anyone = device_at(moved(me, "core", 1))
    rows_to = [((dp + k) % DP, mp) for k in range(1, DP)]
    cols_to = [(dp, (mp + k) % MP) for k in range(1, MP)]
    greet(rows_to + cols_to)

    def remote(src, dst, send, recv, device):
        return pltpu.make_async_remote_copy(
            src_ref=src, dst_ref=dst, send_sem=send, recv_sem=recv, device_id=device, device_id_type=MESH
        )

    results = (o_q, o_k, o_v, o_out, o_gate, o_up, o_down)

    def give(index, share):
        owner = OWNERS[index]
        land = wide_in if COLUMNS[index] == WIDE else slim_in
        copy = remote(share, land.at[dp], own_send.at[index], own_recv.at[dp], (owner, mp))

        @pl.when(dp != owner)
        def away():
            copy.start()

        @pl.when(dp == owner)
        def here():
            land[dp] = share[...]

        return owner, copy

    def settle(given):
        owner, copy = given

        @pl.when(dp != owner)
        def away():
            copy.wait_send()

    def take(index):
        land = wide_in if COLUMNS[index] == WIDE else slim_in
        for k in range(1, DP):
            giver = (dp + k) % DP
            remote(
                land.at[giver], land.at[giver], own_send.at[index], own_recv.at[giver], (giver, mp)
            ).wait_recv()

    def returns(index, wait):
        made = wide_out if COLUMNS[index] == WIDE else slim_out
        for k in range(1, DP):
            taker = (dp + k) % DP
            copy = remote(
                made.at[taker], results[index], back_send.at[taker], back_recv.at[index], (taker, mp)
            )
            copy.wait_send() if wait else copy.start()

    def owned(columns):
        chosen = [i for i in range(len(OWNERS)) if COLUMNS[i] == columns]
        if columns == WIDE:
            steps = newton_steps(wide_in, wide_out, 1.0, w_gram, w_poly, w_total, w_moving, norm)
        else:
            steps = newton_steps(slim_in, slim_out, 1.0, s_gram, s_poly, s_total, s_moving, norm)
        mine = functools.reduce(jnp.logical_or, [dp == OWNERS[i] for i in chosen])
        for index in chosen:
            pl.when(dp == OWNERS[index])(functools.partial(take, index))
        for step in steps:
            pl.when(mine)(step)
            yield
        for index in chosen:
            pl.when(dp == OWNERS[index])(functools.partial(returns, index, False))

            @pl.when(dp == OWNERS[index])
            def keep():
                made = wide_out if COLUMNS[index] == WIDE else slim_out
                results[index][...] = made[dp]

    given = [give(3, s_out), give(4, s_gate), give(5, s_up), give(6, s_down)]

    def qkv_task():
        for k in range(1, DP):
            taker = (dp + k) % DP
            remote(
                g_qkv.at[taker], dp_land.at[dp], dp_send.at[k], dp_recv.at[k], (taker, mp)
            ).start()
        mine = mover.local(g_qkv.at[dp], dp_land.at[dp])
        yield
        yield
        mine.wait()
        for k in range(1, DP):
            giver = (dp + DP - k) % DP
            remote(
                dp_land.at[giver], dp_land.at[giver], dp_send.at[k], dp_recv.at[k], (giver, mp)
            ).wait_recv()
        total = jnp.zeros((SHARE, WIDE), f32)
        for k in range(DP):
            total = total + dp_land[k].astype(f32)
        moment = 0.5 * qkv_momentum[...] + total
        moment_out[...] = moment
        for k in range(3):
            qkv_share[k] = moment[:, k * SLIM : (k + 1) * SLIM].astype(bf16)
        given.extend(give(k, qkv_share.at[k]) for k in range(3))
        yield
        yield from owned(SLIM)

    def gains_task():
        yield from scatter_tokens_part(
            mover, me, grad_normed, own,
            (hop_up, hop_down, from_minus, from_plus, from_mate),
            (pairs, tail_up, tail_down, tail_minus, tail_plus), summed,
        )
        x = stream[...].astype(f32)
        inverse = lax.rsqrt(row_mean(x * x) + norm_epsilon)
        unit = x * inverse
        grad = summed[...]
        scaled = grad * gains[0:1, :]
        input_grad[...] = grad_residual[...] + inverse * (scaled - unit * row_mean(scaled * unit))
        gain_dp[dp] = jnp.concatenate(
            [jnp.sum(grad * unit, axis=0, keepdims=True), gain_two[...]], axis=0
        )
        copies = []
        for k in range(1, DP):
            taker = (dp + k) % DP
            copy = remote(
                gain_dp.at[dp], gain_dp.at[dp], all_send.at[k], all_recv.at[k], (taker, mp)
            )
            copy.start()
            copies.append(copy)
        yield
        for k in range(1, DP):
            giver = (dp + DP - k) % DP
            remote(
                gain_dp.at[giver], gain_dp.at[giver], all_send.at[k], all_recv.at[k], (giver, mp)
            ).wait_recv()
        total = gain_dp[0]
        for k in range(1, DP):
            total = total + gain_dp[k]
        gain_mp[mp] = total
        for k in range(1, MP):
            taker = (mp + k) % MP
            copy = remote(
                gain_mp.at[mp], gain_mp.at[mp], all_send.at[DP + k], all_recv.at[DP + k], (dp, taker)
            )
            copy.start()
            copies.append(copy)
        yield
        for k in range(1, MP):
            giver = (mp + MP - k) % MP
            remote(
                gain_mp.at[giver], gain_mp.at[giver], all_send.at[DP + k], all_recv.at[DP + k],
                (dp, giver),
            ).wait_recv()
        total = gain_mp[0]
        for k in range(1, MP):
            total = total + gain_mp[k]
        gain_grad[...] = total
        for copy in copies:
            copy.wait_send()

    def wide_task():
        yield from owned(WIDE)

    weave(qkv_task(), gains_task(), wide_task())
    for index, owner in enumerate(OWNERS):

        @pl.when(dp != owner)
        def arrive():
            remote(
                results[index], results[index], back_send.at[0], back_recv.at[index], (owner, mp)
            ).wait_recv()

        pl.when(dp == owner)(functools.partial(returns, index, True))
    for k in range(1, DP):
        taker = (dp + k) % DP
        remote(g_qkv.at[taker], dp_land.at[dp], dp_send.at[k], dp_recv.at[k], (taker, mp)).wait_send()
    for one in given:
        settle(one)
    mover.finish()


def tail_block(
    g_qkv, qkv_momentum, s_out, s_gate, s_up, s_down, grad_normed,
    stream, grad_residual, gains, gain_two, collective_id,
):
    slim, wide = (jax.ShapeDtypeStruct((SHARE, c), bf16) for c in (SLIM, WIDE))
    tokens, width = stream.shape
    rest = tokens - LEAD
    cut = (rest // 2 + 15) // 16 * 16
    vm = pltpu.VMEM
    return pl.pallas_call(
        tail_kernel,
        out_shape=(
            jax.ShapeDtypeStruct((SHARE, WIDE), f32), slim, slim, slim, slim, wide, wide, wide,
            jax.ShapeDtypeStruct((tokens, width), f32),
            jax.ShapeDtypeStruct((2, width), f32),
        ),
        in_specs=[ANY] + [VMEM] * 5 + [ANY] + [VMEM] * 4,
        out_specs=[VMEM] * 10,
        scratch_shapes=[
            DMA((17,)), DMA((17,)), DMA((2,)),
            DMA((DP,)), DMA((DP,)),
            DMA((7,)), DMA((DP,)),
            DMA((DP,)), DMA((7,)),
            DMA((DP + MP,)), DMA((DP + MP,)),
            vm((DP, SHARE, WIDE), bf16), vm((3, SHARE, SLIM), bf16),
            vm((DP, SHARE, WIDE), bf16), vm((DP, SHARE, WIDE), bf16),
            vm((DP, SHARE, SLIM), bf16), vm((DP, SHARE, SLIM), bf16),
            vm((WIDE, WIDE), f32), vm((WIDE, WIDE), f32), vm((WIDE, WIDE), f32), vm((DP * SHARE, WIDE), f32),
            vm((SLIM, SLIM), f32), vm((SLIM, SLIM), f32), vm((SLIM, SLIM), f32), vm((DP * SHARE, SLIM), f32),
            vm((8, WIDE), f32),
            vm((4, 2, tokens, width), bf16),
            vm((LEAD, width), bf16), vm((LEAD, width), bf16),
            vm((2, LEAD, width), bf16), vm((2, LEAD, width), bf16), vm((LEAD, width), bf16),
            vm((4, rest, width), bf16), vm((cut, width), bf16), vm((rest - cut, width), bf16),
            vm((rest, width), bf16), vm((rest, width), bf16),
            vm((tokens, width), f32),
            vm((DP, 2, width), f32), vm((MP, 2, width), f32),
        ],
        name="tail_block",
        compiler_params=pltpu.CompilerParams(
            collective_id=collective_id, has_side_effects=True, vmem_limit_bytes=56 * MEGA
        ),
    )(
        g_qkv, qkv_momentum, s_out, s_gate, s_up, s_down, grad_normed,
        stream, grad_residual, gains, gain_two,
    )
STEP = 10
muon_rate = 1.0
out_rate = 4.0
adam_rate = 0.8
beta_first = 0.9
beta_second = 0.95
adam_epsilon = 1e-08


def widen(x):
    return jnp.pad(x, ((0, 0), (0, 384 - x.shape[1])))


def on_device(
    block_input, first_values, out_cotangent, doc_lengths, norm_gains, gain_moment1, gain_moment2,
    qkv_weight, qkv_momentum, out_weight, out_momentum, gate_up_weight, gate_up_momentum,
    down_weight, down_momentum,
):
    tokens, width = block_input.shape
    units = gate_up_weight.shape[2]
    stream = block_input.astype(f32)
    inverse_one = lax.rsqrt(jnp.mean(stream * stream, axis=-1, keepdims=True) + norm_epsilon)
    unit_one = stream * inverse_one
    normed_one = gather_tokens((unit_one * norm_gains[0]).astype(bf16), 0).reshape(LEN, width)
    w_qkv = lax.all_gather(qkv_weight.astype(bf16), "dp", axis=0, tiled=True).reshape(width, 3 * PAIR)
    low_gate_up = gate_up_weight.astype(bf16)
    shares = (
        widen(low_gate_up[:, 0]),
        widen(low_gate_up[:, 1]),
        widen(down_weight.astype(bf16).T),
        out_weight.astype(bf16).T,
    )
    w_gate, w_up, w_down, w_out = (
        whole.reshape(GROUPS, width, whole.shape[-1]) for whole in gather_all(shares, 1)
    )
    q, k, v, heads_out, lse = attn_forward(doc_lengths, normed_one, w_qkv, first_values)
    heads = exchange(heads_out.reshape(GROUPS, tokens, PAIR), 2)
    block_output, grad_residual, grad_heads, gain_two, g_gate, g_up, g_down, g_out = token_block(
        heads, block_input, out_cotangent, norm_gains, w_gate, w_up, w_down, w_out
    )
    grad_heads = exchange(grad_heads, 2).reshape(LEN, PAIR)
    s_gate, s_up, s_down, s_out = scatter_all(
        [g.reshape(4, 2, 4, 2, 2, 64, g.shape[-1]) for g in (g_gate, g_up, g_down, g_out)], 3
    )
    first_values_grad, g_qkv, grad_normed = attn_backward(
        doc_lengths, q, k, v, heads_out, grad_heads, lse, normed_one, w_qkv
    )
    out_moment_new = 0.5 * out_momentum + s_out.T
    gate_up_moment_new = 0.5 * gate_up_momentum + jnp.stack(
        [s_gate[:, :units], s_up[:, :units]], axis=1
    )
    down_moment_new = 0.5 * down_momentum + s_down[:, :units].T
    low_moment = gate_up_moment_new.astype(bf16)
    moment, o_q, o_k, o_v, o_out, o_gate, o_up, o_down, input_grad, gain_grad = tail_block(
        g_qkv.reshape(DP, SHARE, 3 * PAIR),
        qkv_momentum.reshape(SHARE, 3 * PAIR),
        out_moment_new.T.astype(bf16),
        widen(low_moment[:, 0]),
        widen(low_moment[:, 1]),
        widen(down_moment_new.T.astype(bf16)),
        grad_normed.reshape(4, 2, tokens, width),
        block_input, grad_residual, norm_gains, gain_two, 4,
    )
    qkv_moment_new = moment.reshape(qkv_momentum.shape)
    tall = (width / PAIR) ** 0.5
    broad = (width / units) ** 0.5
    qkv_step = muon_rate * tall * jnp.stack([o_q, o_k, o_v], axis=1).astype(f32)
    out_step = out_rate * o_out.astype(f32).T
    gate_up_step = muon_rate * broad * jnp.stack([o_gate[:, :units], o_up[:, :units]], axis=1).astype(f32)
    down_step = muon_rate * o_down[:, :units].astype(f32).T
    moment1_new = beta_first * gain_moment1 + (1.0 - beta_first) * gain_grad
    moment2_new = beta_second * gain_moment2 + (1.0 - beta_second) * gain_grad * gain_grad
    corrected1 = moment1_new / (1.0 - beta_first**STEP)
    corrected2 = moment2_new / (1.0 - beta_second**STEP)
    gains_new = norm_gains - adam_rate * corrected1 / (jnp.sqrt(corrected2) + adam_epsilon)
    return (
        block_output,
        input_grad,
        first_values_grad,
        qkv_weight - qkv_step,
        qkv_moment_new,
        out_weight - out_step,
        out_moment_new,
        gate_up_weight - gate_up_step,
        gate_up_moment_new,
        down_weight - down_step,
        down_moment_new,
        moment1_new,
        moment2_new,
        gains_new,
    )


def solution(mesh):
    placed = (
        P(("dp", "mp"), None), P("dp", "mp"), P(("dp", "mp"), None), P("dp", None),
        P(), P(), P(),
        P("dp", None, "mp"), P("dp", None, "mp"), P("mp", "dp"), P("mp", "dp"),
        P("dp", None, "mp"), P("dp", None, "mp"), P("mp", "dp"), P("mp", "dp"),
    )
    return jax.shard_map(
        on_device,
        mesh=mesh,
        in_specs=placed,
        out_specs=(P(("dp", "mp"), None), P(("dp", "mp"), None), P("dp", "mp")) + placed[7:] + (P(),) * 3,
        check_vma=False,
    )
```

```python
import functools

import jax
import jax.numpy as jnp
import numpy as np
from jax import lax
from jax.experimental import pallas as pl
from jax.experimental.pallas import tpu as pltpu
from jax.sharding import PartitionSpec as P

MEGA = 2**20
f32, bf16 = jnp.float32, jnp.bfloat16
VMEM = pl.BlockSpec(memory_space=pltpu.VMEM)
SMEM = pl.BlockSpec(memory_space=pltpu.SMEM)

HD = 64
LEN = 2048
PAIR = 2 * HD
BLOCK = 256
BLOCKS = LEN // BLOCK
LOG2E = 1.4426950408889634
SCORE_SCALE = HD**-0.5 * LOG2E
mask_fill = -1e30


def dot(a, b):
    return lax.dot_general(a, b, (((1,), (0,)), ((), ())), preferred_element_type=f32)


def dot_t(a, b):
    return lax.dot_general(a, b, (((1,), (1,)), ((), ())), preferred_element_type=f32)


def frequency():
    half = HD // 2
    return np.tile(np.exp(-np.log(10000.0) * np.arange(half) * 2.0 / HD), PAIR // half)


def angle_tables():
    angles = np.arange(BLOCK)[:, None] * frequency()[None, :]
    return np.cos(angles).astype(np.float32), np.sin(angles).astype(np.float32)


def frequency_row():
    return frequency()[None, :].astype(np.float32)


def doc_starts(lens):
    one = lens[0, 0]
    two = one + lens[0, 1]
    return one, two, two + lens[0, 2]


def pick_start(place, starts):
    zero = jnp.zeros_like(place)
    picked = jnp.where(place >= starts[0], starts[0], zero)
    picked = jnp.where(place >= starts[1], starts[1], picked)
    return jnp.where(place >= starts[2], starts[2], picked)


def turn_tables(starts, freq, turns):
    row = lax.broadcasted_iota(jnp.int32, (4 * BLOCKS, PAIR), 0)
    doc = row % 4
    start = jnp.where(doc == 1, starts[0], 0)
    start = jnp.where(doc == 2, starts[1], start)
    start = jnp.where(doc == 3, starts[2], start)
    angle = (row // 4 * BLOCK - start).astype(f32) * freq
    turns[0] = jnp.cos(angle)
    turns[1] = jnp.sin(angle)


def block_angles(block, starts, turns, cos_ref, sin_ref):
    place = block * BLOCK + lax.broadcasted_iota(jnp.int32, (BLOCK, PAIR), 0)

    def pick(table):
        picked = turns[table, pl.ds(4 * block, 1), :]
        for doc, start in enumerate(starts):
            picked = jnp.where(place >= start, turns[table, pl.ds(4 * block + doc + 1, 1), :], picked)
        return picked

    cos_b, sin_b = pick(0), pick(1)
    return cos_ref[...] * cos_b - sin_ref[...] * sin_b, sin_ref[...] * cos_b + cos_ref[...] * sin_b


def swap_halves(x):
    lane = lax.broadcasted_iota(jnp.int32, x.shape, 1)
    front = lane % HD < HD // 2
    return front, jnp.where(front, pltpu.roll(x, PAIR - HD // 2, 1), pltpu.roll(x, HD // 2, 1))


def rotate(x, cos, sin):
    front, other = swap_halves(x)
    return x * cos + jnp.where(front, -other, other) * sin


def rotate_back(x, cos, sin):
    front, other = swap_halves(x)
    return x * cos + jnp.where(front, other, -other) * sin


def head_only(x, head):
    lane = lax.broadcasted_iota(jnp.int32, x.shape, 1)
    return jnp.where(lane // HD == head, x, jnp.zeros_like(x))


def project_block(block, tokens, w_qkv, first_values, starts, turns, cos_ref, sin_ref, q_ref, k_ref, v_ref, vt):
    rows = slice(block * BLOCK, (block + 1) * BLOCK)
    proj = dot(tokens, w_qkv)
    cos, sin = block_angles(block, starts, turns, cos_ref, sin_ref)
    q_ref[rows, :] = rotate(proj[:, :PAIR], cos, sin).astype(bf16)
    k_ref[rows, :] = rotate(proj[:, PAIR : 2 * PAIR], cos, sin).astype(bf16)
    mix = 0.5 * proj[:, 2 * PAIR :] + 0.5 * first_values[rows, :].astype(f32)
    v_ref[rows, :] = mix.astype(bf16)
    vt[:PAIR, rows] = mix.T.astype(bf16)


def attend_block(block, starts, q_ref, k_ref, vt, out_ref, lse_ref):
    rows = slice(block * BLOCK, (block + 1) * BLOCK)
    span = (block + 1) * BLOCK
    row_at = rows.start + lax.broadcasted_iota(jnp.int32, (1, BLOCK), 1)
    start_row = pick_start(row_at, starts)
    key_at = lax.broadcasted_iota(jnp.int32, (span, BLOCK), 0)
    allowed = (key_at >= start_row) & (key_at <= row_at)
    outs = []
    for head in range(2):
        scores = dot_t(k_ref[:span, :], head_only(q_ref[rows, :], head))
        scores = jnp.where(allowed, scores, mask_fill)
        top = jnp.max(scores, axis=0, keepdims=True) * SCORE_SCALE
        weights = jnp.exp2(scores * SCORE_SCALE - top).astype(bf16)
        values = jnp.concatenate([vt[head * HD : (head + 1) * HD, :span], vt[PAIR:, :span]], axis=0)
        mixed = dot(values, weights)
        total = mixed[HD : HD + 1, :]
        outs.append(mixed[:HD, :] / total)
        lse_ref[head : head + 1, rows] = top + jnp.log2(total)
    out_ref[rows, :] = jnp.concatenate(outs, axis=0).T.astype(bf16)


def attn_bwd_kernel(
    lens, q_ref, k_ref, v_ref, heads_ref, grad_ref, lse_ref, normed, w_qkv, cos_ref, sin_ref, freq,
    values_grad_ref, w_grad_ref, normed_grad_ref, kt, dqt, dk_ref, delta, dproj_t, turns,
):
    starts = doc_starts(lens)
    turn_tables(starts, freq[...], turns)
    for block in range(BLOCKS):
        rows = slice(block * BLOCK, (block + 1) * BLOCK)
        kt[:, rows] = k_ref[rows, :].astype(f32).T.astype(bf16)
        both = (grad_ref[rows, :].astype(f32) * heads_ref[rows, :].astype(f32)).T
        for head in range(2):
            delta[head : head + 1, rows] = jnp.sum(
                both[head * HD : (head + 1) * HD, :], axis=0, keepdims=True
            )
    dqt[...] = jnp.zeros_like(dqt)
    chunk = 2 * BLOCK
    for block in range(BLOCKS):
        keys = slice(block * BLOCK, (block + 1) * BLOCK)
        dk = jnp.zeros((BLOCK, PAIR), f32)
        dv = jnp.zeros((BLOCK, PAIR), f32)
        at = block * BLOCK
        while at < LEN:
            width = chunk if at % chunk == 0 else BLOCK
            rows = slice(at, at + width)
            at += width
            row_at = rows.start + lax.broadcasted_iota(jnp.int32, (1, width), 1)
            start_row = pick_start(row_at, starts)
            key_at = keys.start + lax.broadcasted_iota(jnp.int32, (BLOCK, width), 0)
            allowed = key_at >= start_row
            if rows.start == keys.start:
                allowed = allowed & (key_at <= row_at)
            for head in range(2):
                q_h = head_only(q_ref[rows, :], head)
                g_h = head_only(grad_ref[rows, :], head)
                scores = dot_t(k_ref[keys, :], q_h)
                prob = jnp.exp2(scores * SCORE_SCALE - lse_ref[head : head + 1, rows])
                prob = jnp.where(allowed, prob, 0.0)
                grad_prob = dot_t(v_ref[keys, :], g_h)
                grad_scores = (prob * (grad_prob - delta[head : head + 1, rows])).astype(bf16)
                dv = dv + dot(prob.astype(bf16), g_h)
                dk = dk + dot(grad_scores, q_h)
                lanes = slice(head * HD, (head + 1) * HD)
                dqt[lanes, rows] += dot(kt[lanes, keys], grad_scores)
        dk_ref[keys, :] = dk
        values_grad_ref[keys, :] = 0.5 * dv
    for block in range(BLOCKS):
        rows = slice(block * BLOCK, (block + 1) * BLOCK)
        cos, sin = block_angles(block, starts, turns, cos_ref, sin_ref)
        dq = rotate_back(dqt[:, rows].T * HD**-0.5, cos, sin)
        dk = rotate_back(dk_ref[rows, :] * HD**-0.5, cos, sin)
        dproj = jnp.concatenate([dq, dk, values_grad_ref[rows, :]], axis=1)
        dproj_t[:, rows] = dproj.T.astype(bf16)
        normed_grad_ref[rows, :] = dot_t(dproj.astype(bf16), w_qkv[...]).astype(bf16)
    for part in range(4):
        cols = slice(part * BLOCK, (part + 1) * BLOCK)
        w_grad_ref[cols, :] = dot(dproj_t[...], normed[:, cols]).T.astype(bf16)


def attn_backward(lens, q, k, v, heads_out, grad_heads, lse, normed, w_qkv):
    cos, sin = angle_tables()
    return pl.pallas_call(
        attn_bwd_kernel,
        out_shape=(
            jax.ShapeDtypeStruct((LEN, PAIR), f32),
            jax.ShapeDtypeStruct(w_qkv.shape, bf16),
            jax.ShapeDtypeStruct(normed.shape, bf16),
        ),
        in_specs=[SMEM] + [VMEM] * 11,
        out_specs=(VMEM,) * 3,
        scratch_shapes=[
            pltpu.VMEM((PAIR, LEN), bf16),
            pltpu.VMEM((PAIR, LEN), f32),
            pltpu.VMEM((LEN, PAIR), f32),
            pltpu.VMEM((8, LEN), f32),
            pltpu.VMEM((3 * PAIR, LEN), bf16),
            pltpu.VMEM((2, 4 * BLOCKS, PAIR), f32),
        ],
        name="attn_bwd",
        compiler_params=pltpu.CompilerParams(vmem_limit_bytes=56 * MEGA),
    )(lens, q, k, v, heads_out, grad_heads, lse, normed, w_qkv, cos, sin, frequency_row())

MESH = pl.DeviceIdType.MESH
ANY = pl.BlockSpec(memory_space=pl.ANY)
DMA = pltpu.SemaphoreType.DMA


def place():
    dp, mp = lax.axis_index("dp"), lax.axis_index("mp")
    return {"x": (dp // 2) % 2 * 2 + mp % 2, "y": dp // 4, "z": mp // 2, "core": dp % 2}


def device_at(at):
    return ((at["y"] * 2 + at["x"] // 2) * 2 + at["core"], at["z"] * 2 + at["x"] % 2)


def moved(at, axis, step):
    new = dict(at)
    if axis == "core":
        new[axis] = 1 - at[axis]
    elif axis == "pair":
        new["x"] = at["x"] + 1 - 2 * (at["x"] % 2)
    else:
        new[axis] = (at[axis] + step + 4) % 4
    return new


def greet(devices):
    barrier = pltpu.get_barrier_semaphore()
    for device in devices:
        pl.semaphore_signal(barrier, inc=1, device_id=device, device_id_type=MESH)
    pl.semaphore_wait(barrier, len(devices))


class Mover:
    def __init__(self, send_sems, recv_sems, local_sems=None):
        self.send_sems, self.recv_sems, self.local_sems = send_sems, recv_sems, local_sems
        self.used, self.locals, self.started = 0, 0, []

    def remote(self, src, dst, device, slot):
        return pltpu.make_async_remote_copy(
            src_ref=src,
            dst_ref=dst,
            send_sem=self.send_sems.at[slot],
            recv_sem=self.recv_sems.at[slot],
            device_id=device,
            device_id_type=MESH,
        )

    def send(self, src, dst, device):
        slot = self.used
        self.used += 1
        copy = self.remote(src, dst, device, slot)
        copy.start()
        self.started.append(copy)
        return slot

    def arrived(self, slot, region):
        self.remote(region, region, self.anyone, slot).wait_recv()

    def local(self, src, dst):
        copy = pltpu.make_async_copy(src, dst, self.local_sems.at[self.locals])
        self.locals += 1
        copy.start()
        return copy

    def finish(self):
        for copy in self.started:
            copy.wait_send()


def weave(*tasks):
    tasks = list(tasks)
    while tasks:
        for task in list(tasks):
            try:
                next(task)
            except StopIteration:
                tasks.remove(task)


def blocks_of(ref, at, whole, half=None, core=True):
    index = (
        slice(None) if "z" in whole else at["z"],
        slice(None) if "x" in whole else at["x"] % 2,
        slice(None) if "y" in whole else at["y"],
        slice(None) if "x" in whole else at["x"] // 2,
    )
    if core:
        index = index + (at["core"],)
    if half is not None:
        rows = ref.shape[-2] // 2
        index = index + (pl.ds(half * rows, rows),)
    return ref.at[index]


GATHER_ORDERS = (("x", "z", "y"), ("z", "x", "y"), ("y", "x", "z"), ("y", "z", "x"))
ORDERS = (("x", "y", "z"), ("y", "z", "x"), ("z", "x", "y"), ("y", "x", "z"))
RING = ("x", "y", "z")


def ring_ends(me):
    return [moved(me, axis, step) for axis in RING for step in (1, -1)] + [moved(me, "core", 1)]


def gather_part(mover, me, part, whole, order):
    sibling = moved(me, "core", 1)
    mirrors = []

    def mirror(at, done):
        mine = blocks_of(whole, at, done)
        slot = mover.send(mine, mine, device_at(sibling))
        mirrors.append((slot, blocks_of(whole, moved(at, "core", 1), done)))

    own = blocks_of(whole, me, ())
    mover.local(part, own).wait()
    for phase, axis in enumerate(order):
        done = order[:phase]
        plus, minus, across = moved(me, axis, 1), moved(me, axis, -1), moved(me, axis, 2)
        mine = blocks_of(whole, me, done)
        up = mover.send(mine, mine, device_at(plus))
        down = mover.send(mine, mine, device_at(minus))
        if phase == 2:
            mirror(me, done)
        yield
        relay = blocks_of(whole, minus, done)
        mover.arrived(up, relay)
        relay = blocks_of(whole, minus, done, 0)
        up = mover.send(relay, relay, device_at(plus))
        relay = blocks_of(whole, plus, done)
        mover.arrived(down, relay)
        relay = blocks_of(whole, plus, done, 1)
        down = mover.send(relay, relay, device_at(minus))
        if phase == 2:
            mirror(minus, done)
            mirror(plus, done)
        yield
        mover.arrived(up, blocks_of(whole, across, done, 0))
        mover.arrived(down, blocks_of(whole, across, done, 1))
        if phase == 2:
            mirror(across, done)
    yield
    for slot, region in mirrors:
        mover.arrived(slot, region)


LEAD = 144


def gather_tokens_part(mover, me, whole):
    mate, plus, minus, across = (
        moved(me, "pair", 1),
        moved(me, "z", 1),
        moved(me, "z", -1),
        moved(me, "z", 2),
    )
    rows = whole.shape[-2]
    rest = rows - LEAD
    cut = (rest // 2 + 15) // 16 * 16
    lead, tail = pl.ds(0, LEAD), pl.ds(LEAD, rest)
    tails = (pl.ds(LEAD, cut), pl.ds(LEAD + cut, rest - cut))

    def at(place_, span):
        return whole.at[place_["z"], place_["x"] % 2, span]

    def both(place_, side=None):
        return whole.at[place_["z"], slice(None) if side is None else side, lead]

    def pass_on(region, target):
        return mover.send(region, region, device_at(target))

    pair = pass_on(at(me, lead), mate)
    ring = pass_on(at(me, tail), plus), pass_on(at(me, tail), minus)
    crossed = [(pass_on(at(me, tail), mate), at(moved(me, "pair", 1), tail))]
    yield
    mover.arrived(pair, at(mate, lead))
    wide = pass_on(both(me), plus), pass_on(both(me), minus)
    yield
    mover.arrived(ring[0], at(minus, tail))
    relay = [pass_on(at(minus, tails[0]), plus)]
    crossed.append((pass_on(at(minus, tail), mate), at(moved(minus, "pair", 1), tail)))
    mover.arrived(ring[1], at(plus, tail))
    relay.append(pass_on(at(plus, tails[1]), minus))
    crossed.append((pass_on(at(plus, tail), mate), at(moved(plus, "pair", 1), tail)))
    yield
    mover.arrived(relay[0], at(across, tails[0]))
    mover.arrived(relay[1], at(across, tails[1]))
    crossed.append((pass_on(at(across, tail), mate), at(moved(across, "pair", 1), tail)))
    yield
    mover.arrived(wide[0], both(minus))
    last = [pass_on(both(minus, 0), plus)]
    mover.arrived(wide[1], both(plus))
    last.append(pass_on(both(plus, 1), minus))
    yield
    for slot, region in crossed:
        mover.arrived(slot, region)
    mover.arrived(last[0], both(across, 0))
    mover.arrived(last[1], both(across, 1))


def load(ref):
    return ref[...].astype(f32)


def each_block(ref, body):
    lead = ref.shape[:-2]
    total = 1
    for size in lead:
        total *= size

    def step(flat, carry):
        index = []
        for size in reversed(lead):
            index.append(flat % size)
            flat = flat // size
        body(tuple(reversed(index)))
        return carry

    if total == 1:
        body((0,) * len(lead))
    else:
        lax.fori_loop(0, total, step, 0)


def add_into(target, *terms):
    def body(index):
        total = target[index].astype(f32)
        for term in terms:
            total = total + term[index].astype(f32)
        target[index] = total.astype(target.dtype)

    each_block(target, body)


def scatter_part(mover, me, source, kept, twin, lands, out, order):
    sibling = moved(me, "core", 1)
    theirs = source.at[:, :, :, :, sibling["core"]]
    slot = mover.send(theirs, twin, device_at(sibling))
    own = mover.local(source.at[:, :, :, :, me["core"]], kept)
    yield
    own.wait()
    mover.arrived(slot, twin)
    add_into(kept, twin)
    for phase, axis in enumerate(order):
        rest = order[phase + 1 :]
        plus, minus, across = moved(me, axis, 1), moved(me, axis, -1), moved(me, axis, 2)
        hop_up, hop_down, from_minus, from_plus = lands[phase]
        rows = kept.shape[-2] // 2

        def part(at, half=None):
            return blocks_of(kept, at, rest, half, core=False)

        def half_of(ref, half):
            lead = (slice(None),) * (len(ref.shape) - 2)
            return ref.at[lead + (pl.ds(half * rows, rows),)]

        up = mover.send(part(across, 0), hop_up, device_at(plus))
        down = mover.send(part(across, 1), hop_down, device_at(minus))
        plain_up = mover.send(part(plus, 1), half_of(from_minus, 1), device_at(plus))
        plain_down = mover.send(part(minus, 0), half_of(from_plus, 0), device_at(minus))
        yield
        mover.arrived(up, hop_up)
        add_into(part(plus, 0), hop_up)
        up = mover.send(part(plus, 0), half_of(from_minus, 0), device_at(plus))
        mover.arrived(down, hop_down)
        add_into(part(minus, 1), hop_down)
        down = mover.send(part(minus, 1), half_of(from_plus, 1), device_at(minus))
        yield
        mover.arrived(plain_up, half_of(from_minus, 1))
        mover.arrived(plain_down, half_of(from_plus, 0))
        mover.arrived(up, half_of(from_minus, 0))
        mover.arrived(down, half_of(from_plus, 1))
        if phase < 2:
            add_into(part(me), from_minus, from_plus)
        else:
            out[...] = load(part(me)) + load(from_minus) + load(from_plus)


def scatter_all_kernel(count, *refs):
    sources, outs, rest = refs[:count], refs[count : 2 * count], refs[2 * count :]
    mover = Mover(*rest[:3])
    scratch = rest[3:]
    me = place()
    mover.anyone = device_at(moved(me, "core", 1))
    greet([device_at(end) for end in ring_ends(me)])
    tasks = []
    for index in range(count):
        own = scratch[index * 14 : (index + 1) * 14]
        lands = [own[2 + 4 * phase : 6 + 4 * phase] for phase in range(3)]
        tasks.append(
            scatter_part(mover, me, sources[index], own[0], own[1], lands, outs[index], ORDERS[index])
        )
    weave(*tasks)
    mover.finish()


def lead_shape(whole):
    shape = ()
    for axis, size in (("z", 4), ("x", 2), ("y", 4), ("x", 2)):
        if axis in whole:
            shape = shape + (size,)
    return shape


def scatter_all(sources, collective_id):
    count = len(sources)
    scratch = [DMA((19 * count,)), DMA((19 * count,)), DMA((count,))]
    outs = []
    for index, source in enumerate(sources):
        rows, cols = source.shape[-2:]
        scratch += [pltpu.VMEM((4, 2, 4, 2, rows, cols), bf16)] * 2
        for phase in range(3):
            lead = lead_shape(ORDERS[index][phase + 1 :])
            scratch += [pltpu.VMEM(lead + (rows // 2, cols), bf16)] * 2
            scratch += [pltpu.VMEM(lead + (rows, cols), bf16)] * 2
        outs.append(jax.ShapeDtypeStruct((rows, cols), f32))
    return pl.pallas_call(
        functools.partial(scatter_all_kernel, count),
        out_shape=outs,
        in_specs=[ANY] * count,
        out_specs=[VMEM] * count,
        scratch_shapes=scratch,
        name="scatter_all",
        compiler_params=pltpu.CompilerParams(
            collective_id=collective_id, has_side_effects=True, vmem_limit_bytes=56 * MEGA
        ),
    )(*sources)


def exchange_kernel(source, result, *sems):
    mover = Mover(*sems)
    me = place()
    mine = me["z"] * 2 + me["x"] % 2
    mates = [
        moved(moved(me, "z", dz), "pair", 1) if flip else moved(me, "z", dz)
        for dz, flip in ((2, 1), (2, 0), (1, 1), (3, 1), (1, 0), (3, 0), (0, 1))
    ]
    mover.anyone = device_at(mates[-1])
    greet([device_at(mate) for mate in mates])
    own = mover.local(source.at[mine], result.at[mine])
    slots = []
    for mate in mates:
        theirs = mate["z"] * 2 + mate["x"] % 2
        slots.append(mover.send(source.at[theirs], result.at[mine], device_at(mate)))
    for slot, (dz, flip) in zip(slots, ((2, 1), (2, 0), (3, 1), (1, 1), (3, 0), (1, 0), (0, 1))):
        giver = moved(moved(me, "z", dz), "pair", 1) if flip else moved(me, "z", dz)
        mover.arrived(slot, result.at[giver["z"] * 2 + giver["x"] % 2])
    own.wait()
    mover.finish()


def exchange(source, collective_id):
    return pl.pallas_call(
        exchange_kernel,
        out_shape=jax.ShapeDtypeStruct(source.shape, source.dtype),
        in_specs=[ANY],
        out_specs=ANY,
        scratch_shapes=[DMA((7,)), DMA((7,)), DMA((1,))],
        name="exchange",
        compiler_params=pltpu.CompilerParams(collective_id=collective_id, has_side_effects=True),
    )(source)

norm_epsilon = 1e-06
GROUPS = 8


def row_mean(x):
    return jnp.mean(x, axis=-1, keepdims=True)


def token_kernel(
    heads, stream, cotangent, gains, w_gate, w_up, w_down, w_out,
    block_output, grad_residual, grad_heads, gain_part, g_gate, g_up, g_down, g_out,
    residual, normed, normed_t, cot_t, ffn, grad_normed,
):
    group = pl.program_id(0)
    gain = gains[1:2, :]

    @pl.when(group == 0)
    def first():
        branch = jnp.zeros(residual.shape, f32)
        for m in range(GROUPS):
            branch = branch + dot_t(heads[m], w_out[m]).astype(bf16).astype(f32)
        total = stream[...].astype(f32) + branch
        residual[...] = total
        unit = total * lax.rsqrt(row_mean(total * total) + norm_epsilon)
        scaled = unit * gain
        normed[...] = scaled.astype(bf16)
        normed_t[...] = scaled.T.astype(bf16)
        cot_t[...] = cotangent[...].astype(f32).T.astype(bf16)
        ffn[...] = jnp.zeros_like(ffn)
        grad_normed[...] = jnp.zeros_like(grad_normed)

    gate = dot(normed[...], w_gate[0])
    up = dot(normed[...], w_up[0])
    sigmoid = jax.nn.sigmoid(gate)
    silu = gate * sigmoid
    hidden = (silu * up).astype(bf16)
    ffn[...] += dot_t(hidden, w_down[0]).astype(bf16).astype(f32)
    grad_hidden = dot(cotangent[...], w_down[0])
    slope = sigmoid * (1.0 + gate * (1.0 - sigmoid))
    grad_gate = (grad_hidden * up * slope).astype(bf16)
    grad_up = (grad_hidden * silu).astype(bf16)
    grad_normed[...] += dot_t(grad_gate, w_gate[0]) + dot_t(grad_up, w_up[0])
    g_gate[0] = dot(normed_t[...], grad_gate).astype(bf16)
    g_up[0] = dot(normed_t[...], grad_up).astype(bf16)
    g_down[0] = dot(cot_t[...], hidden).astype(bf16)

    @pl.when(group == GROUPS - 1)
    def last():
        total = residual[...]
        block_output[...] = (total + ffn[...]).astype(bf16)
        inverse = lax.rsqrt(row_mean(total * total) + norm_epsilon)
        unit = total * inverse
        grad = grad_normed[...]
        gain_part[...] = jnp.sum(grad * unit, axis=0, keepdims=True)
        scaled = grad * gain
        result = cotangent[...].astype(f32) + inverse * (scaled - unit * row_mean(scaled * unit))
        grad_residual[...] = result
        low = result.astype(bf16)
        low_t = result.T.astype(bf16)
        for m in range(GROUPS):
            grad_heads[m] = dot(low, w_out[m]).astype(bf16)
            g_out[m] = dot(low_t, heads[m]).astype(bf16)


def token_block(heads, stream, cotangent, gains, w_gate, w_up, w_down, w_out):
    tokens, width = stream.shape
    hidden = w_gate.shape[2]
    whole = lambda shape: pl.BlockSpec(shape, lambda m: (0,) * len(shape))
    each = pl.BlockSpec((1, width, hidden), lambda m: (m, 0, 0))
    flat = (tokens, width)
    return pl.pallas_call(
        token_kernel,
        grid=(GROUPS,),
        in_specs=[whole(heads.shape), whole(flat), whole(flat), whole(gains.shape)]
        + [each] * 3
        + [whole(w_out.shape)],
        out_specs=[whole(flat), whole(flat), whole(heads.shape), whole((1, width))]
        + [each] * 3
        + [whole(w_out.shape)],
        out_shape=[
            jax.ShapeDtypeStruct(flat, bf16),
            jax.ShapeDtypeStruct(flat, f32),
            jax.ShapeDtypeStruct(heads.shape, bf16),
            jax.ShapeDtypeStruct((1, width), f32),
        ]
        + [jax.ShapeDtypeStruct(w_gate.shape, bf16)] * 3
        + [jax.ShapeDtypeStruct(w_out.shape, bf16)],
        scratch_shapes=[
            pltpu.VMEM(flat, f32),
            pltpu.VMEM(flat, bf16),
            pltpu.VMEM((width, tokens), bf16),
            pltpu.VMEM((width, tokens), bf16),
            pltpu.VMEM(flat, f32),
            pltpu.VMEM(flat, f32),
        ],
        name="token_block",
        compiler_params=pltpu.CompilerParams(vmem_limit_bytes=56 * MEGA),
    )(heads, stream, cotangent, gains, w_gate, w_up, w_down, w_out)

DP, MP = 16, 8
SHARE = 64


def gather_row_part(mover, me, whole):
    plus, minus, across = moved(me, "y", 1), moved(me, "y", -1), moved(me, "y", 2)
    far, sibling = moved(me, "x", 2), moved(me, "core", 1)

    def one(at, half=None):
        region = whole.at[at["y"], at["x"] // 2, at["core"]]
        return region if half is None else region.at[pl.ds(half * (SHARE // 2), SHARE // 2)]

    def column(at):
        return whole.at[:, at["x"] // 2, at["core"]]

    def pass_on(region, target):
        return mover.send(region, region, device_at(target))

    ring = pass_on(one(me), plus), pass_on(one(me), minus)
    yield
    mover.arrived(ring[0], one(minus))
    relay = [pass_on(one(minus, 0), plus)]
    mover.arrived(ring[1], one(plus))
    relay.append(pass_on(one(plus, 1), minus))
    yield
    mover.arrived(relay[0], one(across, 0))
    mover.arrived(relay[1], one(across, 1))
    half = pass_on(column(me), far)
    mirrors = [(pass_on(column(me), sibling), column(sibling))]
    yield
    mover.arrived(half, column(far))
    mirrors.append((pass_on(column(far), sibling), column(moved(far, "core", 1))))
    yield
    for slot, region in mirrors:
        mover.arrived(slot, region)


def front_kernel(
    lens, stream, gains, s_gate, s_up, s_down, s_out, s_qkv, first_values, cos_ref, sin_ref, freq,
    w_gate, w_up, w_down, w_out, normed, w_qkv, q_ref, k_ref, v_ref, out_ref, lse_ref, heads,
    send_sems, recv_sems, local_sems, head_send, head_recv, vt, turns,
):
    me = place()
    dp, mp = lax.axis_index("dp"), lax.axis_index("mp")
    mover = Mover(send_sems, recv_sems, local_sems)
    mover.anyone = device_at(moved(me, "core", 1))
    x = stream[...].astype(f32)
    unit = x * lax.rsqrt(row_mean(x * x) + norm_epsilon)
    normed[me["z"], me["x"] % 2] = (unit * gains[0:1, :]).astype(bf16)
    w_qkv[me["y"], me["x"] // 2, me["core"]] = s_qkv[...]
    cols_to = [(dp, (mp + k) % MP) for k in range(1, MP)]
    others = [moved(me, axis, step) for axis in ("x", "y") for step in (1, -1)]
    others += [moved(me, "core", 1), moved(me, "x", 2)]
    greet(cols_to + [device_at(end) for end in others])

    tokens = gather_tokens_part(mover, me, normed)
    row = gather_row_part(mover, me, w_qkv)
    parts = [
        gather_part(mover, me, part, whole, order)
        for part, whole, order in zip(
            (s_gate, s_up, s_down, s_out), (w_gate, w_up, w_down, w_out), GATHER_ORDERS
        )
    ]
    starts = doc_starts(lens)

    def step(*tasks):
        for task in tasks:
            next(task, None)

    step(tokens, row, *parts)
    turn_tables(starts, freq[...], turns)
    vt[PAIR:, :] = jnp.ones((16, LEN), bf16)
    lse_ref[...] = jnp.zeros_like(lse_ref)
    step(row, *parts)
    step(tokens, row, *parts)
    step(tokens, row, *parts)
    step(tokens, *parts)
    step(tokens, row)
    step(tokens)
    weights = w_qkv[...].reshape(DP * SHARE, 3 * PAIR)
    for block in range(BLOCKS):
        project_block(
            block, normed[block // 2, block % 2], weights, first_values, starts, turns,
            cos_ref, sin_ref, q_ref, k_ref, v_ref, vt,
        )
    for block in range(BLOCKS):
        attend_block(block, starts, q_ref, k_ref, vt, out_ref, lse_ref)
        if block >= 4:
            step(parts[block - 4])
    copies = []
    for k in (5, 3, 4, 2, 6, 7, 1):
        taker = (mp + k) % MP
        copy = pltpu.make_async_remote_copy(
            src_ref=out_ref.at[pl.ds(pl.multiple_of(taker * BLOCK, BLOCK), BLOCK)],
            dst_ref=heads.at[mp],
            send_sem=head_send.at[k],
            recv_sem=head_recv.at[k],
            device_id=(dp, taker),
            device_id_type=MESH,
        )
        copy.start()
        copies.append(copy)
    heads[mp] = out_ref[pl.ds(pl.multiple_of(mp * BLOCK, BLOCK), BLOCK), :]
    step(*parts)
    for k in range(1, MP):
        giver = (mp + MP - k) % MP
        pltpu.make_async_remote_copy(
            src_ref=heads.at[giver],
            dst_ref=heads.at[giver],
            send_sem=head_send.at[k],
            recv_sem=head_recv.at[k],
            device_id=(dp, giver),
            device_id_type=MESH,
        ).wait_recv()
    step(*parts)
    for copy in copies:
        copy.wait_send()
    mover.finish()


def front(lens, stream, gains, shares, s_qkv, first_values, collective_id):
    cos, sin = angle_tables()
    flat = jax.ShapeDtypeStruct((LEN, PAIR), bf16)
    vm = pltpu.VMEM
    slots = 16 * len(shares) + 13 + 8
    return pl.pallas_call(
        front_kernel,
        out_shape=[jax.ShapeDtypeStruct((4, 2, 4, 2, 2) + p.shape, p.dtype) for p in shares]
        + [
            jax.ShapeDtypeStruct((4, 2) + stream.shape, bf16),
            jax.ShapeDtypeStruct((4, 2, 2) + s_qkv.shape, bf16),
            flat, flat, flat, flat,
            jax.ShapeDtypeStruct((8, LEN), f32),
            jax.ShapeDtypeStruct((MP, BLOCK, PAIR), bf16),
        ],
        in_specs=[SMEM, VMEM, VMEM] + [ANY] * len(shares) + [VMEM] * 5,
        out_specs=[ANY] * len(shares) + [VMEM] * 8,
        scratch_shapes=[
            DMA((slots,)), DMA((slots,)), DMA((len(shares),)), DMA((MP,)), DMA((MP,)),
            vm((PAIR + 16, LEN), bf16), vm((2, 4 * BLOCKS, PAIR), f32),
        ],
        name="front",
        compiler_params=pltpu.CompilerParams(
            collective_id=collective_id, has_side_effects=True, vmem_limit_bytes=56 * MEGA
        ),
    )(lens, stream, gains, *shares, s_qkv, first_values, cos, sin, frequency_row())

newton_a = 3.4445
newton_b = -4.775
newton_c = 2.0315
WIDE, SLIM = 384, 128
OWNERS = (12, 2, 6, 10, 0, 4, 8)
COLUMNS = (SLIM, SLIM, SLIM, SLIM, WIDE, WIDE, WIDE)
ASPECTS = (8.0, 8.0, 8.0, 1.0, 1024 / 352, 1024 / 352, 1.0)


def halves(x):
    high = x.astype(bf16)
    return high, (x - high.astype(f32)).astype(bf16)


def times(a, b, kind=dot):
    (a_high, a_low), (b_high, b_low) = halves(a), halves(b)
    return kind(a_high, b_high) + (kind(a_high, b_low) + kind(a_low, b_high))


def newton_steps(stacked, result, scale, gram, poly, total, moving, norm):
    size = stacked.shape[-1]
    rows = DP * SHARE

    def held():
        return stacked[...].reshape(rows, size)

    def polynomial():
        one = gram[...]
        rank = lax.broadcasted_iota(jnp.int32, (size, size), 0)
        file = lax.broadcasted_iota(jnp.int32, (size, size), 1)
        poly[...] = (
            jnp.where(rank == file, newton_a, 0.0) + newton_b * one + newton_c * times(one, one)
        )

    def advance():
        step = poly[...]
        gram[...] = times(times(step, gram[...]), step)

    def gather():
        total[...] = times(poly[...], total[...])

    def begin():
        block = held()
        wide = block.astype(f32)
        length = jnp.sqrt(jnp.sum(wide * wide)) + 1e-07
        inverse = jnp.full((1, size), 1.0, f32) / length
        norm[0:1, :size] = inverse
        turned = wide.T.astype(bf16)
        gram[...] = dot(turned, block) * (inverse * inverse)

    def first():
        polynomial()
        total[...] = poly[...]

    def middle():
        high, low = halves(total[...])
        block = held()
        moving[...] = (dot(block, high) + dot(block, low)) * norm[0:1, :size]

    def regram():
        now = moving[...]
        high, low = halves(now)
        turned = now.T
        turned_high, turned_low = halves(turned)
        gram[...] = dot(turned_high, high) + (dot(turned_high, low) + dot(turned_low, high))

    def end():
        ending = times(moving[...], total[...]) * scale
        result[...] = ending.astype(bf16).reshape(DP, SHARE, size)

    return [
        begin, first, advance, polynomial, gather, middle, regram,
        first, advance, polynomial, gather, advance, polynomial, gather, end,
    ]


def scatter_tokens_part(mover, me, source, own, lead_lands, tail_lands, out):
    mate, plus, minus, across = (
        moved(me, "pair", 1),
        moved(me, "z", 1),
        moved(me, "z", -1),
        moved(me, "z", 2),
    )
    side, other = me["x"] % 2, mate["x"] % 2
    hop_up, hop_down, from_minus, from_plus, from_mate = lead_lands
    pairs, tail_up, tail_down, tail_minus, tail_plus = tail_lands
    rows = source.shape[-2]
    lead, tail = pl.ds(0, LEAD), pl.ds(LEAD, rows - LEAD)
    cut = tail_up.shape[0]
    low_cut, high_cut = pl.ds(0, cut), pl.ds(cut, rows - LEAD - cut)

    def to(src, dst, target):
        return mover.send(src, dst, device_at(target))

    load_own = mover.local(source, own)
    crossing = []
    for at in (across, plus, minus, me):
        crossing.append((to(source.at[at["z"], other, tail], pairs.at[at["z"]], mate), at))
    up = to(source.at[across["z"], 0, lead], hop_up, plus)
    down = to(source.at[across["z"], 1, lead], hop_down, minus)
    plain_up = to(source.at[plus["z"], 1, lead], from_minus.at[1], plus)
    plain_down = to(source.at[minus["z"], 0, lead], from_plus.at[0], minus)
    yield
    load_own.wait()

    def crossed(index):
        slot, at = crossing[index]
        region = pairs.at[at["z"]]
        mover.arrived(slot, region)
        add_into(region, own.at[at["z"], side, tail])
        return region

    region = crossed(0)
    t_up = to(region.at[low_cut], tail_up, plus)
    t_down = to(region.at[high_cut], tail_down, minus)
    region = crossed(1)
    t_plain_up = to(region.at[high_cut], tail_minus.at[high_cut], plus)
    region = crossed(2)
    t_plain_down = to(region.at[low_cut], tail_plus.at[low_cut], minus)
    yield
    mover.arrived(up, hop_up)
    add_into(hop_up, own.at[plus["z"], 0, lead])
    up = to(hop_up, from_minus.at[0], plus)
    mover.arrived(down, hop_down)
    add_into(hop_down, own.at[minus["z"], 1, lead])
    down = to(hop_down, from_plus.at[1], minus)
    yield
    mover.arrived(t_up, tail_up)
    add_into(tail_up, pairs.at[plus["z"], low_cut])
    t_up = to(tail_up, tail_minus.at[low_cut], plus)
    mover.arrived(t_down, tail_down)
    add_into(tail_down, pairs.at[minus["z"], high_cut])
    t_down = to(tail_down, tail_plus.at[high_cut], minus)
    yield
    mover.arrived(plain_up, from_minus.at[1])
    mover.arrived(plain_down, from_plus.at[0])
    mover.arrived(up, from_minus.at[0])
    mover.arrived(down, from_plus.at[1])
    add_into(from_minus, from_plus, own.at[me["z"], :, lead])
    last = to(from_minus.at[other], from_mate, mate)
    yield
    region = crossed(3)
    mover.arrived(t_plain_up, tail_minus.at[high_cut])
    mover.arrived(t_plain_down, tail_plus.at[low_cut])
    mover.arrived(t_up, tail_minus.at[low_cut])
    mover.arrived(t_down, tail_plus.at[high_cut])
    out[LEAD:, :] = load(region) + load(tail_minus) + load(tail_plus)
    yield
    mover.arrived(last, from_mate)
    out[:LEAD, :] = load(from_minus.at[side]) + load(from_mate)


def tail_kernel(
    g_qkv, qkv_momentum, s_out, s_gate, s_up, s_down, grad_normed,
    stream, grad_residual, gains, gain_two,
    moment_out, o_q, o_k, o_v, o_out, o_gate, o_up, o_down, input_grad, gain_grad,
    send_sems, recv_sems, local_sems, dp_send, dp_recv, own_send, own_recv, back_send, back_recv,
    all_send, all_recv,
    dp_land, qkv_share, wide_in, wide_out, slim_in, slim_out,
    w_gram, w_poly, w_total, w_moving, s_gram, s_poly, s_total, s_moving, norm,
    own, hop_up, hop_down, from_minus, from_plus, from_mate,
    pairs, tail_up, tail_down, tail_minus, tail_plus, summed, gain_dp, gain_mp,
):
    mover = Mover(send_sems, recv_sems, local_sems)
    me = place()
    dp, mp = lax.axis_index("dp"), lax.axis_index("mp")
    mover.anyone = device_at(moved(me, "core", 1))
    rows_to = [((dp + k) % DP, mp) for k in range(1, DP)]
    cols_to = [(dp, (mp + k) % MP) for k in range(1, MP)]
    greet(rows_to + cols_to)

    def remote(src, dst, send, recv, device):
        return pltpu.make_async_remote_copy(
            src_ref=src, dst_ref=dst, send_sem=send, recv_sem=recv, device_id=device, device_id_type=MESH
        )

    results = (o_q, o_k, o_v, o_out, o_gate, o_up, o_down)

    def give(index, share):
        owner = OWNERS[index]
        land = wide_in if COLUMNS[index] == WIDE else slim_in
        copy = remote(share, land.at[dp], own_send.at[index], own_recv.at[dp], (owner, mp))

        @pl.when(dp != owner)
        def away():
            copy.start()

        @pl.when(dp == owner)
        def here():
            land[dp] = share[...]

        return owner, copy

    def settle(given):
        owner, copy = given

        @pl.when(dp != owner)
        def away():
            copy.wait_send()

    def take(index):
        land = wide_in if COLUMNS[index] == WIDE else slim_in
        for k in range(1, DP):
            giver = (dp + k) % DP
            remote(
                land.at[giver], land.at[giver], own_send.at[index], own_recv.at[giver], (giver, mp)
            ).wait_recv()

    def returns(index, wait):
        made = wide_out if COLUMNS[index] == WIDE else slim_out
        for k in range(1, DP):
            taker = (dp + k) % DP
            copy = remote(
                made.at[taker], results[index], back_send.at[taker], back_recv.at[index], (taker, mp)
            )
            copy.wait_send() if wait else copy.start()

    def owned(columns):
        chosen = [i for i in range(len(OWNERS)) if COLUMNS[i] == columns]
        if columns == WIDE:
            steps = newton_steps(wide_in, wide_out, 1.0, w_gram, w_poly, w_total, w_moving, norm)
        else:
            steps = newton_steps(slim_in, slim_out, 1.0, s_gram, s_poly, s_total, s_moving, norm)
        mine = functools.reduce(jnp.logical_or, [dp == OWNERS[i] for i in chosen])
        for index in chosen:
            pl.when(dp == OWNERS[index])(functools.partial(take, index))
        for step in steps:
            pl.when(mine)(step)
            yield
        for index in chosen:
            pl.when(dp == OWNERS[index])(functools.partial(returns, index, False))

            @pl.when(dp == OWNERS[index])
            def keep():
                made = wide_out if COLUMNS[index] == WIDE else slim_out
                results[index][...] = made[dp]

    given = [give(3, s_out), give(4, s_gate), give(5, s_up), give(6, s_down)]

    def qkv_task():
        for k in range(1, DP):
            taker = (dp + k) % DP
            remote(
                g_qkv.at[taker], dp_land.at[dp], dp_send.at[k], dp_recv.at[k], (taker, mp)
            ).start()
        mine = mover.local(g_qkv.at[dp], dp_land.at[dp])
        yield
        yield
        mine.wait()
        for k in range(1, DP):
            giver = (dp + DP - k) % DP
            remote(
                dp_land.at[giver], dp_land.at[giver], dp_send.at[k], dp_recv.at[k], (giver, mp)
            ).wait_recv()
        total = jnp.zeros((SHARE, WIDE), f32)
        for k in range(DP):
            total = total + dp_land[k].astype(f32)
        moment = 0.5 * qkv_momentum[...] + total
        moment_out[...] = moment
        for k in range(3):
            qkv_share[k] = moment[:, k * SLIM : (k + 1) * SLIM].astype(bf16)
        given.extend(give(k, qkv_share.at[k]) for k in range(3))
        yield
        yield from owned(SLIM)

    def gains_task():
        yield from scatter_tokens_part(
            mover, me, grad_normed, own,
            (hop_up, hop_down, from_minus, from_plus, from_mate),
            (pairs, tail_up, tail_down, tail_minus, tail_plus), summed,
        )
        x = stream[...].astype(f32)
        inverse = lax.rsqrt(row_mean(x * x) + norm_epsilon)
        unit = x * inverse
        grad = summed[...]
        scaled = grad * gains[0:1, :]
        input_grad[...] = grad_residual[...] + inverse * (scaled - unit * row_mean(scaled * unit))
        gain_dp[dp] = jnp.concatenate(
            [jnp.sum(grad * unit, axis=0, keepdims=True), gain_two[...]], axis=0
        )
        copies = []
        for k in range(1, DP):
            taker = (dp + k) % DP
            copy = remote(
                gain_dp.at[dp], gain_dp.at[dp], all_send.at[k], all_recv.at[k], (taker, mp)
            )
            copy.start()
            copies.append(copy)
        yield
        for k in range(1, DP):
            giver = (dp + DP - k) % DP
            remote(
                gain_dp.at[giver], gain_dp.at[giver], all_send.at[k], all_recv.at[k], (giver, mp)
            ).wait_recv()
        total = gain_dp[0]
        for k in range(1, DP):
            total = total + gain_dp[k]
        gain_mp[mp] = total
        for k in range(1, MP):
            taker = (mp + k) % MP
            copy = remote(
                gain_mp.at[mp], gain_mp.at[mp], all_send.at[DP + k], all_recv.at[DP + k], (dp, taker)
            )
            copy.start()
            copies.append(copy)
        yield
        for k in range(1, MP):
            giver = (mp + MP - k) % MP
            remote(
                gain_mp.at[giver], gain_mp.at[giver], all_send.at[DP + k], all_recv.at[DP + k],
                (dp, giver),
            ).wait_recv()
        total = gain_mp[0]
        for k in range(1, MP):
            total = total + gain_mp[k]
        gain_grad[...] = total
        for copy in copies:
            copy.wait_send()

    def wide_task():
        yield from owned(WIDE)

    weave(qkv_task(), gains_task(), wide_task())
    for index, owner in enumerate(OWNERS):

        @pl.when(dp != owner)
        def arrive():
            remote(
                results[index], results[index], back_send.at[0], back_recv.at[index], (owner, mp)
            ).wait_recv()

        pl.when(dp == owner)(functools.partial(returns, index, True))
    for k in range(1, DP):
        taker = (dp + k) % DP
        remote(g_qkv.at[taker], dp_land.at[dp], dp_send.at[k], dp_recv.at[k], (taker, mp)).wait_send()
    for one in given:
        settle(one)
    mover.finish()


def tail_block(
    g_qkv, qkv_momentum, s_out, s_gate, s_up, s_down, grad_normed,
    stream, grad_residual, gains, gain_two, collective_id,
):
    slim, wide = (jax.ShapeDtypeStruct((SHARE, c), bf16) for c in (SLIM, WIDE))
    tokens, width = stream.shape
    rest = tokens - LEAD
    cut = (rest // 2 + 15) // 16 * 16
    vm = pltpu.VMEM
    return pl.pallas_call(
        tail_kernel,
        out_shape=(
            jax.ShapeDtypeStruct((SHARE, WIDE), f32), slim, slim, slim, slim, wide, wide, wide,
            jax.ShapeDtypeStruct((tokens, width), f32),
            jax.ShapeDtypeStruct((2, width), f32),
        ),
        in_specs=[ANY] + [VMEM] * 5 + [ANY] + [VMEM] * 4,
        out_specs=[VMEM] * 10,
        scratch_shapes=[
            DMA((17,)), DMA((17,)), DMA((2,)),
            DMA((DP,)), DMA((DP,)),
            DMA((7,)), DMA((DP,)),
            DMA((DP,)), DMA((7,)),
            DMA((DP + MP,)), DMA((DP + MP,)),
            vm((DP, SHARE, WIDE), bf16), vm((3, SHARE, SLIM), bf16),
            vm((DP, SHARE, WIDE), bf16), vm((DP, SHARE, WIDE), bf16),
            vm((DP, SHARE, SLIM), bf16), vm((DP, SHARE, SLIM), bf16),
            vm((WIDE, WIDE), f32), vm((WIDE, WIDE), f32), vm((WIDE, WIDE), f32), vm((DP * SHARE, WIDE), f32),
            vm((SLIM, SLIM), f32), vm((SLIM, SLIM), f32), vm((SLIM, SLIM), f32), vm((DP * SHARE, SLIM), f32),
            vm((8, WIDE), f32),
            vm((4, 2, tokens, width), bf16),
            vm((LEAD, width), bf16), vm((LEAD, width), bf16),
            vm((2, LEAD, width), bf16), vm((2, LEAD, width), bf16), vm((LEAD, width), bf16),
            vm((4, rest, width), bf16), vm((cut, width), bf16), vm((rest - cut, width), bf16),
            vm((rest, width), bf16), vm((rest, width), bf16),
            vm((tokens, width), f32),
            vm((DP, 2, width), f32), vm((MP, 2, width), f32),
        ],
        name="tail_block",
        compiler_params=pltpu.CompilerParams(
            collective_id=collective_id, has_side_effects=True, vmem_limit_bytes=56 * MEGA
        ),
    )(
        g_qkv, qkv_momentum, s_out, s_gate, s_up, s_down, grad_normed,
        stream, grad_residual, gains, gain_two,
    )
STEP = 10
muon_rate = 1.0
out_rate = 4.0
adam_rate = 0.8
beta_first = 0.9
beta_second = 0.95
adam_epsilon = 1e-08


def widen(x):
    return jnp.pad(x, ((0, 0), (0, 384 - x.shape[1])))


def on_device(
    block_input, first_values, out_cotangent, doc_lengths, norm_gains, gain_moment1, gain_moment2,
    qkv_weight, qkv_momentum, out_weight, out_momentum, gate_up_weight, gate_up_momentum,
    down_weight, down_momentum,
):
    tokens, width = block_input.shape
    units = gate_up_weight.shape[2]
    low_gate_up = gate_up_weight.astype(bf16)
    shares = (
        widen(low_gate_up[:, 0]),
        widen(low_gate_up[:, 1]),
        widen(down_weight.astype(bf16).T),
        out_weight.astype(bf16).T,
    )
    *wholes, normed_one, w_qkv, q, k, v, heads_out, lse, heads = front(
        doc_lengths, block_input, norm_gains, shares,
        qkv_weight.astype(bf16).reshape(SHARE, 3 * PAIR), first_values, 0,
    )
    w_gate, w_up, w_down, w_out = (w.reshape(GROUPS, width, w.shape[-1]) for w in wholes)
    normed_one = normed_one.reshape(LEN, width)
    w_qkv = w_qkv.reshape(width, 3 * PAIR)
    block_output, grad_residual, grad_heads, gain_two, g_gate, g_up, g_down, g_out = token_block(
        heads, block_input, out_cotangent, norm_gains, w_gate, w_up, w_down, w_out
    )
    grad_heads = exchange(grad_heads, 2).reshape(LEN, PAIR)
    s_gate, s_up, s_down, s_out = scatter_all(
        [g.reshape(4, 2, 4, 2, 2, 64, g.shape[-1]) for g in (g_gate, g_up, g_down, g_out)], 3
    )
    first_values_grad, g_qkv, grad_normed = attn_backward(
        doc_lengths, q, k, v, heads_out, grad_heads, lse, normed_one, w_qkv
    )
    out_moment_new = 0.5 * out_momentum + s_out.T
    gate_up_moment_new = 0.5 * gate_up_momentum + jnp.stack(
        [s_gate[:, :units], s_up[:, :units]], axis=1
    )
    down_moment_new = 0.5 * down_momentum + s_down[:, :units].T
    low_moment = gate_up_moment_new.astype(bf16)
    moment, o_q, o_k, o_v, o_out, o_gate, o_up, o_down, input_grad, gain_grad = tail_block(
        g_qkv.reshape(DP, SHARE, 3 * PAIR),
        qkv_momentum.reshape(SHARE, 3 * PAIR),
        out_moment_new.T.astype(bf16),
        widen(low_moment[:, 0]),
        widen(low_moment[:, 1]),
        widen(down_moment_new.T.astype(bf16)),
        grad_normed.reshape(4, 2, tokens, width),
        block_input, grad_residual, norm_gains, gain_two, 4,
    )
    qkv_moment_new = moment.reshape(qkv_momentum.shape)
    tall = (width / PAIR) ** 0.5
    broad = (width / units) ** 0.5
    qkv_step = muon_rate * tall * jnp.stack([o_q, o_k, o_v], axis=1).astype(f32)
    out_step = out_rate * o_out.astype(f32).T
    gate_up_step = muon_rate * broad * jnp.stack([o_gate[:, :units], o_up[:, :units]], axis=1).astype(f32)
    down_step = muon_rate * o_down[:, :units].astype(f32).T
    moment1_new = beta_first * gain_moment1 + (1.0 - beta_first) * gain_grad
    moment2_new = beta_second * gain_moment2 + (1.0 - beta_second) * gain_grad * gain_grad
    corrected1 = moment1_new / (1.0 - beta_first**STEP)
    corrected2 = moment2_new / (1.0 - beta_second**STEP)
    gains_new = norm_gains - adam_rate * corrected1 / (jnp.sqrt(corrected2) + adam_epsilon)
    return (
        block_output,
        input_grad,
        first_values_grad,
        qkv_weight - qkv_step,
        qkv_moment_new,
        out_weight - out_step,
        out_moment_new,
        gate_up_weight - gate_up_step,
        gate_up_moment_new,
        down_weight - down_step,
        down_moment_new,
        moment1_new,
        moment2_new,
        gains_new,
    )


def solution(mesh):
    placed = (
        P(("dp", "mp"), None), P("dp", "mp"), P(("dp", "mp"), None), P("dp", None),
        P(), P(), P(),
        P("dp", None, "mp"), P("dp", None, "mp"), P("mp", "dp"), P("mp", "dp"),
        P("dp", None, "mp"), P("dp", None, "mp"), P("mp", "dp"), P("mp", "dp"),
    )
    return jax.shard_map(
        on_device,
        mesh=mesh,
        in_specs=placed,
        out_specs=(P(("dp", "mp"), None), P(("dp", "mp"), None), P("dp", "mp")) + placed[7:] + (P(),) * 3,
        check_vma=False,
    )
```

```python
import functools

import jax
import jax.numpy as jnp
import numpy as np
from jax import lax
from jax.experimental import pallas as pl
from jax.experimental.pallas import tpu as pltpu
from jax.sharding import PartitionSpec as P

MEGA = 2**20
f32, bf16 = jnp.float32, jnp.bfloat16
VMEM = pl.BlockSpec(memory_space=pltpu.VMEM)
SMEM = pl.BlockSpec(memory_space=pltpu.SMEM)

HD = 64
LEN = 2048
PAIR = 2 * HD
BLOCK = 256
BLOCKS = LEN // BLOCK
LOG2E = 1.4426950408889634
SCORE_SCALE = HD**-0.5 * LOG2E
mask_fill = -1e30


def dot(a, b):
    return lax.dot_general(a, b, (((1,), (0,)), ((), ())), preferred_element_type=f32)


def dot_t(a, b):
    return lax.dot_general(a, b, (((1,), (1,)), ((), ())), preferred_element_type=f32)


def frequency():
    half = HD // 2
    return np.tile(np.exp(-np.log(10000.0) * np.arange(half) * 2.0 / HD), PAIR // half)


def angle_tables():
    angles = np.arange(BLOCK)[:, None] * frequency()[None, :]
    return np.cos(angles).astype(np.float32), np.sin(angles).astype(np.float32)


def frequency_row():
    return frequency()[None, :].astype(np.float32)


def doc_starts(lens):
    one = lens[0, 0]
    two = one + lens[0, 1]
    return one, two, two + lens[0, 2]


def pick_start(place, starts):
    zero = jnp.zeros_like(place)
    picked = jnp.where(place >= starts[0], starts[0], zero)
    picked = jnp.where(place >= starts[1], starts[1], picked)
    return jnp.where(place >= starts[2], starts[2], picked)


def turn_tables(starts, freq, turns):
    row = lax.broadcasted_iota(jnp.int32, (4 * BLOCKS, PAIR), 0)
    doc = row % 4
    start = jnp.where(doc == 1, starts[0], 0)
    start = jnp.where(doc == 2, starts[1], start)
    start = jnp.where(doc == 3, starts[2], start)
    angle = (row // 4 * BLOCK - start).astype(f32) * freq
    turns[0] = jnp.cos(angle)
    turns[1] = jnp.sin(angle)


def block_angles(block, starts, turns, cos_ref, sin_ref):
    place = block * BLOCK + lax.broadcasted_iota(jnp.int32, (BLOCK, PAIR), 0)

    def pick(table):
        picked = turns[table, pl.ds(4 * block, 1), :]
        for doc, start in enumerate(starts):
            picked = jnp.where(place >= start, turns[table, pl.ds(4 * block + doc + 1, 1), :], picked)
        return picked

    cos_b, sin_b = pick(0), pick(1)
    return cos_ref[...] * cos_b - sin_ref[...] * sin_b, sin_ref[...] * cos_b + cos_ref[...] * sin_b


def swap_halves(x):
    lane = lax.broadcasted_iota(jnp.int32, x.shape, 1)
    front = lane % HD < HD // 2
    return front, jnp.where(front, pltpu.roll(x, PAIR - HD // 2, 1), pltpu.roll(x, HD // 2, 1))


def rotate(x, cos, sin):
    front, other = swap_halves(x)
    return x * cos + jnp.where(front, -other, other) * sin


def rotate_back(x, cos, sin):
    front, other = swap_halves(x)
    return x * cos + jnp.where(front, other, -other) * sin


def head_only(x, head):
    lane = lax.broadcasted_iota(jnp.int32, x.shape, 1)
    return jnp.where(lane // HD == head, x, jnp.zeros_like(x))


def project_block(block, tokens, w_qkv, first_values, starts, turns, cos_ref, sin_ref, q_ref, k_ref, v_ref, vt):
    rows = slice(block * BLOCK, (block + 1) * BLOCK)
    proj = dot(tokens, w_qkv)
    cos, sin = block_angles(block, starts, turns, cos_ref, sin_ref)
    q_ref[rows, :] = rotate(proj[:, :PAIR], cos, sin).astype(bf16)
    k_ref[rows, :] = rotate(proj[:, PAIR : 2 * PAIR], cos, sin).astype(bf16)
    mix = 0.5 * proj[:, 2 * PAIR :] + 0.5 * first_values[rows, :].astype(f32)
    v_ref[rows, :] = mix.astype(bf16)
    vt[:PAIR, rows] = mix.T.astype(bf16)


def attend_block(block, starts, q_ref, k_ref, vt, out_ref, lse_ref):
    rows = slice(block * BLOCK, (block + 1) * BLOCK)
    span = (block + 1) * BLOCK
    row_at = rows.start + lax.broadcasted_iota(jnp.int32, (1, BLOCK), 1)
    start_row = pick_start(row_at, starts)
    key_at = lax.broadcasted_iota(jnp.int32, (span, BLOCK), 0)
    allowed = (key_at >= start_row) & (key_at <= row_at)
    outs = []
    for head in range(2):
        scores = dot_t(k_ref[:span, :], head_only(q_ref[rows, :], head))
        scores = jnp.where(allowed, scores, mask_fill)
        top = jnp.max(scores, axis=0, keepdims=True) * SCORE_SCALE
        weights = jnp.exp2(scores * SCORE_SCALE - top).astype(bf16)
        values = jnp.concatenate([vt[head * HD : (head + 1) * HD, :span], vt[PAIR:, :span]], axis=0)
        mixed = dot(values, weights)
        total = mixed[HD : HD + 1, :]
        outs.append(mixed[:HD, :] / total)
        lse_ref[head : head + 1, rows] = top + jnp.log2(total)
    out_ref[rows, :] = jnp.concatenate(outs, axis=0).T.astype(bf16)


def attend_back(
    starts, q_ref, k_ref, v_ref, heads_ref, grad_ref, lse_ref, normed, w_qkv, cos_ref, sin_ref, turns,
    values_grad_ref, w_grad_ref, normed_grad_ref, kt, dqt, dk_ref, delta, dproj_t,
):
    for block in range(BLOCKS):
        rows = slice(block * BLOCK, (block + 1) * BLOCK)
        kt[:, rows] = k_ref[rows, :].astype(f32).T.astype(bf16)
        both = (grad_ref[rows, :].astype(f32) * heads_ref[rows, :].astype(f32)).T
        for head in range(2):
            delta[head : head + 1, rows] = jnp.sum(
                both[head * HD : (head + 1) * HD, :], axis=0, keepdims=True
            )
    dqt[...] = jnp.zeros_like(dqt)
    yield
    chunk = 2 * BLOCK
    for block in range(BLOCKS):
        keys = slice(block * BLOCK, (block + 1) * BLOCK)
        dk = jnp.zeros((BLOCK, PAIR), f32)
        dv = jnp.zeros((BLOCK, PAIR), f32)
        at = block * BLOCK
        while at < LEN:
            width = chunk if at % chunk == 0 else BLOCK
            rows = slice(at, at + width)
            at += width
            row_at = rows.start + lax.broadcasted_iota(jnp.int32, (1, width), 1)
            start_row = pick_start(row_at, starts)
            key_at = keys.start + lax.broadcasted_iota(jnp.int32, (BLOCK, width), 0)
            allowed = key_at >= start_row
            if rows.start == keys.start:
                allowed = allowed & (key_at <= row_at)
            for head in range(2):
                q_h = head_only(q_ref[rows, :], head)
                g_h = head_only(grad_ref[rows, :], head)
                scores = dot_t(k_ref[keys, :], q_h)
                prob = jnp.exp2(scores * SCORE_SCALE - lse_ref[head : head + 1, rows])
                prob = jnp.where(allowed, prob, 0.0)
                grad_prob = dot_t(v_ref[keys, :], g_h)
                grad_scores = (prob * (grad_prob - delta[head : head + 1, rows])).astype(bf16)
                dv = dv + dot(prob.astype(bf16), g_h)
                dk = dk + dot(grad_scores, q_h)
                lanes = slice(head * HD, (head + 1) * HD)
                dqt[lanes, rows] += dot(kt[lanes, keys], grad_scores)
        dk_ref[keys, :] = dk
        values_grad_ref[keys, :] = 0.5 * dv
        yield
    for block in range(BLOCKS):
        rows = slice(block * BLOCK, (block + 1) * BLOCK)
        cos, sin = block_angles(block, starts, turns, cos_ref, sin_ref)
        dq = rotate_back(dqt[:, rows].T * HD**-0.5, cos, sin)
        dk = rotate_back(dk_ref[rows, :] * HD**-0.5, cos, sin)
        dproj = jnp.concatenate([dq, dk, values_grad_ref[rows, :]], axis=1)
        dproj_t[:, rows] = dproj.T.astype(bf16)
        normed_grad_ref[block // 2, block % 2] = dot_t(dproj.astype(bf16), w_qkv).astype(bf16)
    yield
    for part in range(4):
        cols = slice(part * BLOCK, (part + 1) * BLOCK)
        tokens = normed[:, :, :, cols].reshape(LEN, BLOCK)
        made = dot(dproj_t[...], tokens).T.astype(bf16)
        w_grad_ref[part * 4 : (part + 1) * 4] = made.reshape(4, BLOCK // 4, 3 * PAIR)


MESH = pl.DeviceIdType.MESH
ANY = pl.BlockSpec(memory_space=pl.ANY)
DMA = pltpu.SemaphoreType.DMA


def place():
    dp, mp = lax.axis_index("dp"), lax.axis_index("mp")
    return {"x": (dp // 2) % 2 * 2 + mp % 2, "y": dp // 4, "z": mp // 2, "core": dp % 2}


def device_at(at):
    return ((at["y"] * 2 + at["x"] // 2) * 2 + at["core"], at["z"] * 2 + at["x"] % 2)


def moved(at, axis, step):
    new = dict(at)
    if axis == "core":
        new[axis] = 1 - at[axis]
    elif axis == "pair":
        new["x"] = at["x"] + 1 - 2 * (at["x"] % 2)
    else:
        new[axis] = (at[axis] + step + 4) % 4
    return new


def greet(devices):
    barrier = pltpu.get_barrier_semaphore()
    for device in devices:
        pl.semaphore_signal(barrier, inc=1, device_id=device, device_id_type=MESH)
    pl.semaphore_wait(barrier, len(devices))


class Mover:
    def __init__(self, send_sems, recv_sems, local_sems=None):
        self.send_sems, self.recv_sems, self.local_sems = send_sems, recv_sems, local_sems
        self.used, self.locals, self.started = 0, 0, []

    def remote(self, src, dst, device, slot):
        return pltpu.make_async_remote_copy(
            src_ref=src,
            dst_ref=dst,
            send_sem=self.send_sems.at[slot],
            recv_sem=self.recv_sems.at[slot],
            device_id=device,
            device_id_type=MESH,
        )

    def send(self, src, dst, device):
        slot = self.used
        self.used += 1
        copy = self.remote(src, dst, device, slot)
        copy.start()
        self.started.append(copy)
        return slot

    def arrived(self, slot, region):
        self.remote(region, region, self.anyone, slot).wait_recv()

    def local(self, src, dst):
        copy = pltpu.make_async_copy(src, dst, self.local_sems.at[self.locals])
        self.locals += 1
        copy.start()
        return copy

    def finish(self):
        for copy in self.started:
            copy.wait_send()


def weave(*tasks):
    tasks = list(tasks)
    while tasks:
        for task in list(tasks):
            try:
                next(task)
            except StopIteration:
                tasks.remove(task)


def blocks_of(ref, at, whole, half=None, core=True):
    index = (
        slice(None) if "z" in whole else at["z"],
        slice(None) if "x" in whole else at["x"] % 2,
        slice(None) if "y" in whole else at["y"],
        slice(None) if "x" in whole else at["x"] // 2,
    )
    if core:
        index = index + (at["core"],)
    if half is not None:
        rows = ref.shape[-2] // 2
        index = index + (pl.ds(half * rows, rows),)
    return ref.at[index]


GATHER_ORDERS = (("x", "z", "y"), ("z", "x", "y"), ("y", "x", "z"), ("y", "z", "x"))
ORDERS = (("x", "y", "z"), ("y", "z", "x"), ("z", "x", "y"), ("y", "x", "z"))
RING = ("x", "y", "z")


def ring_ends(me):
    return [moved(me, axis, step) for axis in RING for step in (1, -1)] + [moved(me, "core", 1)]


def gather_part(mover, me, part, whole, order):
    sibling = moved(me, "core", 1)
    mirrors = []

    def mirror(at, done):
        mine = blocks_of(whole, at, done)
        slot = mover.send(mine, mine, device_at(sibling))
        mirrors.append((slot, blocks_of(whole, moved(at, "core", 1), done)))

    own = blocks_of(whole, me, ())
    mover.local(part, own).wait()
    for phase, axis in enumerate(order):
        done = order[:phase]
        plus, minus, across = moved(me, axis, 1), moved(me, axis, -1), moved(me, axis, 2)
        mine = blocks_of(whole, me, done)
        up = mover.send(mine, mine, device_at(plus))
        down = mover.send(mine, mine, device_at(minus))
        if phase == 2:
            mirror(me, done)
        yield
        relay = blocks_of(whole, minus, done)
        mover.arrived(up, relay)
        relay = blocks_of(whole, minus, done, 0)
        up = mover.send(relay, relay, device_at(plus))
        relay = blocks_of(whole, plus, done)
        mover.arrived(down, relay)
        relay = blocks_of(whole, plus, done, 1)
        down = mover.send(relay, relay, device_at(minus))
        if phase == 2:
            mirror(minus, done)
            mirror(plus, done)
        yield
        mover.arrived(up, blocks_of(whole, across, done, 0))
        mover.arrived(down, blocks_of(whole, across, done, 1))
        if phase == 2:
            mirror(across, done)
    yield
    for slot, region in mirrors:
        mover.arrived(slot, region)


LEAD = 144


def gather_tokens_part(mover, me, whole):
    mate, plus, minus, across = (
        moved(me, "pair", 1),
        moved(me, "z", 1),
        moved(me, "z", -1),
        moved(me, "z", 2),
    )
    rows = whole.shape[-2]
    rest = rows - LEAD
    cut = (rest // 2 + 15) // 16 * 16
    lead, tail = pl.ds(0, LEAD), pl.ds(LEAD, rest)
    tails = (pl.ds(LEAD, cut), pl.ds(LEAD + cut, rest - cut))

    def at(place_, span):
        return whole.at[place_["z"], place_["x"] % 2, span]

    def both(place_, side=None):
        return whole.at[place_["z"], slice(None) if side is None else side, lead]

    def pass_on(region, target):
        return mover.send(region, region, device_at(target))

    pair = pass_on(at(me, lead), mate)
    ring = pass_on(at(me, tail), plus), pass_on(at(me, tail), minus)
    crossed = [(pass_on(at(me, tail), mate), at(moved(me, "pair", 1), tail))]
    yield
    mover.arrived(pair, at(mate, lead))
    wide = pass_on(both(me), plus), pass_on(both(me), minus)
    yield
    mover.arrived(ring[0], at(minus, tail))
    relay = [pass_on(at(minus, tails[0]), plus)]
    crossed.append((pass_on(at(minus, tail), mate), at(moved(minus, "pair", 1), tail)))
    mover.arrived(ring[1], at(plus, tail))
    relay.append(pass_on(at(plus, tails[1]), minus))
    crossed.append((pass_on(at(plus, tail), mate), at(moved(plus, "pair", 1), tail)))
    yield
    mover.arrived(relay[0], at(across, tails[0]))
    mover.arrived(relay[1], at(across, tails[1]))
    crossed.append((pass_on(at(across, tail), mate), at(moved(across, "pair", 1), tail)))
    yield
    mover.arrived(wide[0], both(minus))
    last = [pass_on(both(minus, 0), plus)]
    mover.arrived(wide[1], both(plus))
    last.append(pass_on(both(plus, 1), minus))
    yield
    for slot, region in crossed:
        mover.arrived(slot, region)
    mover.arrived(last[0], both(across, 0))
    mover.arrived(last[1], both(across, 1))


def load(ref):
    return ref[...].astype(f32)


def each_block(ref, body):
    lead = ref.shape[:-2]
    total = 1
    for size in lead:
        total *= size

    def step(flat, carry):
        index = []
        for size in reversed(lead):
            index.append(flat % size)
            flat = flat // size
        body(tuple(reversed(index)))
        return carry

    if total == 1:
        body((0,) * len(lead))
    else:
        lax.fori_loop(0, total, step, 0)


def add_into(target, *terms):
    def body(index):
        total = target[index].astype(f32)
        for term in terms:
            total = total + term[index].astype(f32)
        target[index] = total.astype(target.dtype)

    each_block(target, body)


def scatter_part(mover, me, kept, lands, out, order):
    for phase, axis in enumerate(order):
        rest = order[phase + 1 :]
        plus, minus, across = moved(me, axis, 1), moved(me, axis, -1), moved(me, axis, 2)
        hop_up, hop_down, from_minus, from_plus = lands[phase]
        rows = kept.shape[-2] // 2

        def part(at, half=None):
            return blocks_of(kept, at, rest, half, core=False)

        def half_of(ref, half):
            lead = (slice(None),) * (len(ref.shape) - 2)
            return ref.at[lead + (pl.ds(half * rows, rows),)]

        up = mover.send(part(across, 0), hop_up, device_at(plus))
        down = mover.send(part(across, 1), hop_down, device_at(minus))
        plain_up = mover.send(part(plus, 1), half_of(from_minus, 1), device_at(plus))
        plain_down = mover.send(part(minus, 0), half_of(from_plus, 0), device_at(minus))
        yield
        mover.arrived(up, hop_up)
        add_into(part(plus, 0), hop_up)
        up = mover.send(part(plus, 0), half_of(from_minus, 0), device_at(plus))
        mover.arrived(down, hop_down)
        add_into(part(minus, 1), hop_down)
        down = mover.send(part(minus, 1), half_of(from_plus, 1), device_at(minus))
        yield
        mover.arrived(plain_up, half_of(from_minus, 1))
        mover.arrived(plain_down, half_of(from_plus, 0))
        mover.arrived(up, half_of(from_minus, 0))
        mover.arrived(down, half_of(from_plus, 1))
        if phase < 2:
            add_into(part(me), from_minus, from_plus)
        else:
            out[...] = load(part(me)) + load(from_minus) + load(from_plus)


def lead_shape(whole):
    shape = ()
    for axis, size in (("z", 4), ("x", 2), ("y", 4), ("x", 2)):
        if axis in whole:
            shape = shape + (size,)
    return shape

norm_epsilon = 1e-06
GROUPS = 8
DP, MP = 16, 8
SHARE = 64
WIDE, SLIM = 384, 128


def row_mean(x):
    return jnp.mean(x, axis=-1, keepdims=True)


def token_kernel(
    heads, stream, cotangent, gains, w_gate, w_up, w_down, w_out,
    block_output, grad_residual, grad_heads, gain_part, k_gate, k_up, k_down, k_out,
    residual, normed, normed_t, cot_t, ffn, grad_normed,
    made, twin, made_out, twin_out, send_sems, recv_sems, out_sems,
):
    group = pl.program_id(0)
    gain = gains[1:2, :]
    me = place()
    sibling = device_at(moved(me, "core", 1))

    def pass_half(m):
        return [
            pltpu.make_async_remote_copy(
                src_ref=made.at[m % 2, k, :, 1 - me["core"]],
                dst_ref=twin.at[m, k],
                send_sem=send_sems.at[m, k],
                recv_sem=recv_sems.at[m, k],
                device_id=sibling,
                device_id_type=MESH,
            )
            for k in range(3)
        ]

    def pass_out():
        return pltpu.make_async_remote_copy(
            src_ref=made_out.at[:, :, 1 - me["core"]],
            dst_ref=twin_out,
            send_sem=out_sems.at[0],
            recv_sem=out_sems.at[1],
            device_id=sibling,
            device_id_type=MESH,
        )

    @pl.when(group == 0)
    def first():
        greet([sibling])
        branch = jnp.zeros(residual.shape, f32)
        for m in range(GROUPS):
            branch = branch + dot_t(heads[m], w_out[m]).astype(bf16).astype(f32)
        total = stream[...].astype(f32) + branch
        residual[...] = total
        unit = total * lax.rsqrt(row_mean(total * total) + norm_epsilon)
        scaled = unit * gain
        normed[...] = scaled.astype(bf16)
        normed_t[...] = scaled.T.astype(bf16)
        cot_t[...] = cotangent[...].astype(f32).T.astype(bf16)
        ffn[...] = jnp.zeros_like(ffn)
        grad_normed[...] = jnp.zeros_like(grad_normed)

    @pl.when(group < GROUPS)
    def one():
        gate = dot(normed[...], w_gate[0])
        up = dot(normed[...], w_up[0])
        sigmoid = jax.nn.sigmoid(gate)
        silu = gate * sigmoid
        hidden = (silu * up).astype(bf16)
        ffn[...] += dot_t(hidden, w_down[0]).astype(bf16).astype(f32)
        grad_hidden = dot(cotangent[...], w_down[0])
        slope = sigmoid * (1.0 + gate * (1.0 - sigmoid))
        grad_gate = (grad_hidden * up * slope).astype(bf16)
        grad_up = (grad_hidden * silu).astype(bf16)
        grad_normed[...] += dot_t(grad_gate, w_gate[0]) + dot_t(grad_up, w_up[0])
        half = group % 2
        shape = made.shape[2:]
        made[half, 0] = dot(normed_t[...], grad_gate).astype(bf16).reshape(shape)
        made[half, 1] = dot(normed_t[...], grad_up).astype(bf16).reshape(shape)
        made[half, 2] = dot(cot_t[...], hidden).astype(bf16).reshape(shape)
        for copy in pass_half(group):
            copy.start()

    @pl.when(group == GROUPS - 1)
    def last():
        total = residual[...]
        block_output[...] = (total + ffn[...]).astype(bf16)
        inverse = lax.rsqrt(row_mean(total * total) + norm_epsilon)
        unit = total * inverse
        grad = grad_normed[...]
        gain_part[...] = jnp.sum(grad * unit, axis=0, keepdims=True)
        scaled = grad * gain
        result = cotangent[...].astype(f32) + inverse * (scaled - unit * row_mean(scaled * unit))
        grad_residual[...] = result
        low = result.astype(bf16)
        low_t = result.T.astype(bf16)
        for m in range(GROUPS):
            made_out[m] = dot(low_t, heads[m]).astype(bf16).reshape(made_out.shape[1:])
        pass_out().start()
        for m in range(GROUPS):
            grad_heads[m] = dot(low, w_out[m]).astype(bf16)

    @pl.when(group > 0)
    def join():
        before = group - 1
        for k, (copy, kept) in enumerate(zip(pass_half(before), (k_gate, k_up, k_down))):
            copy.wait_recv()
            own = made[before % 2, k, :, me["core"]].astype(f32)
            kept[0] = (own + twin[before, k].astype(f32)).astype(bf16)
        for copy in pass_half(before):
            copy.wait_send()

    @pl.when(group == GROUPS)
    def join_out():
        copy = pass_out()
        copy.wait_recv()
        for m in range(GROUPS):
            own = made_out[m, :, me["core"]].astype(f32)
            k_out[m] = (own + twin_out[m].astype(f32)).astype(bf16)
        copy.wait_send()


def token_block(heads, stream, cotangent, gains, w_gate, w_up, w_down, w_out, collective_id):
    tokens, width = stream.shape
    hidden = w_gate.shape[2]
    slim = w_out.shape[2]
    pairs = width // SHARE // 2
    whole = lambda shape: pl.BlockSpec(shape, lambda m: (0,) * len(shape))
    each = pl.BlockSpec((1, width, hidden), lambda m: (jnp.minimum(m, GROUPS - 1), 0, 0))
    kept = pl.BlockSpec((1, pairs, SHARE, hidden), lambda m: (jnp.maximum(m - 1, 0), 0, 0, 0))
    flat = (tokens, width)
    vm = pltpu.VMEM
    return pl.pallas_call(
        token_kernel,
        grid=(GROUPS + 1,),
        in_specs=[whole(heads.shape), whole(flat), whole(flat), whole(gains.shape)]
        + [each] * 3
        + [whole(w_out.shape)],
        out_specs=[whole(flat), whole(flat), whole(heads.shape), whole((1, width))]
        + [kept] * 3
        + [whole((GROUPS, pairs, SHARE, slim))],
        out_shape=[
            jax.ShapeDtypeStruct(flat, bf16),
            jax.ShapeDtypeStruct(flat, f32),
            jax.ShapeDtypeStruct(heads.shape, bf16),
            jax.ShapeDtypeStruct((1, width), f32),
        ]
        + [jax.ShapeDtypeStruct((GROUPS, pairs, SHARE, hidden), bf16)] * 3
        + [jax.ShapeDtypeStruct((GROUPS, pairs, SHARE, slim), bf16)],
        scratch_shapes=[
            vm(flat, f32), vm(flat, bf16), vm((width, tokens), bf16), vm((width, tokens), bf16),
            vm(flat, f32), vm(flat, f32),
            vm((2, 3, pairs, 2, SHARE, hidden), bf16), vm((GROUPS, 3, pairs, SHARE, hidden), bf16),
            vm((GROUPS, pairs, 2, SHARE, slim), bf16), vm((GROUPS, pairs, SHARE, slim), bf16),
            DMA((GROUPS, 3)), DMA((GROUPS, 3)), DMA((2,)),
        ],
        name="token_block",
        compiler_params=pltpu.CompilerParams(
            collective_id=collective_id, has_side_effects=True, vmem_limit_bytes=58 * MEGA
        ),
    )(heads, stream, cotangent, gains, w_gate, w_up, w_down, w_out)


def gather_row_part(mover, me, whole):
    plus, minus, across = moved(me, "y", 1), moved(me, "y", -1), moved(me, "y", 2)
    far, sibling = moved(me, "x", 2), moved(me, "core", 1)

    def one(at, half=None):
        region = whole.at[at["y"], at["x"] // 2, at["core"]]
        return region if half is None else region.at[pl.ds(half * (SHARE // 2), SHARE // 2)]

    def column(at):
        return whole.at[:, at["x"] // 2, at["core"]]

    def pass_on(region, target):
        return mover.send(region, region, device_at(target))

    ring = pass_on(one(me), plus), pass_on(one(me), minus)
    yield
    mover.arrived(ring[0], one(minus))
    relay = [pass_on(one(minus, 0), plus)]
    mover.arrived(ring[1], one(plus))
    relay.append(pass_on(one(plus, 1), minus))
    yield
    mover.arrived(relay[0], one(across, 0))
    mover.arrived(relay[1], one(across, 1))
    half = pass_on(column(me), far)
    mirrors = [(pass_on(column(me), sibling), column(sibling))]
    yield
    mover.arrived(half, column(far))
    mirrors.append((pass_on(column(far), sibling), column(moved(far, "core", 1))))
    yield
    for slot, region in mirrors:
        mover.arrived(slot, region)


def front_kernel(
    lens, stream, gains, s_gate, s_up, s_down, s_out, s_qkv, first_values, cos_ref, sin_ref, freq,
    w_gate, w_up, w_down, w_out, normed, w_qkv, q_ref, k_ref, v_ref, out_ref, lse_ref, heads,
    send_sems, recv_sems, local_sems, head_send, head_recv, vt, turns,
):
    me = place()
    dp, mp = lax.axis_index("dp"), lax.axis_index("mp")
    mover = Mover(send_sems, recv_sems, local_sems)
    mover.anyone = device_at(moved(me, "core", 1))
    x = stream[...].astype(f32)
    unit = x * lax.rsqrt(row_mean(x * x) + norm_epsilon)
    normed[me["z"], me["x"] % 2] = (unit * gains[0:1, :]).astype(bf16)
    w_qkv[me["y"], me["x"] // 2, me["core"]] = s_qkv[...]
    cols_to = [(dp, (mp + k) % MP) for k in range(1, MP)]
    others = [moved(me, axis, step) for axis in ("x", "y") for step in (1, -1)]
    others += [moved(me, "core", 1), moved(me, "x", 2)]
    greet(cols_to + [device_at(end) for end in others])

    tokens = gather_tokens_part(mover, me, normed)
    row = gather_row_part(mover, me, w_qkv)
    parts = [
        gather_part(mover, me, part, whole, order)
        for part, whole, order in zip(
            (s_gate, s_up, s_down, s_out), (w_gate, w_up, w_down, w_out), GATHER_ORDERS
        )
    ]
    starts = doc_starts(lens)

    def step(*tasks):
        for task in tasks:
            next(task, None)

    step(tokens, row, *parts)
    turn_tables(starts, freq[...], turns)
    vt[PAIR:, :] = jnp.ones((16, LEN), bf16)
    lse_ref[...] = jnp.zeros_like(lse_ref)
    step(row, *parts)
    step(tokens, row, *parts)
    step(tokens, row, *parts)
    step(tokens, *parts)
    step(tokens, row)
    step(tokens)
    weights = w_qkv[...].reshape(DP * SHARE, 3 * PAIR)
    for block in range(BLOCKS):
        project_block(
            block, normed[block // 2, block % 2], weights, first_values, starts, turns,
            cos_ref, sin_ref, q_ref, k_ref, v_ref, vt,
        )
    for block in range(BLOCKS):
        attend_block(block, starts, q_ref, k_ref, vt, out_ref, lse_ref)
        if block >= 4:
            step(parts[block - 4])
    copies = []
    for k in (5, 3, 4, 2, 6, 7, 1):
        taker = (mp + k) % MP
        copy = pltpu.make_async_remote_copy(
            src_ref=out_ref.at[pl.ds(pl.multiple_of(taker * BLOCK, BLOCK), BLOCK)],
            dst_ref=heads.at[mp],
            send_sem=head_send.at[k],
            recv_sem=head_recv.at[k],
            device_id=(dp, taker),
            device_id_type=MESH,
        )
        copy.start()
        copies.append(copy)
    heads[mp] = out_ref[pl.ds(pl.multiple_of(mp * BLOCK, BLOCK), BLOCK), :]
    step(*parts)
    for k in range(1, MP):
        giver = (mp + MP - k) % MP
        pltpu.make_async_remote_copy(
            src_ref=heads.at[giver],
            dst_ref=heads.at[giver],
            send_sem=head_send.at[k],
            recv_sem=head_recv.at[k],
            device_id=(dp, giver),
            device_id_type=MESH,
        ).wait_recv()
    step(*parts)
    for copy in copies:
        copy.wait_send()
    mover.finish()


def front(lens, stream, gains, shares, s_qkv, first_values, collective_id):
    cos, sin = angle_tables()
    flat = jax.ShapeDtypeStruct((LEN, PAIR), bf16)
    vm = pltpu.VMEM
    slots = 16 * len(shares) + 13 + 8
    return pl.pallas_call(
        front_kernel,
        out_shape=[jax.ShapeDtypeStruct((4, 2, 4, 2, 2) + p.shape, p.dtype) for p in shares]
        + [
            jax.ShapeDtypeStruct((4, 2) + stream.shape, bf16),
            jax.ShapeDtypeStruct((4, 2, 2) + s_qkv.shape, bf16),
            flat, flat, flat, flat,
            jax.ShapeDtypeStruct((8, LEN), f32),
            jax.ShapeDtypeStruct((MP, BLOCK, PAIR), bf16),
        ],
        in_specs=[SMEM, VMEM, VMEM] + [ANY] * len(shares) + [VMEM] * 5,
        out_specs=[ANY] * len(shares) + [VMEM] * 8,
        scratch_shapes=[
            DMA((slots,)), DMA((slots,)), DMA((len(shares),)), DMA((MP,)), DMA((MP,)),
            vm((PAIR + 16, LEN), bf16), vm((2, 4 * BLOCKS, PAIR), f32),
        ],
        name="front",
        compiler_params=pltpu.CompilerParams(
            collective_id=collective_id, has_side_effects=True, vmem_limit_bytes=56 * MEGA
        ),
    )(lens, stream, gains, *shares, s_qkv, first_values, cos, sin, frequency_row())

newton_a = 3.4445
newton_b = -4.775
newton_c = 2.0315
OWNERS = (12, 2, 6, 10, 0, 4, 8)
COLUMNS = (SLIM, SLIM, SLIM, SLIM, WIDE, WIDE, WIDE)
ASPECTS = (8.0, 8.0, 8.0, 1.0, 1024 / 352, 1024 / 352, 1.0)


def halves(x):
    high = x.astype(bf16)
    return high, (x - high.astype(f32)).astype(bf16)


def times(a, b, kind=dot):
    (a_high, a_low), (b_high, b_low) = halves(a), halves(b)
    return kind(a_high, b_high) + (kind(a_high, b_low) + kind(a_low, b_high))


def newton_steps(stacked, result, scale, gram, poly, total, moving, norm):
    size = stacked.shape[-1]
    rows = DP * SHARE

    def held():
        return stacked[...].reshape(rows, size)

    def polynomial():
        one = gram[...]
        rank = lax.broadcasted_iota(jnp.int32, (size, size), 0)
        file = lax.broadcasted_iota(jnp.int32, (size, size), 1)
        poly[...] = (
            jnp.where(rank == file, newton_a, 0.0) + newton_b * one + newton_c * times(one, one)
        )

    def advance():
        step = poly[...]
        gram[...] = times(times(step, gram[...]), step)

    def gather():
        total[...] = times(poly[...], total[...])

    def begin():
        block = held()
        wide = block.astype(f32)
        length = jnp.sqrt(jnp.sum(wide * wide)) + 1e-07
        inverse = jnp.full((1, size), 1.0, f32) / length
        norm[0:1, :size] = inverse
        turned = wide.T.astype(bf16)
        gram[...] = dot(turned, block) * (inverse * inverse)

    def first():
        polynomial()
        total[...] = poly[...]

    def middle():
        high, low = halves(total[...])
        block = held()
        moving[...] = (dot(block, high) + dot(block, low)) * norm[0:1, :size]

    def regram():
        now = moving[...]
        high, low = halves(now)
        turned = now.T
        turned_high, turned_low = halves(turned)
        gram[...] = dot(turned_high, high) + (dot(turned_high, low) + dot(turned_low, high))

    def end():
        ending = times(moving[...], total[...]) * scale
        result[...] = ending.astype(bf16).reshape(DP, SHARE, size)

    return [
        begin, first, advance, polynomial, gather, middle, regram,
        first, advance, polynomial, gather, advance, polynomial, gather, end,
    ]


def scatter_tokens_part(mover, me, own, lead_lands, tail_lands, out):
    mate, plus, minus, across = (
        moved(me, "pair", 1),
        moved(me, "z", 1),
        moved(me, "z", -1),
        moved(me, "z", 2),
    )
    side, other = me["x"] % 2, mate["x"] % 2
    hop_up, hop_down, from_minus, from_plus, from_mate = lead_lands
    pairs, tail_up, tail_down, tail_minus, tail_plus = tail_lands
    rows = own.shape[-2]
    lead, tail = pl.ds(0, LEAD), pl.ds(LEAD, rows - LEAD)
    cut = tail_up.shape[0]
    low_cut, high_cut = pl.ds(0, cut), pl.ds(cut, rows - LEAD - cut)

    def to(src, dst, target):
        return mover.send(src, dst, device_at(target))

    crossing = []
    for at in (across, plus, minus, me):
        crossing.append((to(own.at[at["z"], other, tail], pairs.at[at["z"]], mate), at))
    up = to(own.at[across["z"], 0, lead], hop_up, plus)
    down = to(own.at[across["z"], 1, lead], hop_down, minus)
    plain_up = to(own.at[plus["z"], 1, lead], from_minus.at[1], plus)
    plain_down = to(own.at[minus["z"], 0, lead], from_plus.at[0], minus)
    yield

    def crossed(index):
        slot, at = crossing[index]
        region = pairs.at[at["z"]]
        mover.arrived(slot, region)
        add_into(region, own.at[at["z"], side, tail])
        return region

    region = crossed(0)
    t_up = to(region.at[low_cut], tail_up, plus)
    t_down = to(region.at[high_cut], tail_down, minus)
    region = crossed(1)
    t_plain_up = to(region.at[high_cut], tail_minus.at[high_cut], plus)
    region = crossed(2)
    t_plain_down = to(region.at[low_cut], tail_plus.at[low_cut], minus)
    yield
    mover.arrived(up, hop_up)
    add_into(hop_up, own.at[plus["z"], 0, lead])
    up = to(hop_up, from_minus.at[0], plus)
    mover.arrived(down, hop_down)
    add_into(hop_down, own.at[minus["z"], 1, lead])
    down = to(hop_down, from_plus.at[1], minus)
    yield
    mover.arrived(t_up, tail_up)
    add_into(tail_up, pairs.at[plus["z"], low_cut])
    t_up = to(tail_up, tail_minus.at[low_cut], plus)
    mover.arrived(t_down, tail_down)
    add_into(tail_down, pairs.at[minus["z"], high_cut])
    t_down = to(tail_down, tail_plus.at[high_cut], minus)
    yield
    mover.arrived(plain_up, from_minus.at[1])
    mover.arrived(plain_down, from_plus.at[0])
    mover.arrived(up, from_minus.at[0])
    mover.arrived(down, from_plus.at[1])
    add_into(from_minus, from_plus, own.at[me["z"], :, lead])
    last = to(from_minus.at[other], from_mate, mate)
    yield
    region = crossed(3)
    mover.arrived(t_plain_up, tail_minus.at[high_cut])
    mover.arrived(t_plain_down, tail_plus.at[low_cut])
    mover.arrived(t_up, tail_minus.at[low_cut])
    mover.arrived(t_down, tail_plus.at[high_cut])
    out[LEAD:, :] = load(region) + load(tail_minus) + load(tail_plus)
    yield
    mover.arrived(last, from_mate)
    out[:LEAD, :] = load(from_minus.at[side]) + load(from_mate)


def link(src, dst, send, recv, device):
    return pltpu.make_async_remote_copy(
        src_ref=src, dst_ref=dst, send_sem=send, recv_sem=recv, device_id=device, device_id_type=MESH
    )


def back_kernel(
    lens, q_ref, k_ref, v_ref, heads_ref, lse_ref, grad_parts, normed, w_qkv, cos_ref, sin_ref, freq,
    k_gate, k_up, k_down, k_out, qkv_momentum, out_momentum, gate_up_momentum, down_momentum,
    stream, gain_two,
    values_grad, m_qkv, m_out, m_gate, m_up, m_down, o_q, o_k, o_v, o_out, o_gate, o_up, o_down,
    summed, gain_grad,
    send_sems, recv_sems, local_sems, head_send, head_recv, dp_send, dp_recv, own_send, own_recv,
    back_send, back_recv, all_send, all_recv,
    turns, grad_heads, kt, dqt, dk_ref, delta, dproj_t, g_qkv, normed_grad,
    dp_land, qkv_share, wide_share, slim_share, wide_in, wide_out, slim_in, slim_out,
    w_gram, w_poly, w_total, w_moving, s_gram, s_poly, s_total, s_moving, norm,
    hop_up, hop_down, from_minus, from_plus, from_mate,
    pairs, tail_up, tail_down, tail_minus, tail_plus, gain_dp, gain_mp, *lands,
):
    mover = Mover(send_sems, recv_sems, local_sems)
    me = place()
    dp, mp = lax.axis_index("dp"), lax.axis_index("mp")
    mover.anyone = device_at(moved(me, "core", 1))
    rows_to = [((dp + k) % DP, mp) for k in range(1, DP)]
    cols_to = [(dp, (mp + k) % MP) for k in range(1, MP)]
    kept_from = (k_gate, k_up, k_down, k_out)
    scratch = [lands[13 * index : 13 * (index + 1)] for index in range(4)]
    loads = [mover.local(source, own[0]) for source, own in zip(kept_from, scratch)]
    greet(rows_to + cols_to + [device_at(moved(me, "x", step)) for step in (1, -1)])

    def rows_of(index):
        return pl.ds(pl.multiple_of(index * BLOCK, BLOCK), BLOCK)

    head_copies = []
    for k in (5, 3, 4, 2, 6, 7, 1):
        taker = (mp + k) % MP
        copy = link(
            grad_parts.at[taker], grad_heads.at[rows_of(mp)], head_send.at[k], head_recv.at[k], (dp, taker)
        )
        copy.start()
        head_copies.append(copy)
    grad_heads[rows_of(mp), :] = grad_parts[mp]

    sums = (m_gate, m_up, m_down, m_out)
    scatters = []
    for index in range(4):
        own = scratch[index]
        phases = [own[1 + 4 * phase : 5 + 4 * phase] for phase in range(3)]
        scatters.append(scatter_part(mover, me, own[0], phases, sums[index], ORDERS[index]))

    def step(*tasks):
        for task in tasks:
            next(task, None)

    for copy, task in zip(loads, scatters):
        copy.wait()
        step(task)
    starts = doc_starts(lens)
    turn_tables(starts, freq[...], turns)
    for k in range(1, MP):
        giver = (mp + MP - k) % MP
        region = grad_heads.at[rows_of(giver)]
        link(region, region, head_send.at[k], head_recv.at[k], (dp, giver)).wait_recv()
    attention = attend_back(
        starts, q_ref, k_ref, v_ref, heads_ref, grad_heads, lse_ref, normed, w_qkv[...], cos_ref, sin_ref,
        turns, values_grad, g_qkv, normed_grad, kt, dqt, dk_ref, delta, dproj_t,
    )
    step(attention, attention, attention)
    step(*scatters)
    for block in range(6):
        step(attention)
    step(*scatters)
    step(attention)
    tokens = scatter_tokens_part(
        mover, me, normed_grad,
        (hop_up, hop_down, from_minus, from_plus, from_mate),
        (pairs, tail_up, tail_down, tail_minus, tail_plus), summed,
    )
    step(tokens)
    step(*scatters)
    step(attention)

    dp_copies = []
    for k in range(1, DP):
        taker = (dp + k) % DP
        copy = link(g_qkv.at[taker], dp_land.at[dp], dp_send.at[k], dp_recv.at[k], (taker, mp))
        copy.start()
        dp_copies.append(copy)
    dp_land[dp] = g_qkv[dp]
    step(*scatters)
    step(tokens)
    step(*scatters)
    step(*scatters)

    results = (o_q, o_k, o_v, o_out, o_gate, o_up, o_down)

    def give(index, share):
        owner = OWNERS[index]
        land = wide_in if COLUMNS[index] == WIDE else slim_in
        copy = link(share, land.at[dp], own_send.at[index], own_recv.at[dp], (owner, mp))

        @pl.when(dp != owner)
        def away():
            copy.start()

        @pl.when(dp == owner)
        def here():
            land[dp] = share[...]

        return owner, copy

    def settle(given):
        owner, copy = given

        @pl.when(dp != owner)
        def away():
            copy.wait_send()

    def take(index):
        land = wide_in if COLUMNS[index] == WIDE else slim_in
        for k in range(1, DP):
            giver = (dp + k) % DP
            region = land.at[giver]
            link(region, region, own_send.at[index], own_recv.at[giver], (giver, mp)).wait_recv()

    def returns(index, wait):
        made = wide_out if COLUMNS[index] == WIDE else slim_out
        for k in range(1, DP):
            taker = (dp + k) % DP
            copy = link(made.at[taker], results[index], back_send.at[taker], back_recv.at[index], (taker, mp))
            copy.wait_send() if wait else copy.start()

    def owned(columns):
        chosen = [i for i in range(len(OWNERS)) if COLUMNS[i] == columns]
        if columns == WIDE:
            steps = newton_steps(wide_in, wide_out, 1.0, w_gram, w_poly, w_total, w_moving, norm)
        else:
            steps = newton_steps(slim_in, slim_out, 1.0, s_gram, s_poly, s_total, s_moving, norm)
        mine = functools.reduce(jnp.logical_or, [dp == OWNERS[i] for i in chosen])
        for index in chosen:
            pl.when(dp == OWNERS[index])(functools.partial(take, index))
        for one in steps:
            pl.when(mine)(one)
            yield
        for index in chosen:
            pl.when(dp == OWNERS[index])(functools.partial(returns, index, False))

            @pl.when(dp == OWNERS[index])
            def keep():
                made = wide_out if COLUMNS[index] == WIDE else slim_out
                results[index][...] = made[dp]

    units = down_momentum.shape[0]
    m_out[...] += 0.5 * out_momentum[...].T
    m_gate[:, :units] += 0.5 * gate_up_momentum[:, 0, :]
    m_up[:, :units] += 0.5 * gate_up_momentum[:, 1, :]
    m_down[:, :units] += 0.5 * down_momentum[...].T
    slim_share[...] = m_out[...].astype(bf16)
    for k, moment in enumerate((m_gate, m_up, m_down)):
        wide_share[k] = moment[...].astype(bf16)
    given = [give(3, slim_share)] + [give(4 + k, wide_share.at[k]) for k in range(3)]
    step(tokens)

    def qkv_task():
        for k in range(1, DP):
            giver = (dp + DP - k) % DP
            region = dp_land.at[giver]
            link(region, region, dp_send.at[k], dp_recv.at[k], (giver, mp)).wait_recv()
        total = jnp.zeros((SHARE, WIDE), f32)
        for k in range(DP):
            total = total + dp_land[k].astype(f32)
        for k in range(3):
            cols = slice(k * SLIM, (k + 1) * SLIM)
            moment = 0.5 * qkv_momentum[:, k, :] + total[:, cols]
            m_qkv[:, cols] = moment
            qkv_share[k] = moment.astype(bf16)
        given.extend(give(k, qkv_share.at[k]) for k in range(3))
        yield
        yield from owned(SLIM)

    def gains_task():
        yield from tokens
        x = stream[...].astype(f32)
        unit = x * lax.rsqrt(row_mean(x * x) + norm_epsilon)
        gain_dp[dp] = jnp.concatenate(
            [jnp.sum(summed[...] * unit, axis=0, keepdims=True), gain_two[...]], axis=0
        )
        copies = []
        for k in range(1, DP):
            copy = link(
                gain_dp.at[dp], gain_dp.at[dp], all_send.at[k], all_recv.at[k], ((dp + k) % DP, mp)
            )
            copy.start()
            copies.append(copy)
        yield
        for k in range(1, DP):
            giver = (dp + DP - k) % DP
            region = gain_dp.at[giver]
            link(region, region, all_send.at[k], all_recv.at[k], (giver, mp)).wait_recv()
        total = gain_dp[0]
        for k in range(1, DP):
            total = total + gain_dp[k]
        gain_mp[mp] = total
        for k in range(1, MP):
            copy = link(
                gain_mp.at[mp], gain_mp.at[mp], all_send.at[DP + k], all_recv.at[DP + k], (dp, (mp + k) % MP)
            )
            copy.start()
            copies.append(copy)
        yield
        for k in range(1, MP):
            giver = (mp + MP - k) % MP
            region = gain_mp.at[giver]
            link(region, region, all_send.at[DP + k], all_recv.at[DP + k], (dp, giver)).wait_recv()
        total = gain_mp[0]
        for k in range(1, MP):
            total = total + gain_mp[k]
        gain_grad[...] = total
        for copy in copies:
            copy.wait_send()

    weave(qkv_task(), gains_task(), owned(WIDE))
    for index, owner in enumerate(OWNERS):

        @pl.when(dp != owner)
        def arrive():
            link(
                results[index], results[index], back_send.at[0], back_recv.at[index], (owner, mp)
            ).wait_recv()

        pl.when(dp == owner)(functools.partial(returns, index, True))
    for copy in head_copies + dp_copies:
        copy.wait_send()
    for one in given:
        settle(one)
    mover.finish()


def back_block(
    lens, q, k, v, heads_out, lse, grad_parts, normed, w_qkv, kept, momenta, stream, gain_two, collective_id,
):
    cos, sin = angle_tables()
    tokens, width = stream.shape
    rest = tokens - LEAD
    cut = (rest // 2 + 15) // 16 * 16
    vm = pltpu.VMEM
    slim, wide = (jax.ShapeDtypeStruct((SHARE, c), bf16) for c in (SLIM, WIDE))
    full = jax.ShapeDtypeStruct((SHARE, WIDE), f32)
    lands = []
    for index, source in enumerate(kept):
        rows, cols = source.shape[-2:]
        lands.append(vm(source.shape, bf16))
        for phase in range(3):
            lead = lead_shape(ORDERS[index][phase + 1 :])
            lands += [vm(lead + (rows // 2, cols), bf16)] * 2 + [vm(lead + (rows, cols), bf16)] * 2
    slots = 18 * len(kept) + 17
    return pl.pallas_call(
        back_kernel,
        out_shape=[
            jax.ShapeDtypeStruct((LEN, PAIR), f32),
            full, jax.ShapeDtypeStruct((SHARE, SLIM), f32), full, full, full,
            slim, slim, slim, slim, wide, wide, wide,
            jax.ShapeDtypeStruct((tokens, width), f32),
            jax.ShapeDtypeStruct((2, width), f32),
        ],
        in_specs=[SMEM] + [VMEM] * 11 + [ANY] * 4 + [VMEM] * 6,
        out_specs=[VMEM] * 15,
        scratch_shapes=[
            DMA((slots,)), DMA((slots,)), DMA((4,)), DMA((MP,)), DMA((MP,)),
            DMA((DP,)), DMA((DP,)), DMA((7,)), DMA((DP,)), DMA((DP,)), DMA((7,)),
            DMA((DP + MP,)), DMA((DP + MP,)),
            vm((2, 4 * BLOCKS, PAIR), f32), vm((LEN, PAIR), bf16),
            vm((PAIR, LEN), bf16), vm((PAIR, LEN), f32), vm((LEN, PAIR), f32), vm((8, LEN), f32),
            vm((3 * PAIR, LEN), bf16), vm((DP, SHARE, WIDE), bf16), vm((4, 2, tokens, width), bf16),
            vm((DP, SHARE, WIDE), bf16), vm((3, SHARE, SLIM), bf16), vm((3, SHARE, WIDE), bf16),
            vm((SHARE, SLIM), bf16),
            vm((DP, SHARE, WIDE), bf16), vm((DP, SHARE, WIDE), bf16),
            vm((DP, SHARE, SLIM), bf16), vm((DP, SHARE, SLIM), bf16),
            vm((WIDE, WIDE), f32), vm((WIDE, WIDE), f32), vm((WIDE, WIDE), f32), vm((DP * SHARE, WIDE), f32),
            vm((SLIM, SLIM), f32), vm((SLIM, SLIM), f32), vm((SLIM, SLIM), f32), vm((DP * SHARE, SLIM), f32),
            vm((8, WIDE), f32),
            vm((LEAD, width), bf16), vm((LEAD, width), bf16),
            vm((2, LEAD, width), bf16), vm((2, LEAD, width), bf16), vm((LEAD, width), bf16),
            vm((4, rest, width), bf16), vm((cut, width), bf16), vm((rest - cut, width), bf16),
            vm((rest, width), bf16), vm((rest, width), bf16),
            vm((DP, 2, width), f32), vm((MP, 2, width), f32),
        ]
        + lands,
        name="back",
        compiler_params=pltpu.CompilerParams(
            collective_id=collective_id, has_side_effects=True, vmem_limit_bytes=60 * MEGA
        ),
    )(
        lens, q, k, v, heads_out, lse, grad_parts, normed, w_qkv, cos, sin, frequency_row(),
        *kept, *momenta, stream, gain_two,
    )

STEP = 10
muon_rate = 1.0
out_rate = 4.0
adam_rate = 0.8
beta_first = 0.9
beta_second = 0.95
adam_epsilon = 1e-08


def final_kernel(
    values_grad, m_qkv, m_out, m_gate, m_up, m_down, o_q, o_k, o_v, o_out, o_gate, o_up, o_down,
    summed, gain_grad, stream, grad_residual, gains, moment1, moment2,
    qkv_weight, out_weight, gate_up_weight, down_weight,
    input_grad, values_out, qkv_new, qkv_moment, out_new, out_moment, gate_up_new, gate_up_moment,
    down_new, down_moment, moment1_new, moment2_new, gains_new,
):
    units = down_weight.shape[0]
    tall = muon_rate * (stream.shape[1] / SLIM) ** 0.5
    broad = muon_rate * (stream.shape[1] / units) ** 0.5
    for k, orth in enumerate((o_q, o_k, o_v)):
        qkv_moment[:, k, :] = m_qkv[:, k * SLIM : (k + 1) * SLIM]
        qkv_new[:, k, :] = qkv_weight[:, k, :] - tall * orth[...].astype(f32)
    out_moment[...] = m_out[...].T
    out_new[...] = out_weight[...] - out_rate * o_out[...].astype(f32).T
    for k, (moment, orth) in enumerate(((m_gate, o_gate), (m_up, o_up))):
        gate_up_moment[:, k, :] = moment[:, :units]
        gate_up_new[:, k, :] = gate_up_weight[:, k, :] - broad * orth[:, :units].astype(f32)
    down_moment[...] = m_down[...].T[:units, :]
    down_new[...] = down_weight[...] - muon_rate * o_down[...].astype(f32).T[:units, :]
    values_out[...] = values_grad[...]
    x = stream[...].astype(f32)
    inverse = lax.rsqrt(row_mean(x * x) + norm_epsilon)
    unit = x * inverse
    scaled = summed[...] * gains[0:1, :]
    input_grad[...] = grad_residual[...] + inverse * (scaled - unit * row_mean(scaled * unit))
    grad = gain_grad[...]
    first = beta_first * moment1[...] + (1.0 - beta_first) * grad
    second = beta_second * moment2[...] + (1.0 - beta_second) * grad * grad
    moment1_new[...] = first
    moment2_new[...] = second
    corrected1 = first / (1.0 - beta_first**STEP)
    corrected2 = second / (1.0 - beta_second**STEP)
    gains_new[...] = gains[...] - adam_rate * corrected1 / (jnp.sqrt(corrected2) + adam_epsilon)


def final_block(values_grad, *rest):
    args = (values_grad,) + rest
    stream, residual, gains = rest[14], rest[15], rest[16]
    weights = rest[19:]
    like = lambda x: jax.ShapeDtypeStruct(x.shape, f32)
    return pl.pallas_call(
        final_kernel,
        out_shape=[like(residual), like(values_grad)]
        + [like(w) for weight in weights for w in (weight, weight)]
        + [like(gains)] * 3,
        in_specs=[VMEM] * len(args),
        out_specs=[VMEM] * 13,
        name="final",
        compiler_params=pltpu.CompilerParams(vmem_limit_bytes=56 * MEGA),
    )(*args)
def widen(x):
    return jnp.pad(x, ((0, 0), (0, WIDE - x.shape[1])))


def on_device(
    block_input, first_values, out_cotangent, doc_lengths, norm_gains, gain_moment1, gain_moment2,
    qkv_weight, qkv_momentum, out_weight, out_momentum, gate_up_weight, gate_up_momentum,
    down_weight, down_momentum,
):
    tokens, width = block_input.shape
    low_gate_up = gate_up_weight.astype(bf16)
    shares = (
        widen(low_gate_up[:, 0]),
        widen(low_gate_up[:, 1]),
        widen(down_weight.astype(bf16).T),
        out_weight.astype(bf16).T,
    )
    *wholes, normed, w_qkv, q, k, v, heads_out, lse, heads = front(
        doc_lengths, block_input, norm_gains, shares,
        qkv_weight.astype(bf16).reshape(SHARE, 3 * PAIR), first_values, 0,
    )
    w_gate, w_up, w_down, w_out = (w.reshape(GROUPS, width, w.shape[-1]) for w in wholes)
    block_output, grad_residual, grad_heads, gain_two, *kept = token_block(
        heads, block_input, out_cotangent, norm_gains, w_gate, w_up, w_down, w_out, 1
    )
    done = back_block(
        doc_lengths, q, k, v, heads_out, lse, grad_heads, normed, w_qkv.reshape(width, 3 * PAIR),
        [g.reshape(4, 2, 4, 2, SHARE, g.shape[-1]) for g in kept],
        (qkv_momentum, out_momentum, gate_up_momentum, down_momentum),
        block_input, gain_two, 2,
    )
    return (block_output,) + tuple(
        final_block(
            *done, block_input, grad_residual, norm_gains, gain_moment1, gain_moment2,
            qkv_weight, out_weight, gate_up_weight, down_weight,
        )
    )


def solution(mesh):
    placed = (
        P(("dp", "mp"), None), P("dp", "mp"), P(("dp", "mp"), None), P("dp", None),
        P(), P(), P(),
        P("dp", None, "mp"), P("dp", None, "mp"), P("mp", "dp"), P("mp", "dp"),
        P("dp", None, "mp"), P("dp", None, "mp"), P("mp", "dp"), P("mp", "dp"),
    )
    return jax.shard_map(
        on_device,
        mesh=mesh,
        in_specs=placed,
        out_specs=(P(("dp", "mp"), None), P(("dp", "mp"), None), P("dp", "mp")) + placed[7:] + (P(),) * 3,
        check_vma=False,
    )
```

```python
import functools

import jax
import jax.numpy as jnp
import numpy as np
from jax import lax
from jax.experimental import pallas as pl
from jax.experimental.pallas import tpu as pltpu
from jax.sharding import PartitionSpec as P

MEGA = 2**20
f32, bf16 = jnp.float32, jnp.bfloat16
VMEM = pl.BlockSpec(memory_space=pltpu.VMEM)
SMEM = pl.BlockSpec(memory_space=pltpu.SMEM)

HD = 64
LEN = 2048
PAIR = 2 * HD
BLOCK = 256
BLOCKS = LEN // BLOCK
LOG2E = 1.4426950408889634
SCORE_SCALE = HD**-0.5 * LOG2E
mask_fill = -1e30


def dot(a, b):
    return lax.dot_general(a, b, (((1,), (0,)), ((), ())), preferred_element_type=f32)


def dot_t(a, b):
    return lax.dot_general(a, b, (((1,), (1,)), ((), ())), preferred_element_type=f32)


def frequency():
    half = HD // 2
    return np.tile(np.exp(-np.log(10000.0) * np.arange(half) * 2.0 / HD), PAIR // half)


def angle_tables():
    angles = np.arange(BLOCK)[:, None] * frequency()[None, :]
    return np.cos(angles).astype(np.float32), np.sin(angles).astype(np.float32)


def frequency_row():
    return frequency()[None, :].astype(np.float32)


def doc_starts(lens):
    one = lens[0, 0]
    two = one + lens[0, 1]
    return one, two, two + lens[0, 2]


def pick_start(place, starts):
    zero = jnp.zeros_like(place)
    picked = jnp.where(place >= starts[0], starts[0], zero)
    picked = jnp.where(place >= starts[1], starts[1], picked)
    return jnp.where(place >= starts[2], starts[2], picked)


def turn_tables(starts, freq, turns):
    row = lax.broadcasted_iota(jnp.int32, (4 * BLOCKS, PAIR), 0)
    doc = row % 4
    start = jnp.where(doc == 1, starts[0], 0)
    start = jnp.where(doc == 2, starts[1], start)
    start = jnp.where(doc == 3, starts[2], start)
    angle = (row // 4 * BLOCK - start).astype(f32) * freq
    turns[0] = jnp.cos(angle)
    turns[1] = jnp.sin(angle)


def block_angles(block, starts, turns, cos_ref, sin_ref):
    place = block * BLOCK + lax.broadcasted_iota(jnp.int32, (BLOCK, PAIR), 0)

    def pick(table):
        picked = turns[table, pl.ds(4 * block, 1), :]
        for doc, start in enumerate(starts):
            picked = jnp.where(place >= start, turns[table, pl.ds(4 * block + doc + 1, 1), :], picked)
        return picked

    cos_b, sin_b = pick(0), pick(1)
    return cos_ref[...] * cos_b - sin_ref[...] * sin_b, sin_ref[...] * cos_b + cos_ref[...] * sin_b


def swap_halves(x):
    lane = lax.broadcasted_iota(jnp.int32, x.shape, 1)
    front = lane % HD < HD // 2
    return front, jnp.where(front, pltpu.roll(x, PAIR - HD // 2, 1), pltpu.roll(x, HD // 2, 1))


def rotate(x, cos, sin):
    front, other = swap_halves(x)
    return x * cos + jnp.where(front, -other, other) * sin


def rotate_back(x, cos, sin):
    front, other = swap_halves(x)
    return x * cos + jnp.where(front, other, -other) * sin


def head_only(x, head):
    lane = lax.broadcasted_iota(jnp.int32, x.shape, 1)
    return jnp.where(lane // HD == head, x, jnp.zeros_like(x))


def project_block(block, tokens, w_qkv, first_values, starts, turns, cos_ref, sin_ref, q_ref, k_ref, v_ref, vt):
    rows = slice(block * BLOCK, (block + 1) * BLOCK)
    proj = dot(tokens, w_qkv)
    cos, sin = block_angles(block, starts, turns, cos_ref, sin_ref)
    q_ref[rows, :] = rotate(proj[:, :PAIR], cos, sin).astype(bf16)
    k_ref[rows, :] = rotate(proj[:, PAIR : 2 * PAIR], cos, sin).astype(bf16)
    mix = 0.5 * proj[:, 2 * PAIR :] + 0.5 * first_values[rows, :].astype(f32)
    v_ref[rows, :] = mix.astype(bf16)
    vt[:PAIR, rows] = mix.T.astype(bf16)


def attend_block(block, starts, q_ref, k_ref, vt, out_ref, lse_ref):
    rows = slice(block * BLOCK, (block + 1) * BLOCK)
    span = (block + 1) * BLOCK
    row_at = rows.start + lax.broadcasted_iota(jnp.int32, (1, BLOCK), 1)
    start_row = pick_start(row_at, starts)
    key_at = lax.broadcasted_iota(jnp.int32, (span, BLOCK), 0)
    allowed = (key_at >= start_row) & (key_at <= row_at)
    outs = []
    for head in range(2):
        scores = dot_t(k_ref[:span, :], head_only(q_ref[rows, :], head))
        scores = jnp.where(allowed, scores, mask_fill)
        top = jnp.max(scores, axis=0, keepdims=True) * SCORE_SCALE
        weights = jnp.exp2(scores * SCORE_SCALE - top).astype(bf16)
        values = jnp.concatenate([vt[head * HD : (head + 1) * HD, :span], vt[PAIR:, :span]], axis=0)
        mixed = dot(values, weights)
        total = mixed[HD : HD + 1, :]
        outs.append(mixed[:HD, :] / total)
        lse_ref[head : head + 1, rows] = top + jnp.log2(total)
    out_ref[rows, :] = jnp.concatenate(outs, axis=0).T.astype(bf16)


def attend_back(
    starts, q_ref, k_ref, v_ref, heads_ref, grad_ref, lse_ref, normed, cos_ref, sin_ref, turns,
    values_grad_ref, w_grad_ref, dproj_ref, kt, dqt, delta, dproj_t,
):
    for block in range(BLOCKS):
        rows = slice(block * BLOCK, (block + 1) * BLOCK)
        kt[:, rows] = k_ref[rows, :].astype(f32).T.astype(bf16)
        both = (grad_ref[rows, :].astype(f32) * heads_ref[rows, :].astype(f32)).T
        for head in range(2):
            delta[head : head + 1, rows] = jnp.sum(
                both[head * HD : (head + 1) * HD, :], axis=0, keepdims=True
            )
    dqt[...] = jnp.zeros_like(dqt)
    yield
    chunk = 2 * BLOCK
    for block in range(BLOCKS):
        keys = slice(block * BLOCK, (block + 1) * BLOCK)
        dk = jnp.zeros((BLOCK, PAIR), f32)
        dv = jnp.zeros((BLOCK, PAIR), f32)
        at = block * BLOCK
        while at < LEN:
            width = chunk if at % chunk == 0 else BLOCK
            rows = slice(at, at + width)
            at += width
            row_at = rows.start + lax.broadcasted_iota(jnp.int32, (1, width), 1)
            start_row = pick_start(row_at, starts)
            key_at = keys.start + lax.broadcasted_iota(jnp.int32, (BLOCK, width), 0)
            allowed = key_at >= start_row
            if rows.start == keys.start:
                allowed = allowed & (key_at <= row_at)
            for head in range(2):
                q_h = head_only(q_ref[rows, :], head)
                g_h = head_only(grad_ref[rows, :], head)
                scores = dot_t(k_ref[keys, :], q_h)
                prob = jnp.exp2(scores * SCORE_SCALE - lse_ref[head : head + 1, rows])
                prob = jnp.where(allowed, prob, 0.0)
                grad_prob = dot_t(v_ref[keys, :], g_h)
                grad_scores = (prob * (grad_prob - delta[head : head + 1, rows])).astype(bf16)
                dv = dv + dot(prob.astype(bf16), g_h)
                dk = dk + dot(grad_scores, q_h)
                lanes = slice(head * HD, (head + 1) * HD)
                dqt[lanes, rows] += dot(kt[lanes, keys], grad_scores)
        half_dv = 0.5 * dv
        values_grad_ref[keys, :] = half_dv
        cos, sin = block_angles(block, starts, turns, cos_ref, sin_ref)
        dq = rotate_back(dqt[:, keys].T * HD**-0.5, cos, sin)
        dk = rotate_back(dk * HD**-0.5, cos, sin)
        dproj = jnp.concatenate([dq, dk, half_dv], axis=1)
        dproj_t[:, keys] = dproj.T.astype(bf16)
        dproj_ref[block] = dproj.astype(bf16)
        yield
    for part in range(4):
        cols = slice(part * BLOCK, (part + 1) * BLOCK)
        tokens = normed[:, :, :, cols].reshape(LEN, BLOCK)
        made = dot(dproj_t[...], tokens).T.astype(bf16)
        w_grad_ref[part * 4 : (part + 1) * 4] = made.reshape(4, BLOCK // 4, 3 * PAIR)


MESH = pl.DeviceIdType.MESH
ANY = pl.BlockSpec(memory_space=pl.ANY)
DMA = pltpu.SemaphoreType.DMA


def place():
    dp, mp = lax.axis_index("dp"), lax.axis_index("mp")
    return {"x": (dp // 2) % 2 * 2 + mp % 2, "y": dp // 4, "z": mp // 2, "core": dp % 2}


def device_at(at):
    return ((at["y"] * 2 + at["x"] // 2) * 2 + at["core"], at["z"] * 2 + at["x"] % 2)


def moved(at, axis, step):
    new = dict(at)
    if axis == "core":
        new[axis] = 1 - at[axis]
    elif axis == "pair":
        new["x"] = at["x"] + 1 - 2 * (at["x"] % 2)
    else:
        new[axis] = (at[axis] + step + 4) % 4
    return new


def greet(devices):
    barrier = pltpu.get_barrier_semaphore()
    for device in devices:
        pl.semaphore_signal(barrier, inc=1, device_id=device, device_id_type=MESH)
    pl.semaphore_wait(barrier, len(devices))


class Mover:
    def __init__(self, send_sems, recv_sems, local_sems=None):
        self.send_sems, self.recv_sems, self.local_sems = send_sems, recv_sems, local_sems
        self.used, self.locals, self.started = 0, 0, []

    def remote(self, src, dst, device, slot):
        return pltpu.make_async_remote_copy(
            src_ref=src,
            dst_ref=dst,
            send_sem=self.send_sems.at[slot],
            recv_sem=self.recv_sems.at[slot],
            device_id=device,
            device_id_type=MESH,
        )

    def send(self, src, dst, device):
        slot = self.used
        self.used += 1
        copy = self.remote(src, dst, device, slot)
        copy.start()
        self.started.append(copy)
        return slot

    def arrived(self, slot, region):
        self.remote(region, region, self.anyone, slot).wait_recv()

    def local(self, src, dst):
        copy = pltpu.make_async_copy(src, dst, self.local_sems.at[self.locals])
        self.locals += 1
        copy.start()
        return copy

    def finish(self):
        for copy in self.started:
            copy.wait_send()


def weave(*tasks):
    tasks = list(tasks)
    while tasks:
        for task in list(tasks):
            try:
                next(task)
            except StopIteration:
                tasks.remove(task)


def blocks_of(ref, at, whole, half=None, core=True):
    index = (
        slice(None) if "z" in whole else at["z"],
        slice(None) if "x" in whole else at["x"] % 2,
        slice(None) if "y" in whole else at["y"],
        slice(None) if "x" in whole else at["x"] // 2,
    )
    if core:
        index = index + (at["core"],)
    if half is not None:
        rows = ref.shape[-2] // 2
        index = index + (pl.ds(half * rows, rows),)
    return ref.at[index]


GATHER_ORDERS = (("z", "x", "y"), ("y", "z", "x"), ("y", "x", "z"))
ROW_ORDER = ("z", "x", "y")
ORDERS = (("x", "z", "y"), ("z", "x", "y"), ("y", "z", "x"), ("y", "x", "z"))
ORDERS = (("x", "y", "z"), ("y", "z", "x"), ("z", "x", "y"), ("y", "x", "z"))
RING = ("x", "y", "z")


def ring_ends(me):
    return [moved(me, axis, step) for axis in RING for step in (1, -1)] + [moved(me, "core", 1)]


def gather_part(mover, me, part, whole, order):
    sibling = moved(me, "core", 1)
    twin = device_at(sibling)
    mirrors = []
    one, two, three = order

    def pass_on(region, target):
        return mover.send(region, region, device_at(target))

    def four(at, half=None):
        return blocks_of(whole, at, (one,), half)

    def mirror(at):
        mine = four(at)
        slot = mover.send(mine, mine, twin)
        mirrors.append((slot, four(moved(at, "core", 1))))

    def ends(at, axis):
        return moved(at, axis, 1), moved(at, axis, -1), moved(at, axis, 2)

    def spread(at):
        plus, minus, _ = ends(me, three)
        slots = pass_on(four(at), plus), pass_on(four(at), minus)
        mirror(at)
        return at, slots

    def relay(sent):
        at, slots = sent
        plus, minus, across = ends(at, three)
        mover.arrived(slots[0], four(minus))
        up = pass_on(four(minus, 0), moved(me, three, 1))
        mover.arrived(slots[1], four(plus))
        down = pass_on(four(plus, 1), moved(me, three, -1))
        mirror(minus)
        mirror(plus)
        return across, (up, down)

    own = blocks_of(whole, me, ())
    mover.local(part, own).wait()
    plus, minus, across = ends(me, one)
    up, down = pass_on(own, plus), pass_on(own, minus)
    yield
    mover.arrived(up, blocks_of(whole, minus, ()))
    up = pass_on(blocks_of(whole, minus, (), 0), plus)
    mover.arrived(down, blocks_of(whole, plus, ()))
    down = pass_on(blocks_of(whole, plus, (), 1), minus)
    yield
    mover.arrived(up, blocks_of(whole, across, (), 0))
    mover.arrived(down, blocks_of(whole, across, (), 1))
    plus, minus, across = ends(me, two)
    up, down = pass_on(four(me), plus), pass_on(four(me), minus)
    sets = [spread(me)]
    yield
    mover.arrived(up, four(minus))
    up = pass_on(four(minus, 0), plus)
    mover.arrived(down, four(plus))
    down = pass_on(four(plus, 1), minus)
    sets += [spread(minus), spread(plus)]
    yield
    mover.arrived(up, four(across, 0))
    mover.arrived(down, four(across, 1))
    sets.append(spread(across))
    yield
    lasts = [relay(sets[0])]
    yield
    lasts += [relay(sets[1]), relay(sets[2])]
    yield
    lasts.append(relay(sets[3]))
    yield
    for at, slots in lasts:
        mover.arrived(slots[0], four(at, 0))
        mover.arrived(slots[1], four(at, 1))
        mirror(at)
    yield
    for slot, region in mirrors:
        mover.arrived(slot, region)


def gather_plain(mover, me, part, whole, order):
    twin = device_at(moved(me, "core", 1))
    mirrors = []

    def pass_on(region, target):
        return mover.send(region, region, device_at(target))

    def mirror(at, done):
        mine = blocks_of(whole, at, done)
        slot = mover.send(mine, mine, twin)
        mirrors.append((slot, blocks_of(whole, moved(at, "core", 1), done)))

    mover.local(part, blocks_of(whole, me, ())).wait()
    for phase, axis in enumerate(order):
        done = order[:phase]
        plus, minus, across = moved(me, axis, 1), moved(me, axis, -1), moved(me, axis, 2)
        mine = blocks_of(whole, me, done)
        up, down = pass_on(mine, plus), pass_on(mine, minus)
        if phase == 2:
            mirror(me, done)
        yield
        mover.arrived(up, blocks_of(whole, minus, done))
        up = pass_on(blocks_of(whole, minus, done, 0), plus)
        mover.arrived(down, blocks_of(whole, plus, done))
        down = pass_on(blocks_of(whole, plus, done, 1), minus)
        if phase == 2:
            mirror(minus, done)
            mirror(plus, done)
        yield
        mover.arrived(up, blocks_of(whole, across, done, 0))
        mover.arrived(down, blocks_of(whole, across, done, 1))
        if phase == 2:
            mirror(across, done)
    yield
    for slot, region in mirrors:
        mover.arrived(slot, region)


LEAD = 176


def gather_tokens_part(mover, me, whole):
    mate, plus, minus, across = (
        moved(me, "pair", 1),
        moved(me, "z", 1),
        moved(me, "z", -1),
        moved(me, "z", 2),
    )
    rows = whole.shape[-2]
    rest = rows - LEAD
    cut = (rest // 2 + 15) // 16 * 16
    lead, tail = pl.ds(0, LEAD), pl.ds(LEAD, rest)
    tails = (pl.ds(LEAD, cut), pl.ds(LEAD + cut, rest - cut))

    def at(place_, span):
        return whole.at[place_["z"], place_["x"] % 2, span]

    def both(place_, side=None):
        return whole.at[place_["z"], slice(None) if side is None else side, lead]

    def pass_on(region, target):
        return mover.send(region, region, device_at(target))

    pair = pass_on(at(me, lead), mate)
    ring = pass_on(at(me, tail), plus), pass_on(at(me, tail), minus)
    crossed = [(pass_on(at(me, tail), mate), at(moved(me, "pair", 1), tail))]
    yield
    mover.arrived(pair, at(mate, lead))
    wide = pass_on(both(me), plus), pass_on(both(me), minus)
    yield
    mover.arrived(ring[0], at(minus, tail))
    relay = [pass_on(at(minus, tails[0]), plus)]
    crossed.append((pass_on(at(minus, tail), mate), at(moved(minus, "pair", 1), tail)))
    mover.arrived(ring[1], at(plus, tail))
    relay.append(pass_on(at(plus, tails[1]), minus))
    crossed.append((pass_on(at(plus, tail), mate), at(moved(plus, "pair", 1), tail)))
    yield
    mover.arrived(relay[0], at(across, tails[0]))
    mover.arrived(relay[1], at(across, tails[1]))
    crossed.append((pass_on(at(across, tail), mate), at(moved(across, "pair", 1), tail)))
    yield
    mover.arrived(wide[0], both(minus))
    last = [pass_on(both(minus, 0), plus)]
    mover.arrived(wide[1], both(plus))
    last.append(pass_on(both(plus, 1), minus))
    yield
    for slot, region in crossed:
        mover.arrived(slot, region)
    mover.arrived(last[0], both(across, 0))
    mover.arrived(last[1], both(across, 1))


def load(ref):
    return ref[...].astype(f32)


def each_block(ref, body):
    lead = ref.shape[:-2]
    total = 1
    for size in lead:
        total *= size

    def step(flat, carry):
        index = []
        for size in reversed(lead):
            index.append(flat % size)
            flat = flat // size
        body(tuple(reversed(index)))
        return carry

    if total == 1:
        body((0,) * len(lead))
    else:
        lax.fori_loop(0, total, step, 0)


def add_into(target, *terms):
    def body(index):
        total = target[index].astype(f32)
        for term in terms:
            total = total + term[index].astype(f32)
        target[index] = total.astype(target.dtype)

    each_block(target, body)


def half_of(ref, half):
    rows = ref.shape[-2] // 2
    return ref.at[(slice(None),) * (len(ref.shape) - 2) + (pl.ds(half * rows, rows),)]


def scatter_part(mover, me, kept, lands, out, order, early=False):
    for phase, axis in enumerate(order):
        rest = order[phase + 1 :]
        plus, minus, across = moved(me, axis, 1), moved(me, axis, -1), moved(me, axis, 2)
        hop_up, hop_down, from_minus, from_plus = lands[phase]
        landed = early and phase == 0

        def part(at, half=None):
            return blocks_of(kept, at, rest, half, core=False)

        if not landed:
            up = mover.send(part(across, 0), hop_up, device_at(plus))
            down = mover.send(part(across, 1), hop_down, device_at(minus))
            plain_up = mover.send(part(plus, 1), half_of(from_minus, 1), device_at(plus))
            plain_down = mover.send(part(minus, 0), half_of(from_plus, 0), device_at(minus))
            yield
            mover.arrived(up, hop_up)
        add_into(part(plus, 0), hop_up)
        up = mover.send(part(plus, 0), half_of(from_minus, 0), device_at(plus))
        if not landed:
            mover.arrived(down, hop_down)
        add_into(part(minus, 1), hop_down)
        down = mover.send(part(minus, 1), half_of(from_plus, 1), device_at(minus))
        yield
        if not landed:
            mover.arrived(plain_up, half_of(from_minus, 1))
            mover.arrived(plain_down, half_of(from_plus, 0))
        mover.arrived(up, half_of(from_minus, 0))
        mover.arrived(down, half_of(from_plus, 1))
        if phase < 2:
            add_into(part(me), from_minus, from_plus)
        else:
            out[...] = load(part(me)) + load(from_minus) + load(from_plus)


def lead_shape(whole):
    shape = ()
    for axis, size in (("z", 4), ("x", 2), ("y", 4), ("x", 2)):
        if axis in whole:
            shape = shape + (size,)
    return shape

norm_epsilon = 1e-06
GROUPS = 8
DP, MP = 16, 8
SHARE = 64
WIDE, SLIM = 384, 128


def row_mean(x):
    return jnp.mean(x, axis=-1, keepdims=True)


def token_kernel(
    heads, stream, cotangent, gains, w_gate, w_up, w_down, w_out,
    block_output, grad_residual, grad_heads, gain_part, k_gate, k_up, k_down, k_out, *rest,
):
    lands = [rest[4 * k : 4 * k + 4] for k in range(3)]
    (
        residual, normed, normed_t, cot_t, ffn, grad_normed,
        made, twin, made_out, twin_out, send_sems, recv_sems, out_sems,
        gate_send, gate_recv, up_send, up_recv, down_send, down_recv,
    ) = rest[12:]
    group = pl.program_id(0)
    gain = gains[1:2, :]
    me = place()
    ends = [device_at(end) for end in ring_ends(me)]

    sibling = device_at(moved(me, "core", 1))

    def pass_half(m):
        return [
            pltpu.make_async_remote_copy(
                src_ref=made.at[m % 2, k, :, :, 1 - me["core"]],
                dst_ref=twin.at[m, k],
                send_sem=send_sems.at[m, k],
                recv_sem=recv_sems.at[m, k],
                device_id=sibling,
                device_id_type=MESH,
            )
            for k in range(3)
        ]

    def pass_out():
        return pltpu.make_async_remote_copy(
            src_ref=made_out.at[:, :, 1 - me["core"]],
            dst_ref=twin_out,
            send_sem=out_sems.at[0],
            recv_sem=out_sems.at[1],
            device_id=sibling,
            device_id_type=MESH,
        )

    ahead = {axis: (device_at(moved(me, axis, 1)), device_at(moved(me, axis, -1))) for axis in RING}

    def hop(src, dst, sems, slot, device):
        return pltpu.make_async_remote_copy(
            src_ref=src, dst_ref=dst, send_sem=sems[0].at[slot], recv_sem=sems[1].at[slot],
            device_id=device, device_id_type=MESH,
        )

    def first_sends(piece, land, sems, index, where, axis):
        up, down, from_minus, from_plus = land
        plus, minus = ahead[axis]
        return {
            "far": (
                hop(half_of(piece, 0), up.at[where], sems, (0,) + index, plus),
                hop(half_of(piece, 1), down.at[where], sems, (1,) + index, minus),
            ),
            "plus": (hop(half_of(piece, 1), half_of(from_minus.at[where], 1), sems, (2,) + index, plus),),
            "minus": (hop(half_of(piece, 0), half_of(from_plus.at[where], 0), sems, (3,) + index, minus),),
        }

    def go(copies, delta):
        for name, value in (("plus", 1), ("far", 2), ("minus", 3)):

            @pl.when(delta == value)
            def start():
                for copy in copies[name]:
                    copy.start()

    gate_sems, up_sems, down_sems = (gate_send, gate_recv), (up_send, up_recv), (down_send, down_recv)

    def start_round(m):
        z, side = m // 2, m % 2
        for x_half in range(2):
            delta = (2 * x_half + side - me["x"] + 4) % 4
            piece = twin.at[m, 0, :, x_half]
            go(first_sends(piece, lands[0], gate_sems, (z,), (z,), "x"), delta)
        for step, name in ((2, "far"), (1, "plus"), (3, "minus")):
            piece = twin.at[m, 1, (me["y"] + step) % 4]
            for copy in first_sends(piece, lands[1], up_sems, (m,), (z, side), "y")[name]:
                copy.start()
        go(
            first_sends(twin.at[m, 2], lands[2], down_sems, (side,), (side,), "z"),
            (z - me["z"] + 4) % 4,
        )

    def end_round():
        for land, sems, count, where in (
            (lands[0], gate_sems, 4, lambda i: (i,)),
            (lands[1], up_sems, 8, lambda i: (i // 2, i % 2)),
            (lands[2], down_sems, 2, lambda i: (i,)),
        ):
            for i in range(count):
                regions = (
                    land[0].at[where(i)], land[1].at[where(i)],
                    half_of(land[2].at[where(i)], 1), half_of(land[3].at[where(i)], 0),
                )
                for kind, region in enumerate(regions):
                    copy = hop(region, region, sems, (kind, i), sibling)
                    copy.wait_recv()
                    copy.wait_send()

    @pl.when(group == 0)
    def first():
        greet(ends)
        branch = jnp.zeros(residual.shape, f32)
        for m in range(GROUPS):
            branch = branch + dot_t(heads[m], w_out[m]).astype(bf16).astype(f32)
        total = stream[...].astype(f32) + branch
        residual[...] = total
        unit = total * lax.rsqrt(row_mean(total * total) + norm_epsilon)
        scaled = unit * gain
        normed[...] = scaled.astype(bf16)
        normed_t[...] = scaled.T.astype(bf16)
        cot_t[...] = cotangent[...].astype(f32).T.astype(bf16)
        ffn[...] = jnp.zeros_like(ffn)
        grad_normed[...] = jnp.zeros_like(grad_normed)

    @pl.when(group < GROUPS)
    def one():
        gate = dot(normed[...], w_gate[0, :, :WIDE])
        up = dot(normed[...], w_up[0])
        sigmoid = jax.nn.sigmoid(gate)
        silu = gate * sigmoid
        hidden = (silu * up).astype(bf16)
        ffn[...] += dot_t(hidden, w_down[0]).astype(bf16).astype(f32)
        grad_hidden = dot(cotangent[...], w_down[0])
        slope = sigmoid * (1.0 + gate * (1.0 - sigmoid))
        grad_gate = (grad_hidden * up * slope).astype(bf16)
        grad_up = (grad_hidden * silu).astype(bf16)
        grad_normed[...] += dot_t(grad_gate, w_gate[0, :, :WIDE]) + dot_t(grad_up, w_up[0])
        half = group % 2
        shape = made.shape[2:]
        made[half, 0] = dot(normed_t[...], grad_gate).astype(bf16).reshape(shape)
        made[half, 1] = dot(normed_t[...], grad_up).astype(bf16).reshape(shape)
        made[half, 2] = dot(cot_t[...], hidden).astype(bf16).reshape(shape)
        for copy in pass_half(group):
            copy.start()

    @pl.when(group == GROUPS - 1)
    def last():
        total = residual[...]
        block_output[...] = (total + ffn[...]).astype(bf16)
        inverse = lax.rsqrt(row_mean(total * total) + norm_epsilon)
        unit = total * inverse
        grad = grad_normed[...]
        gain_part[...] = jnp.sum(grad * unit, axis=0, keepdims=True)
        scaled = grad * gain
        result = cotangent[...].astype(f32) + inverse * (scaled - unit * row_mean(scaled * unit))
        grad_residual[...] = result
        low = result.astype(bf16)
        low_t = result.T.astype(bf16)
        for m in range(GROUPS):
            made_out[m] = dot(low_t, heads[m]).astype(bf16).reshape(made_out.shape[1:])
        pass_out().start()
        for m in range(GROUPS):
            grad_heads[m] = dot(low, w_out[m]).astype(bf16)

    @pl.when(group > 0)
    def join():
        before = group - 1
        for k, (copy, kept) in enumerate(zip(pass_half(before), (k_gate, k_up, k_down))):
            copy.wait_recv()
            own = made[before % 2, k, :, :, me["core"]].astype(f32)
            both = (own + twin[before, k].astype(f32)).astype(bf16)
            twin[before, k] = both
            kept[0] = both.reshape(kept.shape[1:])
        start_round(before)
        for copy in pass_half(before):
            copy.wait_send()

    @pl.when(group == GROUPS)
    def join_out():
        copy = pass_out()
        copy.wait_recv()
        for m in range(GROUPS):
            own = made_out[m, :, me["core"]].astype(f32)
            k_out[m] = (own + twin_out[m].astype(f32)).astype(bf16)
        copy.wait_send()
        end_round()


def token_block(heads, stream, cotangent, gains, w_gate, w_up, w_down, collective_id):
    tokens, width = stream.shape
    hidden, slim = WIDE, SLIM
    pairs = width // SHARE // 2
    whole = lambda shape: pl.BlockSpec(shape, lambda m: (0,) * len(shape))
    each = lambda cols: pl.BlockSpec((1, width, cols), lambda m: (jnp.minimum(m, GROUPS - 1), 0, 0))
    w_out = pl.BlockSpec((GROUPS, width, SLIM), lambda m: (0, 0, WIDE // SLIM))
    kept = pl.BlockSpec((1, pairs, SHARE, hidden), lambda m: (jnp.maximum(m - 1, 0), 0, 0, 0))
    flat = (tokens, width)
    vm = pltpu.VMEM
    return pl.pallas_call(
        token_kernel,
        grid=(GROUPS + 1,),
        in_specs=[whole(heads.shape), whole(flat), whole(flat), whole(gains.shape)]
        + [each(WIDE + SLIM), each(WIDE), each(WIDE), w_out],
        out_specs=[whole(flat), whole(flat), whole(heads.shape), whole((1, width))]
        + [kept] * 3
        + [whole((GROUPS, pairs, SHARE, slim))]
        + [ANY] * 12,
        out_shape=[
            jax.ShapeDtypeStruct(flat, bf16),
            jax.ShapeDtypeStruct(flat, f32),
            jax.ShapeDtypeStruct(heads.shape, bf16),
            jax.ShapeDtypeStruct((1, width), f32),
        ]
        + [jax.ShapeDtypeStruct((GROUPS, pairs, SHARE, hidden), bf16)] * 3
        + [jax.ShapeDtypeStruct((GROUPS, pairs, SHARE, slim), bf16)]
        + [
            jax.ShapeDtypeStruct(lead_shape(order[1:]) + (rows, hidden), bf16)
            for order in ORDERS[:3]
            for rows in (SHARE // 2, SHARE // 2, SHARE, SHARE)
        ],
        scratch_shapes=[
            vm(flat, f32), vm(flat, bf16), vm((width, tokens), bf16), vm((width, tokens), bf16),
            vm(flat, f32), vm(flat, f32),
            vm((2, 3, 4, 2, 2, SHARE, hidden), bf16), vm((GROUPS, 3, 4, 2, SHARE, hidden), bf16),
            vm((GROUPS, pairs, 2, SHARE, slim), bf16), vm((GROUPS, pairs, SHARE, slim), bf16),
            DMA((GROUPS, 3)), DMA((GROUPS, 3)), DMA((2,)),
            DMA((4, 4)), DMA((4, 4)), DMA((4, 8)), DMA((4, 8)), DMA((4, 2)), DMA((4, 2)),
        ],
        name="token_block",
        compiler_params=pltpu.CompilerParams(
            collective_id=collective_id, has_side_effects=True, vmem_limit_bytes=58 * MEGA
        ),
    )(heads, stream, cotangent, gains, w_gate, w_up, w_down, w_gate)


def gather_row_part(mover, me, whole):
    plus, minus, across = moved(me, "y", 1), moved(me, "y", -1), moved(me, "y", 2)
    far, sibling = moved(me, "x", 2), moved(me, "core", 1)

    def one(at, half=None):
        region = whole.at[at["y"], at["x"] // 2, at["core"]]
        return region if half is None else region.at[pl.ds(half * (SHARE // 2), SHARE // 2)]

    def column(at):
        return whole.at[:, at["x"] // 2, at["core"]]

    def pass_on(region, target):
        return mover.send(region, region, device_at(target))

    ring = pass_on(one(me), plus), pass_on(one(me), minus)
    yield
    mover.arrived(ring[0], one(minus))
    relay = [pass_on(one(minus, 0), plus)]
    mover.arrived(ring[1], one(plus))
    relay.append(pass_on(one(plus, 1), minus))
    yield
    mover.arrived(relay[0], one(across, 0))
    mover.arrived(relay[1], one(across, 1))
    half = pass_on(column(me), far)
    mirrors = [(pass_on(column(me), sibling), column(sibling))]
    yield
    mover.arrived(half, column(far))
    mirrors.append((pass_on(column(far), sibling), column(moved(far, "core", 1))))
    yield
    for slot, region in mirrors:
        mover.arrived(slot, region)


def front_kernel(
    lens, stream, gains, gate_up_weight, down_weight, out_weight, qkv_weight, first_values,
    cos_ref, sin_ref, freq,
    w_gate, w_up, w_down, w_rows, normed, q_ref, k_ref, v_ref, out_ref, lse_ref, heads,
    send_sems, recv_sems, local_sems, head_send, head_recv, vt, turns, w_qkv, s_gate, s_up, s_down, s_qkv,
):
    me = place()
    dp, mp = lax.axis_index("dp"), lax.axis_index("mp")
    mover = Mover(send_sems, recv_sems, local_sems)
    mover.anyone = device_at(moved(me, "core", 1))
    cols_to = [(dp, (mp + k) % MP) for k in range(1, MP)]
    others = [moved(me, axis, step) for axis in ("x", "y") for step in (1, -1)]
    others += [moved(me, "core", 1), moved(me, "x", 2)]
    units = down_weight.shape[1]
    for share, weight in (
        (s_gate, gate_up_weight[:, 0, :]), (s_up, gate_up_weight[:, 1, :]), (s_down, down_weight[...])
    ):
        share[...] = jnp.zeros_like(share)
        share[:, :units] = weight.astype(bf16)
    s_gate[:, WIDE:] = out_weight[...].astype(bf16)
    for k in range(3):
        s_qkv[:, k * PAIR : (k + 1) * PAIR] = qkv_weight[k].astype(bf16)
    w_qkv[me["y"], me["x"] // 2, me["core"]] = s_qkv[...]
    x = stream[...].astype(f32)
    unit = x * lax.rsqrt(row_mean(x * x) + norm_epsilon)
    normed[me["z"], me["x"] % 2] = (unit * gains[0:1, :]).astype(bf16)
    greet(cols_to + [device_at(end) for end in others])

    tokens = gather_tokens_part(mover, me, normed)
    row = gather_row_part(mover, me, w_qkv)
    gate = gather_part(mover, me, s_gate, w_gate, GATHER_ORDERS[0])
    up = gather_plain(mover, me, s_up, w_up, GATHER_ORDERS[1])
    down = gather_plain(mover, me, s_down, w_down, GATHER_ORDERS[2])
    every = gather_plain(mover, me, s_qkv, w_rows, ROW_ORDER)
    starts = doc_starts(lens)

    def step(*tasks):
        for task in tasks:
            next(task, None)

    step(gate, row, tokens, up, down, every)
    turn_tables(starts, freq[...], turns)
    vt[PAIR:, :] = jnp.ones((16, LEN), bf16)
    lse_ref[...] = jnp.zeros_like(lse_ref)
    step(gate, row, up, down, every)
    step(gate, row)
    step(tokens)
    step(gate, row)
    step(tokens, up, down, every)
    step(gate)
    step(tokens)
    step(gate, up, down)
    step(tokens, row, every)
    step(tokens, up, down)
    weights = w_qkv[...].reshape(DP * SHARE, 3 * PAIR)
    for block in range(BLOCKS):
        project_block(
            block, normed[block // 2, block % 2], weights, first_values, starts, turns,
            cos_ref, sin_ref, q_ref, k_ref, v_ref, vt,
        )
        if block == 3:
            step(gate, every)
    for block in range(BLOCKS):
        attend_block(block, starts, q_ref, k_ref, vt, out_ref, lse_ref)
        if block == 4:
            step(gate)
    copies = []
    for k in (5, 3, 4, 2, 6, 7, 1):
        taker = (mp + k) % MP
        copy = pltpu.make_async_remote_copy(
            src_ref=out_ref.at[pl.ds(pl.multiple_of(taker * BLOCK, BLOCK), BLOCK)],
            dst_ref=heads.at[mp],
            send_sem=head_send.at[k],
            recv_sem=head_recv.at[k],
            device_id=(dp, taker),
            device_id_type=MESH,
        )
        copy.start()
        copies.append(copy)
    heads[mp] = out_ref[pl.ds(pl.multiple_of(mp * BLOCK, BLOCK), BLOCK), :]
    step(up, down, gate, every)
    for k in range(1, MP):
        giver = (mp + MP - k) % MP
        pltpu.make_async_remote_copy(
            src_ref=heads.at[giver],
            dst_ref=heads.at[giver],
            send_sem=head_send.at[k],
            recv_sem=head_recv.at[k],
            device_id=(dp, giver),
            device_id_type=MESH,
        ).wait_recv()
    step(up, down)
    step(gate, up, down, every)
    step(every)
    for copy in copies:
        copy.wait_send()
    mover.finish()


def front(lens, stream, gains, weights, first_values, collective_id):
    gate_up, down, out, qkv = weights
    cos, sin = angle_tables()
    flat = jax.ShapeDtypeStruct((LEN, PAIR), bf16)
    vm = pltpu.VMEM
    widths = (WIDE + SLIM, WIDE, WIDE)
    slots = 40 + 3 * 16 + 13 + 8
    return pl.pallas_call(
        front_kernel,
        out_shape=[jax.ShapeDtypeStruct((4, 2, 4, 2, 2, SHARE, w), bf16) for w in widths + (3 * PAIR,)]
        + [
            jax.ShapeDtypeStruct((4, 2) + stream.shape, bf16),
            flat, flat, flat, flat,
            jax.ShapeDtypeStruct((8, LEN), f32),
            jax.ShapeDtypeStruct((MP, BLOCK, PAIR), bf16),
        ],
        in_specs=[SMEM] + [VMEM] * 10,
        out_specs=[ANY] * 4 + [VMEM] * 7,
        scratch_shapes=[
            DMA((slots,)), DMA((slots,)), DMA((4,)), DMA((MP,)), DMA((MP,)),
            vm((PAIR + 16, LEN), bf16), vm((2, 4 * BLOCKS, PAIR), f32),
        ]
        + [vm((4, 2, 2, SHARE, 3 * PAIR), bf16)]
        + [vm((SHARE, w), bf16) for w in widths + (3 * PAIR,)],
        name="front",
        compiler_params=pltpu.CompilerParams(
            collective_id=collective_id, has_side_effects=True, vmem_limit_bytes=56 * MEGA
        ),
    )(lens, stream, gains, gate_up, down, out, qkv, first_values, cos, sin, frequency_row())

newton_a = 3.4445
newton_b = -4.775
newton_c = 2.0315
OWNERS = (12, 2, 6, 10, 0, 4, 8)
COLUMNS = (SLIM, SLIM, SLIM, SLIM, WIDE, WIDE, WIDE)
ASPECTS = (8.0, 8.0, 8.0, 1.0, 1024 / 352, 1024 / 352, 1.0)


def halves(x):
    high = x.astype(bf16)
    return high, (x - high.astype(f32)).astype(bf16)


def left_side(x):
    high, low = halves(x)
    return jnp.concatenate([high, high, low], axis=1)


def right_side(x):
    high, low = halves(x)
    return jnp.concatenate([high, low, high], axis=0)


def newton_steps(stacked, result, gram, poly, total, moving, norm, left, right, wide_left):
    size = stacked.shape[-1]
    rows = DP * SHARE

    def held():
        return stacked[...].reshape(rows, size)

    def polynomial():
        one = gram[...]
        rank = lax.broadcasted_iota(jnp.int32, (size, size), 0)
        file = lax.broadcasted_iota(jnp.int32, (size, size), 1)
        left[0] = left_side(one)
        right[0] = right_side(one)
        poly[...] = (
            jnp.where(rank == file, newton_a, 0.0) + newton_b * one + newton_c * dot(left[0], right[0])
        )
        right[1] = right_side(poly[...])

    def advance():
        half = dot(left[0], right[1])
        gram[...] = dot(left_side(half), right[1])

    def gather():
        total[...] = dot(left_side(total[...]), right[1])

    def begin():
        block = held()
        wide = block.astype(f32)
        length = jnp.sqrt(jnp.sum(wide * wide)) + 1e-07
        inverse = jnp.full((1, size), 1.0, f32) / length
        norm[0:1, :size] = inverse
        turned = wide.T.astype(bf16)
        gram[...] = dot(turned, block) * (inverse * inverse)

    def first():
        polynomial()
        total[...] = poly[...]

    def middle():
        high, low = halves(total[...])
        block = held()
        moving[...] = (dot(block, high) + dot(block, low)) * norm[0:1, :size]

    def regram():
        now = moving[...]
        high, low = halves(now)
        wide_left[...] = jnp.concatenate([high, high, low], axis=1)
        turned = now.T
        turned_high, turned_low = halves(turned)
        gram[...] = dot(turned_high, high) + (dot(turned_high, low) + dot(turned_low, high))

    def end():
        ending = dot(wide_left[...], right_side(total[...]))
        result[...] = ending.astype(bf16).reshape(DP, SHARE, size)

    return [
        begin, first, advance, polynomial, gather, middle, regram,
        first, advance, polynomial, gather, advance, polynomial, gather, end,
    ]


def newton_scratch(size):
    square = pltpu.VMEM((size, size), f32)
    return [
        square, square, square, pltpu.VMEM((DP * SHARE, size), f32), pltpu.VMEM((8, size), f32),
        pltpu.VMEM((1, size, 3 * size), bf16), pltpu.VMEM((2, 3 * size, size), bf16),
        pltpu.VMEM((DP * SHARE, 3 * size), bf16),
    ]


def link(src, dst, send, recv, device):
    return pltpu.make_async_remote_copy(
        src_ref=src, dst_ref=dst, send_sem=send, recv_sem=recv, device_id=device, device_id_type=MESH
    )


def back_kernel(
    lens, q_ref, k_ref, v_ref, heads_ref, lse_ref, grad_parts, normed, cos_ref, sin_ref, freq,
    k_gate, k_up, k_down, k_out, all_rows, *rest,
):
    landed, rest = [rest[4 * k : 4 * k + 4] for k in range(3)], rest[12:]
    (
        qkv_momentum,
    out_momentum, gate_up_momentum, down_momentum,
        stream, gain_two,
        values_grad, m_qkv, m_out, m_gate, m_up, m_down, o_q, o_k, o_v, o_out, o_gate, o_up, o_down,
        summed, gain_grad,
        send_sems, recv_sems, local_sems, head_send, head_recv, dp_send, dp_recv, own_send, own_recv,
        back_send, back_recv, all_send, all_recv, proj_send, proj_recv,
        turns, grad_heads, kt, dqt, delta, dproj_t, dproj, dproj_in, w_rows, g_qkv,
        dp_land, qkv_share, wide_share, slim_share, wide_in, wide_out, slim_in, slim_out,
        gain_dp, gain_mp, *own_lands,
    ) = rest
    newton, own_lands = own_lands[:16], own_lands[16:]
    mover = Mover(send_sems, recv_sems, local_sems)
    me = place()
    dp, mp = lax.axis_index("dp"), lax.axis_index("mp")
    mover.anyone = device_at(moved(me, "core", 1))
    rows_to = [((dp + k) % DP, mp) for k in range(1, DP)]
    cols_to = [(dp, (mp + k) % MP) for k in range(1, MP)]
    kept_from = (k_gate, k_up, k_down, k_out)
    scratch = [own_lands[13 * index : 13 * (index + 1)] for index in range(4)]
    loads = [mover.local(source, own[0]) for source, own in zip(kept_from, scratch)]
    early = []
    for sources, own in zip(landed, scratch):
        up, down, from_minus, from_plus = own[1:5]
        early.append(
            [
                mover.local(source, target)
                for source, target in (
                    (sources[0], up), (sources[1], down),
                    (half_of(sources[2], 1), half_of(from_minus, 1)),
                    (half_of(sources[3], 0), half_of(from_plus, 0)),
                )
            ]
        )
    loads.append(mover.local(all_rows, w_rows))
    greet(rows_to + cols_to + [device_at(moved(me, "x", step)) for step in (1, -1)])

    def rows_of(index):
        return pl.ds(pl.multiple_of(index * BLOCK, BLOCK), BLOCK)

    head_copies = []
    for k in (5, 3, 4, 2, 6, 7, 1):
        taker = (mp + k) % MP
        copy = link(
            grad_parts.at[taker], grad_heads.at[rows_of(mp)], head_send.at[k], head_recv.at[k], (dp, taker)
        )
        copy.start()
        head_copies.append(copy)
    grad_heads[rows_of(mp), :] = grad_parts[mp]

    sums = (m_gate, m_up, m_down, m_out)
    scatters = []
    for index in range(4):
        own = scratch[index]
        phases = [own[1 + 4 * phase : 5 + 4 * phase] for phase in range(3)]
        scatters.append(scatter_part(mover, me, own[0], phases, sums[index], ORDERS[index], index < 3))

    def step(*tasks):
        for task in tasks:
            next(task, None)

    for index in (3, 0, 1, 2):
        loads[index].wait()
        for copy in early[index] if index < 3 else ():
            copy.wait()
        step(scatters[index])
    starts = doc_starts(lens)
    turn_tables(starts, freq[...], turns)
    for k in range(1, MP):
        giver = (mp + MP - k) % MP
        region = grad_heads.at[rows_of(giver)]
        link(region, region, head_send.at[k], head_recv.at[k], (dp, giver)).wait_recv()
    attention = attend_back(
        starts, q_ref, k_ref, v_ref, heads_ref, grad_heads, lse_ref, normed, cos_ref, sin_ref,
        turns, values_grad, g_qkv, dproj, kt, dqt, delta, dproj_t,
    )

    def pass_rows(block):
        return link(
            dproj.at[block], dproj_in.at[mp], proj_send.at[block], proj_recv.at[mp], (dp, block)
        )

    step(attention)
    for block in range(BLOCKS):
        step(attention)

        @pl.when(mp != block)
        def away():
            pass_rows(block).start()

        @pl.when(mp == block)
        def here():
            dproj_in[mp] = dproj[block]

        if block in (0, 2, 4, 6, 7):
            step(*scatters)
    step(attention)
    dp_copies = []
    for k in range(1, DP):
        taker = (dp + k) % DP
        copy = link(g_qkv.at[taker], dp_land.at[dp], dp_send.at[k], dp_recv.at[k], (taker, mp))
        copy.start()
        dp_copies.append(copy)
    dp_land[dp] = g_qkv[dp]
    step(*scatters)
    step(*scatters)

    results = (o_q, o_k, o_v, o_out, o_gate, o_up, o_down)

    def give(index, share):
        owner = OWNERS[index]
        land = wide_in if COLUMNS[index] == WIDE else slim_in
        copy = link(share, land.at[dp], own_send.at[index], own_recv.at[dp], (owner, mp))

        @pl.when(dp != owner)
        def away():
            copy.start()

        @pl.when(dp == owner)
        def here():
            land[dp] = share[...]

        return owner, copy

    def settle(given):
        owner, copy = given

        @pl.when(dp != owner)
        def away():
            copy.wait_send()

    def take(index):
        land = wide_in if COLUMNS[index] == WIDE else slim_in
        for k in range(1, DP):
            giver = (dp + k) % DP
            region = land.at[giver]
            link(region, region, own_send.at[index], own_recv.at[giver], (giver, mp)).wait_recv()

    def returns(index, wait):
        made = wide_out if COLUMNS[index] == WIDE else slim_out
        for k in range(1, DP):
            taker = (dp + k) % DP
            copy = link(made.at[taker], results[index], back_send.at[taker], back_recv.at[index], (taker, mp))
            copy.wait_send() if wait else copy.start()

    def owned(columns):
        chosen = [i for i in range(len(OWNERS)) if COLUMNS[i] == columns]
        if columns == WIDE:
            steps = newton_steps(wide_in, wide_out, *newton[:8])
        else:
            steps = newton_steps(slim_in, slim_out, *newton[8:])
        mine = functools.reduce(jnp.logical_or, [dp == OWNERS[i] for i in chosen])
        for index in chosen:
            pl.when(dp == OWNERS[index])(functools.partial(take, index))
        for one in steps:
            pl.when(mine)(one)
            yield
        for index in chosen:
            pl.when(dp == OWNERS[index])(functools.partial(returns, index, False))

            @pl.when(dp == OWNERS[index])
            def keep():
                made = wide_out if COLUMNS[index] == WIDE else slim_out
                results[index][...] = made[dp]

    units = down_momentum.shape[1]
    m_out[...] += 0.5 * out_momentum[...]
    m_gate[:, :units] += 0.5 * gate_up_momentum[:, 0, :]
    m_up[:, :units] += 0.5 * gate_up_momentum[:, 1, :]
    m_down[:, :units] += 0.5 * down_momentum[...]
    slim_share[...] = m_out[...].astype(bf16)
    for k, moment in enumerate((m_gate, m_up, m_down)):
        wide_share[k] = moment[...].astype(bf16)
    given = [give(4 + k, wide_share.at[k]) for k in range(3)] + [give(3, slim_share)]

    def gains_task():
        loads[4].wait()
        for k in range(1, MP):
            giver = (mp + k) % MP
            region = dproj_in.at[giver]
            link(region, region, proj_send.at[0], proj_recv.at[giver], (dp, giver)).wait_recv()
        grad_normed = jnp.zeros(summed.shape, f32)
        for m in range(MP):
            grad_normed = grad_normed + dot_t(dproj_in[m], w_rows[m])
        summed[...] = grad_normed
        x = stream[...].astype(f32)
        unit = x * lax.rsqrt(row_mean(x * x) + norm_epsilon)
        gain_dp[dp] = jnp.concatenate(
            [jnp.sum(grad_normed * unit, axis=0, keepdims=True), gain_two[...]], axis=0
        )
        copies = []
        for k in range(1, DP):
            copy = link(
                gain_dp.at[dp], gain_dp.at[dp], all_send.at[k], all_recv.at[k], ((dp + k) % DP, mp)
            )
            copy.start()
            copies.append(copy)
        yield
        for k in range(1, DP):
            giver = (dp + DP - k) % DP
            region = gain_dp.at[giver]
            link(region, region, all_send.at[k], all_recv.at[k], (giver, mp)).wait_recv()
        total = gain_dp[0]
        for k in range(1, DP):
            total = total + gain_dp[k]
        gain_mp[mp] = total
        for k in range(1, MP):
            copy = link(
                gain_mp.at[mp], gain_mp.at[mp], all_send.at[DP + k], all_recv.at[DP + k], (dp, (mp + k) % MP)
            )
            copy.start()
            copies.append(copy)
        yield
        for k in range(1, MP):
            giver = (mp + MP - k) % MP
            region = gain_mp.at[giver]
            link(region, region, all_send.at[DP + k], all_recv.at[DP + k], (dp, giver)).wait_recv()
        total = gain_mp[0]
        for k in range(1, MP):
            total = total + gain_mp[k]
        gain_grad[...] = total
        for copy in copies:
            copy.wait_send()

    def qkv_task():
        for k in range(1, DP):
            giver = (dp + DP - k) % DP
            region = dp_land.at[giver]
            link(region, region, dp_send.at[k], dp_recv.at[k], (giver, mp)).wait_recv()
        total = jnp.zeros((SHARE, WIDE), f32)
        for k in range(DP):
            total = total + dp_land[k].astype(f32)
        for k in range(3):
            cols = slice(k * SLIM, (k + 1) * SLIM)
            moment = 0.5 * qkv_momentum[k] + total[:, cols]
            m_qkv[:, cols] = moment
            qkv_share[k] = moment.astype(bf16)
        given.extend(give(k, qkv_share.at[k]) for k in range(3))
        yield
        yield from owned(SLIM)

    gains, sums_task, wide_task = gains_task(), qkv_task(), owned(WIDE)
    step(gains)
    step(sums_task)
    for _ in range(8):
        step(wide_task)
    step(gains)
    for _ in range(8):
        step(wide_task)
    for _ in range(16):
        step(sums_task)
    step(gains)
    for index, owner in enumerate(OWNERS):

        @pl.when(dp != owner)
        def arrive():
            link(
                results[index], results[index], back_send.at[0], back_recv.at[index], (owner, mp)
            ).wait_recv()

        pl.when(dp == owner)(functools.partial(returns, index, True))
    for copy in head_copies + dp_copies:
        copy.wait_send()
    for block in range(BLOCKS):

        @pl.when(mp != block)
        def sent():
            pass_rows(block).wait_send()

    for one in given:
        settle(one)
    mover.finish()


def back_block(
    lens, q, k, v, heads_out, lse, grad_parts, normed, kept, all_rows, landed, momenta, stream, gain_two, collective_id,
):
    cos, sin = angle_tables()
    tokens, width = stream.shape
    vm = pltpu.VMEM
    slim, wide = (jax.ShapeDtypeStruct((SHARE, c), bf16) for c in (SLIM, WIDE))
    full = jax.ShapeDtypeStruct((SHARE, WIDE), f32)
    lands = []
    for index, source in enumerate(kept):
        rows, cols = source.shape[-2:]
        lands.append(vm(source.shape, bf16))
        for phase in range(3):
            lead = lead_shape(ORDERS[index][phase + 1 :])
            lands += [vm(lead + (rows // 2, cols), bf16)] * 2 + [vm(lead + (rows, cols), bf16)] * 2
    slots = 18 * len(kept)
    return pl.pallas_call(
        back_kernel,
        out_shape=[
            jax.ShapeDtypeStruct((LEN, PAIR), f32),
            full, jax.ShapeDtypeStruct((SHARE, SLIM), f32), full, full, full,
            slim, slim, slim, slim, wide, wide, wide,
            jax.ShapeDtypeStruct((tokens, width), f32),
            jax.ShapeDtypeStruct((2, width), f32),
        ],
        in_specs=[SMEM] + [VMEM] * 10 + [ANY] * 17 + [VMEM] * 6,
        out_specs=[VMEM] * 15,
        scratch_shapes=[
            DMA((slots,)), DMA((slots,)), DMA((19,)), DMA((MP,)), DMA((MP,)),
            DMA((DP,)), DMA((DP,)), DMA((7,)), DMA((DP,)), DMA((DP,)), DMA((7,)),
            DMA((DP + MP,)), DMA((DP + MP,)), DMA((MP,)), DMA((MP,)),
            vm((2, 4 * BLOCKS, PAIR), f32), vm((LEN, PAIR), bf16),
            vm((PAIR, LEN), bf16), vm((PAIR, LEN), f32), vm((8, LEN), f32),
            vm((3 * PAIR, LEN), bf16), vm((BLOCKS, BLOCK, 3 * PAIR), bf16), vm((MP, BLOCK, 3 * PAIR), bf16),
            vm((MP, width, 3 * PAIR), bf16), vm((DP, SHARE, WIDE), bf16),
            vm((DP, SHARE, WIDE), bf16), vm((3, SHARE, SLIM), bf16), vm((3, SHARE, WIDE), bf16),
            vm((SHARE, SLIM), bf16),
            vm((DP, SHARE, WIDE), bf16), vm((DP, SHARE, WIDE), bf16),
            vm((DP, SHARE, SLIM), bf16), vm((DP, SHARE, SLIM), bf16),
            vm((DP, 2, width), f32), vm((MP, 2, width), f32),
        ]
        + newton_scratch(WIDE)
        + newton_scratch(SLIM)
        + lands,
        name="back",
        compiler_params=pltpu.CompilerParams(
            collective_id=collective_id, has_side_effects=True, vmem_limit_bytes=60 * MEGA
        ),
    )(
        lens, q, k, v, heads_out, lse, grad_parts, normed, cos, sin, frequency_row(),
        *kept, all_rows, *landed, *momenta, stream, gain_two,
    )

STEP = 10
muon_rate = 1.0
out_rate = 4.0
adam_rate = 0.8
beta_first = 0.9
beta_second = 0.95
adam_epsilon = 1e-08


def final_kernel(
    values_grad, m_qkv, m_out, m_gate, m_up, m_down, o_q, o_k, o_v, o_out, o_gate, o_up, o_down,
    summed, gain_grad, stream, grad_residual, gains, moment1, moment2,
    qkv_weight, out_weight, gate_up_weight, down_weight,
    input_grad, values_out, qkv_new, qkv_moment, out_new, out_moment, gate_up_new, gate_up_moment,
    down_new, down_moment, moment1_new, moment2_new, gains_new,
):
    units = down_weight.shape[1]
    tall = muon_rate * (stream.shape[1] / SLIM) ** 0.5
    broad = muon_rate * (stream.shape[1] / units) ** 0.5
    for k, orth in enumerate((o_q, o_k, o_v)):
        qkv_moment[k] = m_qkv[:, k * SLIM : (k + 1) * SLIM]
        qkv_new[k] = qkv_weight[k] - tall * orth[...].astype(f32)
    out_moment[...] = m_out[...]
    out_new[...] = out_weight[...] - out_rate * o_out[...].astype(f32)
    for k, (moment, orth) in enumerate(((m_gate, o_gate), (m_up, o_up))):
        gate_up_moment[:, k, :] = moment[:, :units]
        gate_up_new[:, k, :] = gate_up_weight[:, k, :] - broad * orth[:, :units].astype(f32)
    down_moment[...] = m_down[:, :units]
    down_new[...] = down_weight[...] - muon_rate * o_down[:, :units].astype(f32)
    values_out[...] = values_grad[...]
    x = stream[...].astype(f32)
    inverse = lax.rsqrt(row_mean(x * x) + norm_epsilon)
    unit = x * inverse
    scaled = summed[...] * gains[0:1, :]
    input_grad[...] = grad_residual[...] + inverse * (scaled - unit * row_mean(scaled * unit))
    grad = gain_grad[...]
    first = beta_first * moment1[...] + (1.0 - beta_first) * grad
    second = beta_second * moment2[...] + (1.0 - beta_second) * grad * grad
    moment1_new[...] = first
    moment2_new[...] = second
    corrected1 = first / (1.0 - beta_first**STEP)
    corrected2 = second / (1.0 - beta_second**STEP)
    gains_new[...] = gains[...] - adam_rate * corrected1 / (jnp.sqrt(corrected2) + adam_epsilon)


def final_block(values_grad, *rest):
    args = (values_grad,) + rest
    stream, residual, gains = rest[14], rest[15], rest[16]
    weights = rest[19:]
    like = lambda x: jax.ShapeDtypeStruct(x.shape, f32)
    return pl.pallas_call(
        final_kernel,
        out_shape=[like(residual), like(values_grad)]
        + [like(w) for weight in weights for w in (weight, weight)]
        + [like(gains)] * 3,
        in_specs=[VMEM] * len(args),
        out_specs=[VMEM] * 13,
        name="final",
        compiler_params=pltpu.CompilerParams(vmem_limit_bytes=56 * MEGA),
    )(*args)
def on_device(
    block_input, first_values, out_cotangent, doc_lengths, norm_gains, gain_moment1, gain_moment2,
    qkv_weight, qkv_momentum, out_weight, out_momentum, gate_up_weight, gate_up_momentum,
    down_weight, down_momentum,
):
    tokens, width = block_input.shape
    qkv_weight, qkv_momentum = (a.transpose(1, 0, 2) for a in (qkv_weight, qkv_momentum))
    out_weight, out_momentum, down_weight, down_momentum = (
        a.T for a in (out_weight, out_momentum, down_weight, down_momentum)
    )
    *wholes, all_rows, normed, q, k, v, heads_out, lse, heads = front(
        doc_lengths, block_input, norm_gains,
        (gate_up_weight, down_weight, out_weight, qkv_weight), first_values, 0,
    )
    w_gate, w_up, w_down = (w.reshape(GROUPS, width, w.shape[-1]) for w in wholes)
    block_output, grad_residual, grad_heads, gain_two, *rest = token_block(
        heads, block_input, out_cotangent, norm_gains, w_gate, w_up, w_down, 1
    )
    kept, landed = rest[:4], rest[4:]
    done = back_block(
        doc_lengths, q, k, v, heads_out, lse, grad_heads, normed,
        [g.reshape(4, 2, 4, 2, SHARE, g.shape[-1]) for g in kept],
        all_rows.reshape(GROUPS, width, all_rows.shape[-1]),
        landed,
        (qkv_momentum, out_momentum, gate_up_momentum, down_momentum),
        block_input, gain_two, 2,
    )
    (
        input_grad, values_grad, qkv_new, qkv_moment, out_new, out_moment,
        gate_up_new, gate_up_moment, down_new, down_moment, *gains_out,
    ) = final_block(
        *done, block_input, grad_residual, norm_gains, gain_moment1, gain_moment2,
        qkv_weight, out_weight, gate_up_weight, down_weight,
    )
    return (
        block_output, input_grad, values_grad,
        qkv_new.transpose(1, 0, 2), qkv_moment.transpose(1, 0, 2), out_new.T, out_moment.T,
        gate_up_new, gate_up_moment, down_new.T, down_moment.T, *gains_out,
    )


def solution(mesh):
    placed = (
        P(("dp", "mp"), None), P("dp", "mp"), P(("dp", "mp"), None), P("dp", None),
        P(), P(), P(),
        P("dp", None, "mp"), P("dp", None, "mp"), P("mp", "dp"), P("mp", "dp"),
        P("dp", None, "mp"), P("dp", None, "mp"), P("mp", "dp"), P("mp", "dp"),
    )
    return jax.shard_map(
        on_device,
        mesh=mesh,
        in_specs=placed,
        out_specs=(P(("dp", "mp"), None), P(("dp", "mp"), None), P("dp", "mp")) + placed[7:] + (P(),) * 3,
        check_vma=False,
    )
```

```python
import functools

import jax
import jax.numpy as jnp
import numpy as np
from jax import lax
from jax.experimental import pallas as pl
from jax.experimental.pallas import tpu as pltpu
from jax.sharding import PartitionSpec as P

MEGA = 2**20
f32, bf16 = jnp.float32, jnp.bfloat16
VMEM = pl.BlockSpec(memory_space=pltpu.VMEM)
SMEM = pl.BlockSpec(memory_space=pltpu.SMEM)

HD = 64
LEN = 2048
PAIR = 2 * HD
BLOCK = 256
BLOCKS = LEN // BLOCK
LOG2E = 1.4426950408889634
SCORE_SCALE = HD**-0.5 * LOG2E
mask_fill = -1e30


def dot(a, b):
    return lax.dot_general(a, b, (((1,), (0,)), ((), ())), preferred_element_type=f32)


def dot_t(a, b):
    return lax.dot_general(a, b, (((1,), (1,)), ((), ())), preferred_element_type=f32)


def frequency():
    half = HD // 2
    return np.tile(np.exp(-np.log(10000.0) * np.arange(half) * 2.0 / HD), PAIR // half)


def angle_tables():
    angles = np.arange(BLOCK)[:, None] * frequency()[None, :]
    return np.cos(angles).astype(np.float32), np.sin(angles).astype(np.float32)


def frequency_row():
    return frequency()[None, :].astype(np.float32)


def doc_starts(lens):
    one = lens[0, 0]
    two = one + lens[0, 1]
    return one, two, two + lens[0, 2]


def pick_start(place, starts):
    zero = jnp.zeros_like(place)
    picked = jnp.where(place >= starts[0], starts[0], zero)
    picked = jnp.where(place >= starts[1], starts[1], picked)
    return jnp.where(place >= starts[2], starts[2], picked)


def turn_tables(starts, freq, turns):
    row = lax.broadcasted_iota(jnp.int32, (4 * BLOCKS, PAIR), 0)
    doc = row % 4
    start = jnp.where(doc == 1, starts[0], 0)
    start = jnp.where(doc == 2, starts[1], start)
    start = jnp.where(doc == 3, starts[2], start)
    angle = (row // 4 * BLOCK - start).astype(f32) * freq
    turns[0] = jnp.cos(angle)
    turns[1] = jnp.sin(angle)


def block_angles(block, starts, turns, cos_ref, sin_ref):
    place = block * BLOCK + lax.broadcasted_iota(jnp.int32, (BLOCK, PAIR), 0)

    def pick(table):
        picked = turns[table, pl.ds(4 * block, 1), :]
        for doc, start in enumerate(starts):
            picked = jnp.where(place >= start, turns[table, pl.ds(4 * block + doc + 1, 1), :], picked)
        return picked

    cos_b, sin_b = pick(0), pick(1)
    return cos_ref[...] * cos_b - sin_ref[...] * sin_b, sin_ref[...] * cos_b + cos_ref[...] * sin_b


def swap_halves(x):
    lane = lax.broadcasted_iota(jnp.int32, x.shape, 1)
    front = lane % HD < HD // 2
    return front, jnp.where(front, pltpu.roll(x, PAIR - HD // 2, 1), pltpu.roll(x, HD // 2, 1))


def rotate(x, cos, sin):
    front, other = swap_halves(x)
    return x * cos + jnp.where(front, -other, other) * sin


def rotate_back(x, cos, sin):
    front, other = swap_halves(x)
    return x * cos + jnp.where(front, other, -other) * sin


def head_only(x, head):
    lane = lax.broadcasted_iota(jnp.int32, x.shape, 1)
    return jnp.where(lane // HD == head, x, jnp.zeros_like(x))


def project_block(block, tokens, w_qkv, first_values, starts, turns, cos_ref, sin_ref, q_ref, k_ref, v_ref, vt):
    rows = slice(block * BLOCK, (block + 1) * BLOCK)
    proj = dot(tokens, w_qkv)
    cos, sin = block_angles(block, starts, turns, cos_ref, sin_ref)
    q_ref[rows, :] = rotate(proj[:, :PAIR], cos, sin).astype(bf16)
    k_ref[rows, :] = rotate(proj[:, PAIR : 2 * PAIR], cos, sin).astype(bf16)
    mix = 0.5 * proj[:, 2 * PAIR :] + 0.5 * first_values[rows, :].astype(f32)
    v_ref[rows, :] = mix.astype(bf16)
    vt[:PAIR, rows] = mix.T.astype(bf16)


def attend_block(block, starts, q_ref, k_ref, vt, out_ref, lse_ref):
    rows = slice(block * BLOCK, (block + 1) * BLOCK)
    span = (block + 1) * BLOCK
    row_at = rows.start + lax.broadcasted_iota(jnp.int32, (1, BLOCK), 1)
    start_row = pick_start(row_at, starts)
    key_at = lax.broadcasted_iota(jnp.int32, (span, BLOCK), 0)
    allowed = (key_at >= start_row) & (key_at <= row_at)
    outs = []
    for head in range(2):
        scores = dot_t(k_ref[:span, :], head_only(q_ref[rows, :], head))
        scores = jnp.where(allowed, scores, mask_fill)
        top = jnp.max(scores, axis=0, keepdims=True) * SCORE_SCALE
        weights = jnp.exp2(scores * SCORE_SCALE - top).astype(bf16)
        values = jnp.concatenate([vt[head * HD : (head + 1) * HD, :span], vt[PAIR:, :span]], axis=0)
        mixed = dot(values, weights)
        total = mixed[HD : HD + 1, :]
        outs.append(mixed[:HD, :] / total)
        lse_ref[head : head + 1, rows] = top + jnp.log2(total)
    out_ref[rows, :] = jnp.concatenate(outs, axis=0).T.astype(bf16)


def attend_back(
    starts, q_ref, k_ref, v_ref, heads_ref, grad_ref, lse_ref, normed, cos_ref, sin_ref, turns,
    values_grad_ref, w_grad_ref, dproj_ref, kt, dqt, delta, dproj_t,
):
    for block in range(BLOCKS):
        rows = slice(block * BLOCK, (block + 1) * BLOCK)
        kt[:, rows] = k_ref[rows, :].astype(f32).T.astype(bf16)
        both = (grad_ref[rows, :].astype(f32) * heads_ref[rows, :].astype(f32)).T
        for head in range(2):
            delta[head : head + 1, rows] = jnp.sum(
                both[head * HD : (head + 1) * HD, :], axis=0, keepdims=True
            )
    dqt[...] = jnp.zeros_like(dqt)
    yield
    chunk = 2 * BLOCK
    for block in range(BLOCKS):
        keys = slice(block * BLOCK, (block + 1) * BLOCK)
        dk = jnp.zeros((BLOCK, PAIR), f32)
        dv = jnp.zeros((BLOCK, PAIR), f32)
        at = block * BLOCK
        while at < LEN:
            width = chunk if at % chunk == 0 else BLOCK
            rows = slice(at, at + width)
            at += width
            row_at = rows.start + lax.broadcasted_iota(jnp.int32, (1, width), 1)
            start_row = pick_start(row_at, starts)
            key_at = keys.start + lax.broadcasted_iota(jnp.int32, (BLOCK, width), 0)
            allowed = key_at >= start_row
            if rows.start == keys.start:
                allowed = allowed & (key_at <= row_at)
            for head in range(2):
                q_h = head_only(q_ref[rows, :], head)
                g_h = head_only(grad_ref[rows, :], head)
                scores = dot_t(k_ref[keys, :], q_h)
                prob = jnp.exp2(scores * SCORE_SCALE - lse_ref[head : head + 1, rows])
                prob = jnp.where(allowed, prob, 0.0)
                grad_prob = dot_t(v_ref[keys, :], g_h)
                grad_scores = (prob * (grad_prob - delta[head : head + 1, rows])).astype(bf16)
                dv = dv + dot(prob.astype(bf16), g_h)
                dk = dk + dot(grad_scores, q_h)
                lanes = slice(head * HD, (head + 1) * HD)
                dqt[lanes, rows] += dot(kt[lanes, keys], grad_scores)
        half_dv = 0.5 * dv
        values_grad_ref[keys, :] = half_dv
        cos, sin = block_angles(block, starts, turns, cos_ref, sin_ref)
        dq = rotate_back(dqt[:, keys].T * HD**-0.5, cos, sin)
        dk = rotate_back(dk * HD**-0.5, cos, sin)
        dproj = jnp.concatenate([dq, dk, half_dv], axis=1)
        dproj_t[:, keys] = dproj.T.astype(bf16)
        dproj_ref[block] = dproj.astype(bf16)
        yield
    for part in range(4):
        cols = slice(part * BLOCK, (part + 1) * BLOCK)
        tokens = normed[:, :, :, cols].reshape(LEN, BLOCK)
        made = dot(dproj_t[...], tokens).T.astype(bf16)
        w_grad_ref[part * 4 : (part + 1) * 4] = made.reshape(4, BLOCK // 4, 3 * PAIR)


MESH = pl.DeviceIdType.MESH
ANY = pl.BlockSpec(memory_space=pl.ANY)
DMA = pltpu.SemaphoreType.DMA


def place():
    dp, mp = lax.axis_index("dp"), lax.axis_index("mp")
    return {"x": (dp // 2) % 2 * 2 + mp % 2, "y": dp // 4, "z": mp // 2, "core": dp % 2}


def device_at(at):
    return ((at["y"] * 2 + at["x"] // 2) * 2 + at["core"], at["z"] * 2 + at["x"] % 2)


def moved(at, axis, step):
    new = dict(at)
    if axis == "core":
        new[axis] = 1 - at[axis]
    elif axis == "pair":
        new["x"] = at["x"] + 1 - 2 * (at["x"] % 2)
    else:
        new[axis] = (at[axis] + step + 4) % 4
    return new


def greet(devices):
    barrier = pltpu.get_barrier_semaphore()
    for device in devices:
        pl.semaphore_signal(barrier, inc=1, device_id=device, device_id_type=MESH)
    pl.semaphore_wait(barrier, len(devices))


class Mover:
    def __init__(self, send_sems, recv_sems, local_sems=None):
        self.send_sems, self.recv_sems, self.local_sems = send_sems, recv_sems, local_sems
        self.used, self.locals, self.started = 0, 0, []

    def remote(self, src, dst, device, slot):
        return pltpu.make_async_remote_copy(
            src_ref=src,
            dst_ref=dst,
            send_sem=self.send_sems.at[slot],
            recv_sem=self.recv_sems.at[slot],
            device_id=device,
            device_id_type=MESH,
        )

    def send(self, src, dst, device):
        slot = self.used
        self.used += 1
        copy = self.remote(src, dst, device, slot)
        copy.start()
        self.started.append(copy)
        return slot

    def arrived(self, slot, region):
        self.remote(region, region, self.anyone, slot).wait_recv()

    def local(self, src, dst):
        copy = pltpu.make_async_copy(src, dst, self.local_sems.at[self.locals])
        self.locals += 1
        copy.start()
        return copy

    def finish(self):
        for copy in self.started:
            copy.wait_send()


def weave(*tasks):
    tasks = list(tasks)
    while tasks:
        for task in list(tasks):
            try:
                next(task)
            except StopIteration:
                tasks.remove(task)


def blocks_of(ref, at, whole, half=None, core=True):
    index = (
        slice(None) if "z" in whole else at["z"],
        slice(None) if "x" in whole else at["x"] % 2,
        slice(None) if "y" in whole else at["y"],
        slice(None) if "x" in whole else at["x"] // 2,
    )
    if core:
        index = index + (at["core"],)
    if half is not None:
        rows = ref.shape[-2] // 2
        index = index + (pl.ds(half * rows, rows),)
    return ref.at[index]


GATHER_ORDERS = (("z", "x", "y"), ("y", "z", "x"), ("y", "x", "z"))
ROW_ORDER = ("z", "x", "y")
ORDERS = (("x", "z", "y"), ("z", "x", "y"), ("y", "z", "x"), ("y", "x", "z"))
ORDERS = (("x", "y", "z"), ("y", "z", "x"), ("z", "x", "y"), ("y", "x", "z"))
RING = ("x", "y", "z")


def ring_ends(me):
    return [moved(me, axis, step) for axis in RING for step in (1, -1)] + [moved(me, "core", 1)]


def gather_part(mover, me, part, whole, order):
    sibling = moved(me, "core", 1)
    twin = device_at(sibling)
    mirrors = []
    one, two, three = order

    def pass_on(region, target):
        return mover.send(region, region, device_at(target))

    def four(at, half=None):
        return blocks_of(whole, at, (one,), half)

    def mirror(at):
        mine = four(at)
        slot = mover.send(mine, mine, twin)
        mirrors.append((slot, four(moved(at, "core", 1))))

    def ends(at, axis):
        return moved(at, axis, 1), moved(at, axis, -1), moved(at, axis, 2)

    def spread(at):
        plus, minus, _ = ends(me, three)
        slots = pass_on(four(at), plus), pass_on(four(at), minus)
        mirror(at)
        return at, slots

    def relay(sent):
        at, slots = sent
        plus, minus, across = ends(at, three)
        mover.arrived(slots[0], four(minus))
        up = pass_on(four(minus, 0), moved(me, three, 1))
        mover.arrived(slots[1], four(plus))
        down = pass_on(four(plus, 1), moved(me, three, -1))
        mirror(minus)
        mirror(plus)
        return across, (up, down)

    own = blocks_of(whole, me, ())
    mover.local(part, own).wait()
    plus, minus, across = ends(me, one)
    up, down = pass_on(own, plus), pass_on(own, minus)
    yield
    mover.arrived(up, blocks_of(whole, minus, ()))
    up = pass_on(blocks_of(whole, minus, (), 0), plus)
    mover.arrived(down, blocks_of(whole, plus, ()))
    down = pass_on(blocks_of(whole, plus, (), 1), minus)
    yield
    mover.arrived(up, blocks_of(whole, across, (), 0))
    mover.arrived(down, blocks_of(whole, across, (), 1))
    plus, minus, across = ends(me, two)
    up, down = pass_on(four(me), plus), pass_on(four(me), minus)
    sets = [spread(me)]
    yield
    mover.arrived(up, four(minus))
    up = pass_on(four(minus, 0), plus)
    mover.arrived(down, four(plus))
    down = pass_on(four(plus, 1), minus)
    sets += [spread(minus), spread(plus)]
    yield
    mover.arrived(up, four(across, 0))
    mover.arrived(down, four(across, 1))
    sets.append(spread(across))
    yield
    lasts = [relay(sets[0])]
    yield
    lasts += [relay(sets[1]), relay(sets[2])]
    yield
    lasts.append(relay(sets[3]))
    yield
    for at, slots in lasts:
        mover.arrived(slots[0], four(at, 0))
        mover.arrived(slots[1], four(at, 1))
        mirror(at)
    yield
    for slot, region in mirrors:
        mover.arrived(slot, region)


def gather_plain(mover, me, part, whole, order):
    twin = device_at(moved(me, "core", 1))
    mirrors = []

    def pass_on(region, target):
        return mover.send(region, region, device_at(target))

    def mirror(at, done):
        mine = blocks_of(whole, at, done)
        slot = mover.send(mine, mine, twin)
        mirrors.append((slot, blocks_of(whole, moved(at, "core", 1), done)))

    mover.local(part, blocks_of(whole, me, ())).wait()
    for phase, axis in enumerate(order):
        done = order[:phase]
        plus, minus, across = moved(me, axis, 1), moved(me, axis, -1), moved(me, axis, 2)
        mine = blocks_of(whole, me, done)
        up, down = pass_on(mine, plus), pass_on(mine, minus)
        if phase == 2:
            mirror(me, done)
        yield
        mover.arrived(up, blocks_of(whole, minus, done))
        up = pass_on(blocks_of(whole, minus, done, 0), plus)
        mover.arrived(down, blocks_of(whole, plus, done))
        down = pass_on(blocks_of(whole, plus, done, 1), minus)
        if phase == 2:
            mirror(minus, done)
            mirror(plus, done)
        yield
        mover.arrived(up, blocks_of(whole, across, done, 0))
        mover.arrived(down, blocks_of(whole, across, done, 1))
        if phase == 2:
            mirror(across, done)
    yield
    for slot, region in mirrors:
        mover.arrived(slot, region)


LEAD = 176


def gather_tokens_part(mover, me, whole):
    mate, plus, minus, across = (
        moved(me, "pair", 1),
        moved(me, "z", 1),
        moved(me, "z", -1),
        moved(me, "z", 2),
    )
    rows = whole.shape[-2]
    rest = rows - LEAD
    cut = (rest // 2 + 15) // 16 * 16
    lead, tail = pl.ds(0, LEAD), pl.ds(LEAD, rest)
    tails = (pl.ds(LEAD, cut), pl.ds(LEAD + cut, rest - cut))

    def at(place_, span):
        return whole.at[place_["z"], place_["x"] % 2, span]

    def both(place_, side=None):
        return whole.at[place_["z"], slice(None) if side is None else side, lead]

    def pass_on(region, target):
        return mover.send(region, region, device_at(target))

    pair = pass_on(at(me, lead), mate)
    ring = pass_on(at(me, tail), plus), pass_on(at(me, tail), minus)
    crossed = [(pass_on(at(me, tail), mate), at(moved(me, "pair", 1), tail))]
    yield
    mover.arrived(pair, at(mate, lead))
    wide = pass_on(both(me), plus), pass_on(both(me), minus)
    yield
    mover.arrived(ring[0], at(minus, tail))
    relay = [pass_on(at(minus, tails[0]), plus)]
    crossed.append((pass_on(at(minus, tail), mate), at(moved(minus, "pair", 1), tail)))
    mover.arrived(ring[1], at(plus, tail))
    relay.append(pass_on(at(plus, tails[1]), minus))
    crossed.append((pass_on(at(plus, tail), mate), at(moved(plus, "pair", 1), tail)))
    yield
    mover.arrived(relay[0], at(across, tails[0]))
    mover.arrived(relay[1], at(across, tails[1]))
    crossed.append((pass_on(at(across, tail), mate), at(moved(across, "pair", 1), tail)))
    yield
    mover.arrived(wide[0], both(minus))
    last = [pass_on(both(minus, 0), plus)]
    mover.arrived(wide[1], both(plus))
    last.append(pass_on(both(plus, 1), minus))
    yield
    for slot, region in crossed:
        mover.arrived(slot, region)
    mover.arrived(last[0], both(across, 0))
    mover.arrived(last[1], both(across, 1))


def load(ref):
    return ref[...].astype(f32)


def each_block(ref, body):
    lead = ref.shape[:-2]
    total = 1
    for size in lead:
        total *= size

    def step(flat, carry):
        index = []
        for size in reversed(lead):
            index.append(flat % size)
            flat = flat // size
        body(tuple(reversed(index)))
        return carry

    if total == 1:
        body((0,) * len(lead))
    else:
        lax.fori_loop(0, total, step, 0)


def add_into(target, *terms):
    def body(index):
        total = target[index].astype(f32)
        for term in terms:
            total = total + term[index].astype(f32)
        target[index] = total.astype(target.dtype)

    each_block(target, body)


def half_of(ref, half):
    rows = ref.shape[-2] // 2
    return ref.at[(slice(None),) * (len(ref.shape) - 2) + (pl.ds(half * rows, rows),)]


def scatter_part(mover, me, kept, lands, out, order, early=False):
    for phase, axis in enumerate(order):
        rest = order[phase + 1 :]
        plus, minus, across = moved(me, axis, 1), moved(me, axis, -1), moved(me, axis, 2)
        hop_up, hop_down, from_minus, from_plus = lands[phase]
        landed = early and phase == 0

        def part(at, half=None):
            return blocks_of(kept, at, rest, half, core=False)

        if not landed:
            up = mover.send(part(across, 0), hop_up, device_at(plus))
            down = mover.send(part(across, 1), hop_down, device_at(minus))
            plain_up = mover.send(part(plus, 1), half_of(from_minus, 1), device_at(plus))
            plain_down = mover.send(part(minus, 0), half_of(from_plus, 0), device_at(minus))
            yield
            mover.arrived(up, hop_up)
        add_into(part(plus, 0), hop_up)
        up = mover.send(part(plus, 0), half_of(from_minus, 0), device_at(plus))
        if not landed:
            mover.arrived(down, hop_down)
        add_into(part(minus, 1), hop_down)
        down = mover.send(part(minus, 1), half_of(from_plus, 1), device_at(minus))
        yield
        if not landed:
            mover.arrived(plain_up, half_of(from_minus, 1))
            mover.arrived(plain_down, half_of(from_plus, 0))
        mover.arrived(up, half_of(from_minus, 0))
        mover.arrived(down, half_of(from_plus, 1))
        if phase < 2:
            add_into(part(me), from_minus, from_plus)
        else:
            out[...] = load(part(me)) + load(from_minus) + load(from_plus)


def lead_shape(whole):
    shape = ()
    for axis, size in (("z", 4), ("x", 2), ("y", 4), ("x", 2)):
        if axis in whole:
            shape = shape + (size,)
    return shape

norm_epsilon = 1e-06
GROUPS = 8
DP, MP = 16, 8
SHARE = 64
WIDE, SLIM = 384, 128


def group_at(step):
    return step % 4 * 2 + step // 4


def row_mean(x):
    return jnp.mean(x, axis=-1, keepdims=True)


def token_kernel(
    heads, stream, cotangent, gains, w_gate, w_up, w_down, w_out,
    block_output, grad_residual, grad_heads, gain_part, k_gate, k_up, k_down, k_out, *rest,
):
    lands = [rest[4 * k : 4 * k + 4] for k in range(3)]
    (
        residual, normed, normed_t, cot_t, ffn, grad_normed,
        made, twin, made_out, twin_out, send_sems, recv_sems, out_sems,
        gate_send, gate_recv, up_send, up_recv, down_send, down_recv,
    ) = rest[12:]
    group = pl.program_id(0)
    gain = gains[1:2, :]
    me = place()
    ends = [device_at(end) for end in ring_ends(me)]

    sibling = device_at(moved(me, "core", 1))

    def pass_half(m):
        return [
            pltpu.make_async_remote_copy(
                src_ref=made.at[m % 2, k, :, :, 1 - me["core"]],
                dst_ref=twin.at[m, k],
                send_sem=send_sems.at[m, k],
                recv_sem=recv_sems.at[m, k],
                device_id=sibling,
                device_id_type=MESH,
            )
            for k in range(3)
        ]

    def pass_out():
        return pltpu.make_async_remote_copy(
            src_ref=made_out.at[:, :, 1 - me["core"]],
            dst_ref=twin_out,
            send_sem=out_sems.at[0],
            recv_sem=out_sems.at[1],
            device_id=sibling,
            device_id_type=MESH,
        )

    ahead = {axis: (device_at(moved(me, axis, 1)), device_at(moved(me, axis, -1))) for axis in RING}

    def hop(src, dst, sems, slot, device):
        return pltpu.make_async_remote_copy(
            src_ref=src, dst_ref=dst, send_sem=sems[0].at[slot], recv_sem=sems[1].at[slot],
            device_id=device, device_id_type=MESH,
        )

    def first_sends(piece, land, sems, index, where, axis):
        up, down, from_minus, from_plus = land
        plus, minus = ahead[axis]
        return {
            "far": (
                hop(half_of(piece, 0), up.at[where], sems, (0,) + index, plus),
                hop(half_of(piece, 1), down.at[where], sems, (1,) + index, minus),
            ),
            "plus": (hop(half_of(piece, 1), half_of(from_minus.at[where], 1), sems, (2,) + index, plus),),
            "minus": (hop(half_of(piece, 0), half_of(from_plus.at[where], 0), sems, (3,) + index, minus),),
        }

    def go(copies, delta):
        for name, value in (("plus", 1), ("far", 2), ("minus", 3)):

            @pl.when(delta == value)
            def start():
                for copy in copies[name]:
                    copy.start()

    gate_sems, up_sems, down_sems = (gate_send, gate_recv), (up_send, up_recv), (down_send, down_recv)

    def start_round(slot):
        m = group_at(slot)
        z, side = m // 2, m % 2
        for x_half in range(2):
            delta = (2 * x_half + side - me["x"] + 4) % 4
            piece = twin.at[slot, 0, :, x_half]
            go(first_sends(piece, lands[0], gate_sems, (z,), (z,), "x"), delta)
        for step, name in ((2, "far"), (1, "plus"), (3, "minus")):
            piece = twin.at[slot, 1, (me["y"] + step) % 4]
            for copy in first_sends(piece, lands[1], up_sems, (m,), (z, side), "y")[name]:
                copy.start()
        go(
            first_sends(twin.at[slot, 2], lands[2], down_sems, (side,), (side,), "z"),
            (z - me["z"] + 4) % 4,
        )

    def end_round():
        for land, sems, count, where in (
            (lands[0], gate_sems, 4, lambda i: (i,)),
            (lands[1], up_sems, 8, lambda i: (i // 2, i % 2)),
            (lands[2], down_sems, 2, lambda i: (i,)),
        ):
            for i in range(count):
                regions = (
                    land[0].at[where(i)], land[1].at[where(i)],
                    half_of(land[2].at[where(i)], 1), half_of(land[3].at[where(i)], 0),
                )
                for kind, region in enumerate(regions):
                    copy = hop(region, region, sems, (kind, i), sibling)
                    copy.wait_recv()
                    copy.wait_send()

    @pl.when(group == 0)
    def first():
        greet(ends)
        branch = jnp.zeros(residual.shape, f32)
        for m in range(GROUPS):
            branch = branch + dot_t(heads[m], w_out[m]).astype(bf16).astype(f32)
        total = stream[...].astype(f32) + branch
        residual[...] = total
        unit = total * lax.rsqrt(row_mean(total * total) + norm_epsilon)
        scaled = unit * gain
        normed[...] = scaled.astype(bf16)
        normed_t[...] = scaled.T.astype(bf16)
        cot_t[...] = cotangent[...].astype(f32).T.astype(bf16)
        ffn[...] = jnp.zeros_like(ffn)
        grad_normed[...] = jnp.zeros_like(grad_normed)

    @pl.when(group < GROUPS)
    def one():
        gate = dot(normed[...], w_gate[0, :, :WIDE])
        up = dot(normed[...], w_up[0])
        sigmoid = jax.nn.sigmoid(gate)
        silu = gate * sigmoid
        hidden = (silu * up).astype(bf16)
        ffn[...] += dot_t(hidden, w_down[0]).astype(bf16).astype(f32)
        grad_hidden = dot(cotangent[...], w_down[0])
        slope = sigmoid * (1.0 + gate * (1.0 - sigmoid))
        grad_gate = (grad_hidden * up * slope).astype(bf16)
        grad_up = (grad_hidden * silu).astype(bf16)
        grad_normed[...] += dot_t(grad_gate, w_gate[0, :, :WIDE]) + dot_t(grad_up, w_up[0])
        half = group % 2
        shape = made.shape[2:]
        made[half, 0] = dot(normed_t[...], grad_gate).astype(bf16).reshape(shape)
        made[half, 1] = dot(normed_t[...], grad_up).astype(bf16).reshape(shape)
        made[half, 2] = dot(cot_t[...], hidden).astype(bf16).reshape(shape)
        for copy in pass_half(group):
            copy.start()

    @pl.when(group == GROUPS - 1)
    def last():
        total = residual[...]
        block_output[...] = (total + ffn[...]).astype(bf16)
        inverse = lax.rsqrt(row_mean(total * total) + norm_epsilon)
        unit = total * inverse
        grad = grad_normed[...]
        gain_part[...] = jnp.sum(grad * unit, axis=0, keepdims=True)
        scaled = grad * gain
        result = cotangent[...].astype(f32) + inverse * (scaled - unit * row_mean(scaled * unit))
        grad_residual[...] = result
        low = result.astype(bf16)
        low_t = result.T.astype(bf16)
        for m in range(GROUPS):
            made_out[m] = dot(low_t, heads[m]).astype(bf16).reshape(made_out.shape[1:])
        pass_out().start()
        for m in range(GROUPS):
            grad_heads[m] = dot(low, w_out[m]).astype(bf16)

    @pl.when(group > 0)
    def join():
        before = group - 1
        for k, (copy, kept) in enumerate(zip(pass_half(before), (k_gate, k_up, k_down))):
            copy.wait_recv()
            own = made[before % 2, k, :, :, me["core"]].astype(f32)
            both = (own + twin[before, k].astype(f32)).astype(bf16)
            twin[before, k] = both
            kept[0] = both.reshape(kept.shape[1:])
        start_round(before)
        for copy in pass_half(before):
            copy.wait_send()

    @pl.when(group == GROUPS)
    def join_out():
        copy = pass_out()
        copy.wait_recv()
        for m in range(GROUPS):
            own = made_out[m, :, me["core"]].astype(f32)
            k_out[m] = (own + twin_out[m].astype(f32)).astype(bf16)
        copy.wait_send()
        end_round()


def token_block(heads, stream, cotangent, gains, w_gate, w_up, w_down, collective_id):
    tokens, width = stream.shape
    hidden, slim = WIDE, SLIM
    pairs = width // SHARE // 2
    whole = lambda shape: pl.BlockSpec(shape, lambda m: (0,) * len(shape))
    each = lambda cols: pl.BlockSpec((1, width, cols), lambda m: (group_at(jnp.minimum(m, GROUPS - 1)), 0, 0))
    w_out = pl.BlockSpec((GROUPS, width, SLIM), lambda m: (0, 0, WIDE // SLIM))
    kept = pl.BlockSpec((1, pairs, SHARE, hidden), lambda m: (group_at(jnp.maximum(m - 1, 0)), 0, 0, 0))
    flat = (tokens, width)
    vm = pltpu.VMEM
    return pl.pallas_call(
        token_kernel,
        grid=(GROUPS + 1,),
        in_specs=[whole(heads.shape), whole(flat), whole(flat), whole(gains.shape)]
        + [each(WIDE + SLIM), each(WIDE), each(WIDE), w_out],
        out_specs=[whole(flat), whole(flat), whole(heads.shape), whole((1, width))]
        + [kept] * 3
        + [whole((GROUPS, pairs, SHARE, slim))]
        + [ANY] * 12,
        out_shape=[
            jax.ShapeDtypeStruct(flat, bf16),
            jax.ShapeDtypeStruct(flat, f32),
            jax.ShapeDtypeStruct(heads.shape, bf16),
            jax.ShapeDtypeStruct((1, width), f32),
        ]
        + [jax.ShapeDtypeStruct((GROUPS, pairs, SHARE, hidden), bf16)] * 3
        + [jax.ShapeDtypeStruct((GROUPS, pairs, SHARE, slim), bf16)]
        + [
            jax.ShapeDtypeStruct(lead_shape(order[1:]) + (rows, hidden), bf16)
            for order in ORDERS[:3]
            for rows in (SHARE // 2, SHARE // 2, SHARE, SHARE)
        ],
        scratch_shapes=[
            vm(flat, f32), vm(flat, bf16), vm((width, tokens), bf16), vm((width, tokens), bf16),
            vm(flat, f32), vm(flat, f32),
            vm((2, 3, 4, 2, 2, SHARE, hidden), bf16), vm((GROUPS, 3, 4, 2, SHARE, hidden), bf16),
            vm((GROUPS, pairs, 2, SHARE, slim), bf16), vm((GROUPS, pairs, SHARE, slim), bf16),
            DMA((GROUPS, 3)), DMA((GROUPS, 3)), DMA((2,)),
            DMA((4, 4)), DMA((4, 4)), DMA((4, 8)), DMA((4, 8)), DMA((4, 2)), DMA((4, 2)),
        ],
        name="token_block",
        compiler_params=pltpu.CompilerParams(
            collective_id=collective_id, has_side_effects=True, vmem_limit_bytes=58 * MEGA
        ),
    )(heads, stream, cotangent, gains, w_gate, w_up, w_down, w_gate)


def gather_row_part(mover, me, whole):
    plus, minus, across = moved(me, "y", 1), moved(me, "y", -1), moved(me, "y", 2)
    far, sibling = moved(me, "x", 2), moved(me, "core", 1)

    def one(at, half=None):
        region = whole.at[at["y"], at["x"] // 2, at["core"]]
        return region if half is None else region.at[pl.ds(half * (SHARE // 2), SHARE // 2)]

    def column(at):
        return whole.at[:, at["x"] // 2, at["core"]]

    def pass_on(region, target):
        return mover.send(region, region, device_at(target))

    ring = pass_on(one(me), plus), pass_on(one(me), minus)
    yield
    mover.arrived(ring[0], one(minus))
    relay = [pass_on(one(minus, 0), plus)]
    mover.arrived(ring[1], one(plus))
    relay.append(pass_on(one(plus, 1), minus))
    yield
    mover.arrived(relay[0], one(across, 0))
    mover.arrived(relay[1], one(across, 1))
    half = pass_on(column(me), far)
    mirrors = [(pass_on(column(me), sibling), column(sibling))]
    yield
    mover.arrived(half, column(far))
    mirrors.append((pass_on(column(far), sibling), column(moved(far, "core", 1))))
    yield
    for slot, region in mirrors:
        mover.arrived(slot, region)


def front_kernel(
    lens, stream, gains, gate_up_weight, down_weight, out_weight, qkv_weight, first_values,
    cos_ref, sin_ref, freq,
    w_gate, w_up, w_down, w_rows, normed, q_ref, k_ref, v_ref, out_ref, lse_ref, heads,
    send_sems, recv_sems, local_sems, head_send, head_recv, vt, turns, w_qkv, s_gate, s_up, s_down, s_qkv,
):
    me = place()
    dp, mp = lax.axis_index("dp"), lax.axis_index("mp")
    mover = Mover(send_sems, recv_sems, local_sems)
    mover.anyone = device_at(moved(me, "core", 1))
    cols_to = [(dp, (mp + k) % MP) for k in range(1, MP)]
    others = [moved(me, axis, step) for axis in ("x", "y") for step in (1, -1)]
    others += [moved(me, "core", 1), moved(me, "x", 2)]
    units = down_weight.shape[1]
    for share, weight in (
        (s_gate, gate_up_weight[:, 0, :]), (s_up, gate_up_weight[:, 1, :]), (s_down, down_weight[...])
    ):
        share[...] = jnp.zeros_like(share)
        share[:, :units] = weight.astype(bf16)
    s_gate[:, WIDE:] = out_weight[...].astype(bf16)
    for k in range(3):
        s_qkv[:, k * PAIR : (k + 1) * PAIR] = qkv_weight[k].astype(bf16)
    w_qkv[me["y"], me["x"] // 2, me["core"]] = s_qkv[...]
    x = stream[...].astype(f32)
    unit = x * lax.rsqrt(row_mean(x * x) + norm_epsilon)
    normed[me["z"], me["x"] % 2] = (unit * gains[0:1, :]).astype(bf16)
    greet(cols_to + [device_at(end) for end in others])

    tokens = gather_tokens_part(mover, me, normed)
    row = gather_row_part(mover, me, w_qkv)
    gate = gather_part(mover, me, s_gate, w_gate, GATHER_ORDERS[0])
    up = gather_plain(mover, me, s_up, w_up, GATHER_ORDERS[1])
    down = gather_plain(mover, me, s_down, w_down, GATHER_ORDERS[2])
    every = gather_plain(mover, me, s_qkv, w_rows, ROW_ORDER)
    starts = doc_starts(lens)

    def step(*tasks):
        for task in tasks:
            next(task, None)

    step(gate, row, tokens, up, down, every)
    turn_tables(starts, freq[...], turns)
    vt[PAIR:, :] = jnp.ones((16, LEN), bf16)
    lse_ref[...] = jnp.zeros_like(lse_ref)
    step(gate, row, up, down, every)
    step(gate, row)
    step(tokens)
    step(gate, row)
    step(tokens, up, down, every)
    step(gate)
    step(tokens)
    step(gate, up, down)
    step(tokens, row, every)
    step(gate)
    step(tokens, up, down, every)
    step(gate)
    weights = w_qkv[...].reshape(DP * SHARE, 3 * PAIR)
    for block in range(BLOCKS):
        project_block(
            block, normed[block // 2, block % 2], weights, first_values, starts, turns,
            cos_ref, sin_ref, q_ref, k_ref, v_ref, vt,
        )
    for block in range(BLOCKS):
        attend_block(block, starts, q_ref, k_ref, vt, out_ref, lse_ref)
    copies = []
    for k in (5, 3, 4, 2, 6, 7, 1):
        taker = (mp + k) % MP
        copy = pltpu.make_async_remote_copy(
            src_ref=out_ref.at[pl.ds(pl.multiple_of(taker * BLOCK, BLOCK), BLOCK)],
            dst_ref=heads.at[mp],
            send_sem=head_send.at[k],
            recv_sem=head_recv.at[k],
            device_id=(dp, taker),
            device_id_type=MESH,
        )
        copy.start()
        copies.append(copy)
    heads[mp] = out_ref[pl.ds(pl.multiple_of(mp * BLOCK, BLOCK), BLOCK), :]
    step(up, down, gate, every)
    for k in range(1, MP):
        giver = (mp + MP - k) % MP
        pltpu.make_async_remote_copy(
            src_ref=heads.at[giver],
            dst_ref=heads.at[giver],
            send_sem=head_send.at[k],
            recv_sem=head_recv.at[k],
            device_id=(dp, giver),
            device_id_type=MESH,
        ).wait_recv()
    step(up, down)
    step(gate, up, down, every)
    step(every)
    for copy in copies:
        copy.wait_send()
    mover.finish()


def front(lens, stream, gains, weights, first_values, collective_id):
    gate_up, down, out, qkv = weights
    cos, sin = angle_tables()
    flat = jax.ShapeDtypeStruct((LEN, PAIR), bf16)
    vm = pltpu.VMEM
    widths = (WIDE + SLIM, WIDE, WIDE)
    slots = 40 + 3 * 16 + 13 + 8
    return pl.pallas_call(
        front_kernel,
        out_shape=[jax.ShapeDtypeStruct((4, 2, 4, 2, 2, SHARE, w), bf16) for w in widths + (3 * PAIR,)]
        + [
            jax.ShapeDtypeStruct((4, 2) + stream.shape, bf16),
            flat, flat, flat, flat,
            jax.ShapeDtypeStruct((8, LEN), f32),
            jax.ShapeDtypeStruct((MP, BLOCK, PAIR), bf16),
        ],
        in_specs=[SMEM] + [VMEM] * 10,
        out_specs=[ANY] * 4 + [VMEM] * 7,
        scratch_shapes=[
            DMA((slots,)), DMA((slots,)), DMA((4,)), DMA((MP,)), DMA((MP,)),
            vm((PAIR + 16, LEN), bf16), vm((2, 4 * BLOCKS, PAIR), f32),
        ]
        + [vm((4, 2, 2, SHARE, 3 * PAIR), bf16)]
        + [vm((SHARE, w), bf16) for w in widths + (3 * PAIR,)],
        name="front",
        compiler_params=pltpu.CompilerParams(
            collective_id=collective_id, has_side_effects=True, vmem_limit_bytes=56 * MEGA
        ),
    )(lens, stream, gains, gate_up, down, out, qkv, first_values, cos, sin, frequency_row())

newton_a = 3.4445
newton_b = -4.775
newton_c = 2.0315
OWNERS = (12, 2, 6, 10, 0, 4, 8)
COLUMNS = (SLIM, SLIM, SLIM, SLIM, WIDE, WIDE, WIDE)
ASPECTS = (8.0, 8.0, 8.0, 1.0, 1024 / 352, 1024 / 352, 1.0)


def halves(x):
    high = x.astype(bf16)
    return high, (x - high.astype(f32)).astype(bf16)


def left_side(x):
    high, low = halves(x)
    return jnp.concatenate([high, high, low], axis=1)


def right_side(x):
    high, low = halves(x)
    return jnp.concatenate([high, low, high], axis=0)


def newton_steps(stacked, result, gram, poly, total, moving, norm, left, right, wide_left):
    size = stacked.shape[-1]
    rows = DP * SHARE

    def held():
        return stacked[...].reshape(rows, size)

    def polynomial():
        one = gram[...]
        rank = lax.broadcasted_iota(jnp.int32, (size, size), 0)
        file = lax.broadcasted_iota(jnp.int32, (size, size), 1)
        left[0] = left_side(one)
        right[0] = right_side(one)
        poly[...] = (
            jnp.where(rank == file, newton_a, 0.0) + newton_b * one + newton_c * dot(left[0], right[0])
        )
        right[1] = right_side(poly[...])

    def advance():
        half = dot(left[0], right[1])
        gram[...] = dot(left_side(half), right[1])

    def gather():
        total[...] = dot(left_side(total[...]), right[1])

    def begin():
        block = held()
        wide = block.astype(f32)
        length = jnp.sqrt(jnp.sum(wide * wide)) + 1e-07
        inverse = jnp.full((1, size), 1.0, f32) / length
        norm[0:1, :size] = inverse
        turned = wide.T.astype(bf16)
        gram[...] = dot(turned, block) * (inverse * inverse)

    def first():
        polynomial()
        total[...] = poly[...]

    def middle():
        high, low = halves(total[...])
        block = held()
        moving[...] = (dot(block, high) + dot(block, low)) * norm[0:1, :size]

    def regram():
        now = moving[...]
        high, low = halves(now)
        wide_left[...] = jnp.concatenate([high, high, low], axis=1)
        turned = now.T
        turned_high, turned_low = halves(turned)
        gram[...] = dot(turned_high, high) + (dot(turned_high, low) + dot(turned_low, high))

    def end():
        ending = dot(wide_left[...], right_side(total[...]))
        result[...] = ending.astype(bf16).reshape(DP, SHARE, size)

    return [
        begin, first, advance, polynomial, gather, middle, regram,
        first, advance, polynomial, gather, advance, polynomial, gather, end,
    ]


def newton_scratch(size):
    square = pltpu.VMEM((size, size), f32)
    return [
        square, square, square, pltpu.VMEM((DP * SHARE, size), f32), pltpu.VMEM((8, size), f32),
        pltpu.VMEM((1, size, 3 * size), bf16), pltpu.VMEM((2, 3 * size, size), bf16),
        pltpu.VMEM((DP * SHARE, 3 * size), bf16),
    ]


def link(src, dst, send, recv, device):
    return pltpu.make_async_remote_copy(
        src_ref=src, dst_ref=dst, send_sem=send, recv_sem=recv, device_id=device, device_id_type=MESH
    )


def back_kernel(
    lens, q_ref, k_ref, v_ref, heads_ref, lse_ref, grad_parts, all_normed, cos_ref, sin_ref, freq,
    k_gate, k_up, k_down, k_out, all_rows, *rest,
):
    landed, rest = [rest[4 * k : 4 * k + 4] for k in range(3)], rest[12:]
    (
        qkv_momentum,
    out_momentum, gate_up_momentum, down_momentum,
        stream, gain_two,
        values_grad, m_qkv, m_out, m_gate, m_up, m_down, o_q, o_k, o_v, o_out, o_gate, o_up, o_down,
        summed, gain_grad,
        send_sems, recv_sems, local_sems, head_send, head_recv, dp_send, dp_recv, own_send, own_recv,
        back_send, back_recv, all_send, all_recv, proj_send, proj_recv,
        turns, grad_heads, kt, dqt, delta, dproj_t, dproj, dproj_in, w_rows, g_qkv, normed,
        dp_land, qkv_share, wide_share, slim_share, wide_in, wide_out, slim_in, slim_out,
        gain_dp, gain_mp, *own_lands,
    ) = rest
    newton, own_lands = own_lands[:16], own_lands[16:]
    mover = Mover(send_sems, recv_sems, local_sems)
    me = place()
    dp, mp = lax.axis_index("dp"), lax.axis_index("mp")
    mover.anyone = device_at(moved(me, "core", 1))
    rows_to = [((dp + k) % DP, mp) for k in range(1, DP)]
    cols_to = [(dp, (mp + k) % MP) for k in range(1, MP)]
    kept_from = (k_gate, k_up, k_down, k_out)
    scratch = [own_lands[13 * index : 13 * (index + 1)] for index in range(4)]
    loads = [mover.local(source, own[0]) for source, own in zip(kept_from, scratch)]
    early = []
    for sources, own in zip(landed, scratch):
        up, down, from_minus, from_plus = own[1:5]
        early.append(
            [
                mover.local(source, target)
                for source, target in (
                    (sources[0], up), (sources[1], down),
                    (half_of(sources[2], 1), half_of(from_minus, 1)),
                    (half_of(sources[3], 0), half_of(from_plus, 0)),
                )
            ]
        )
    loads += [mover.local(all_rows, w_rows), mover.local(all_normed, normed)]
    greet(rows_to + cols_to + [device_at(moved(me, "x", step)) for step in (1, -1)])

    def rows_of(index):
        return pl.ds(pl.multiple_of(index * BLOCK, BLOCK), BLOCK)

    head_copies = []
    for k in (5, 3, 4, 2, 6, 7, 1):
        taker = (mp + k) % MP
        copy = link(
            grad_parts.at[taker], grad_heads.at[rows_of(mp)], head_send.at[k], head_recv.at[k], (dp, taker)
        )
        copy.start()
        head_copies.append(copy)
    grad_heads[rows_of(mp), :] = grad_parts[mp]

    sums = (m_gate, m_up, m_down, m_out)
    scatters = []
    for index in range(4):
        own = scratch[index]
        phases = [own[1 + 4 * phase : 5 + 4 * phase] for phase in range(3)]
        scatters.append(scatter_part(mover, me, own[0], phases, sums[index], ORDERS[index], index < 3))

    def step(*tasks):
        for task in tasks:
            next(task, None)

    for index in (3, 0, 1, 2):
        loads[index].wait()
        for copy in early[index] if index < 3 else ():
            copy.wait()
        step(scatters[index])
    starts = doc_starts(lens)
    turn_tables(starts, freq[...], turns)
    for k in range(1, MP):
        giver = (mp + MP - k) % MP
        region = grad_heads.at[rows_of(giver)]
        link(region, region, head_send.at[k], head_recv.at[k], (dp, giver)).wait_recv()
    attention = attend_back(
        starts, q_ref, k_ref, v_ref, heads_ref, grad_heads, lse_ref, normed, cos_ref, sin_ref,
        turns, values_grad, g_qkv, dproj, kt, dqt, delta, dproj_t,
    )

    def pass_rows(block):
        return link(
            dproj.at[block], dproj_in.at[mp], proj_send.at[block], proj_recv.at[mp], (dp, block)
        )

    step(attention)
    for block in range(BLOCKS):
        step(attention)

        @pl.when(mp != block)
        def away():
            pass_rows(block).start()

        @pl.when(mp == block)
        def here():
            dproj_in[mp] = dproj[block]

        if block in (0, 2, 4, 6, 7):
            step(*scatters)
    loads[5].wait()
    step(attention)
    dp_copies = []
    for k in range(1, DP):
        taker = (dp + k) % DP
        copy = link(g_qkv.at[taker], dp_land.at[dp], dp_send.at[k], dp_recv.at[k], (taker, mp))
        copy.start()
        dp_copies.append(copy)
    dp_land[dp] = g_qkv[dp]
    step(*scatters)
    step(*scatters)

    results = (o_q, o_k, o_v, o_out, o_gate, o_up, o_down)

    def give(index, share):
        owner = OWNERS[index]
        land = wide_in if COLUMNS[index] == WIDE else slim_in
        copy = link(share, land.at[dp], own_send.at[index], own_recv.at[dp], (owner, mp))

        @pl.when(dp != owner)
        def away():
            copy.start()

        @pl.when(dp == owner)
        def here():
            land[dp] = share[...]

        return owner, copy

    def settle(given):
        owner, copy = given

        @pl.when(dp != owner)
        def away():
            copy.wait_send()

    def take(index):
        land = wide_in if COLUMNS[index] == WIDE else slim_in
        for k in range(1, DP):
            giver = (dp + k) % DP
            region = land.at[giver]
            link(region, region, own_send.at[index], own_recv.at[giver], (giver, mp)).wait_recv()

    def returns(index, wait):
        made = wide_out if COLUMNS[index] == WIDE else slim_out
        for k in range(1, DP):
            taker = (dp + k) % DP
            copy = link(made.at[taker], results[index], back_send.at[taker], back_recv.at[index], (taker, mp))
            copy.wait_send() if wait else copy.start()

    def owned(columns):
        chosen = [i for i in range(len(OWNERS)) if COLUMNS[i] == columns]
        if columns == WIDE:
            steps = newton_steps(wide_in, wide_out, *newton[:8])
        else:
            steps = newton_steps(slim_in, slim_out, *newton[8:])
        mine = functools.reduce(jnp.logical_or, [dp == OWNERS[i] for i in chosen])
        for index in chosen:
            pl.when(dp == OWNERS[index])(functools.partial(take, index))
        for one in steps:
            pl.when(mine)(one)
            yield
        for index in chosen:
            pl.when(dp == OWNERS[index])(functools.partial(returns, index, False))

            @pl.when(dp == OWNERS[index])
            def keep():
                made = wide_out if COLUMNS[index] == WIDE else slim_out
                results[index][...] = made[dp]

    units = down_momentum.shape[1]
    m_out[...] += 0.5 * out_momentum[...]
    m_gate[:, :units] += 0.5 * gate_up_momentum[:, 0, :]
    m_up[:, :units] += 0.5 * gate_up_momentum[:, 1, :]
    m_down[:, :units] += 0.5 * down_momentum[...]
    slim_share[...] = m_out[...].astype(bf16)
    for k, moment in enumerate((m_gate, m_up, m_down)):
        wide_share[k] = moment[...].astype(bf16)
    given = [give(4 + k, wide_share.at[k]) for k in range(3)] + [give(3, slim_share)]

    def gains_task():
        loads[4].wait()
        for k in range(1, MP):
            giver = (mp + k) % MP
            region = dproj_in.at[giver]
            link(region, region, proj_send.at[0], proj_recv.at[giver], (dp, giver)).wait_recv()
        grad_normed = jnp.zeros(summed.shape, f32)
        for m in range(MP):
            grad_normed = grad_normed + dot_t(dproj_in[m], w_rows[m])
        summed[...] = grad_normed
        x = stream[...].astype(f32)
        unit = x * lax.rsqrt(row_mean(x * x) + norm_epsilon)
        gain_dp[dp] = jnp.concatenate(
            [jnp.sum(grad_normed * unit, axis=0, keepdims=True), gain_two[...]], axis=0
        )
        copies = []
        for k in range(1, DP):
            copy = link(
                gain_dp.at[dp], gain_dp.at[dp], all_send.at[k], all_recv.at[k], ((dp + k) % DP, mp)
            )
            copy.start()
            copies.append(copy)
        yield
        for k in range(1, DP):
            giver = (dp + DP - k) % DP
            region = gain_dp.at[giver]
            link(region, region, all_send.at[k], all_recv.at[k], (giver, mp)).wait_recv()
        total = gain_dp[0]
        for k in range(1, DP):
            total = total + gain_dp[k]
        gain_mp[mp] = total
        for k in range(1, MP):
            copy = link(
                gain_mp.at[mp], gain_mp.at[mp], all_send.at[DP + k], all_recv.at[DP + k], (dp, (mp + k) % MP)
            )
            copy.start()
            copies.append(copy)
        yield
        for k in range(1, MP):
            giver = (mp + MP - k) % MP
            region = gain_mp.at[giver]
            link(region, region, all_send.at[DP + k], all_recv.at[DP + k], (dp, giver)).wait_recv()
        total = gain_mp[0]
        for k in range(1, MP):
            total = total + gain_mp[k]
        gain_grad[...] = total
        for copy in copies:
            copy.wait_send()

    def qkv_task():
        for k in range(1, DP):
            giver = (dp + DP - k) % DP
            region = dp_land.at[giver]
            link(region, region, dp_send.at[k], dp_recv.at[k], (giver, mp)).wait_recv()
        total = jnp.zeros((SHARE, WIDE), f32)
        for k in range(DP):
            total = total + dp_land[k].astype(f32)
        for k in range(3):
            cols = slice(k * SLIM, (k + 1) * SLIM)
            moment = 0.5 * qkv_momentum[k] + total[:, cols]
            m_qkv[:, cols] = moment
            qkv_share[k] = moment.astype(bf16)
        given.extend(give(k, qkv_share.at[k]) for k in range(3))
        yield
        yield from owned(SLIM)

    gains, sums_task, wide_task = gains_task(), qkv_task(), owned(WIDE)
    step(gains)
    step(sums_task)
    for _ in range(8):
        step(wide_task)
    step(gains)
    for _ in range(8):
        step(wide_task)
    for _ in range(16):
        step(sums_task)
    step(gains)
    for index, owner in enumerate(OWNERS):

        @pl.when(dp != owner)
        def arrive():
            link(
                results[index], results[index], back_send.at[0], back_recv.at[index], (owner, mp)
            ).wait_recv()

        pl.when(dp == owner)(functools.partial(returns, index, True))
    for copy in head_copies + dp_copies:
        copy.wait_send()
    for block in range(BLOCKS):

        @pl.when(mp != block)
        def sent():
            pass_rows(block).wait_send()

    for one in given:
        settle(one)
    mover.finish()


def back_block(
    lens, q, k, v, heads_out, lse, grad_parts, normed, kept, all_rows, landed, momenta, stream, gain_two, collective_id,
):
    cos, sin = angle_tables()
    tokens, width = stream.shape
    vm = pltpu.VMEM
    slim, wide = (jax.ShapeDtypeStruct((SHARE, c), bf16) for c in (SLIM, WIDE))
    full = jax.ShapeDtypeStruct((SHARE, WIDE), f32)
    lands = []
    for index, source in enumerate(kept):
        rows, cols = source.shape[-2:]
        lands.append(vm(source.shape, bf16))
        for phase in range(3):
            lead = lead_shape(ORDERS[index][phase + 1 :])
            lands += [vm(lead + (rows // 2, cols), bf16)] * 2 + [vm(lead + (rows, cols), bf16)] * 2
    slots = 18 * len(kept)
    return pl.pallas_call(
        back_kernel,
        out_shape=[
            jax.ShapeDtypeStruct((LEN, PAIR), f32),
            full, jax.ShapeDtypeStruct((SHARE, SLIM), f32), full, full, full,
            slim, slim, slim, slim, wide, wide, wide,
            jax.ShapeDtypeStruct((tokens, width), f32),
            jax.ShapeDtypeStruct((2, width), f32),
        ],
        in_specs=[SMEM] + [VMEM] * 6 + [ANY] + [VMEM] * 3 + [ANY] * 17 + [VMEM] * 6,
        out_specs=[VMEM] * 15,
        scratch_shapes=[
            DMA((slots,)), DMA((slots,)), DMA((19,)), DMA((MP,)), DMA((MP,)),
            DMA((DP,)), DMA((DP,)), DMA((7,)), DMA((DP,)), DMA((DP,)), DMA((7,)),
            DMA((DP + MP,)), DMA((DP + MP,)), DMA((MP,)), DMA((MP,)),
            vm((2, 4 * BLOCKS, PAIR), f32), vm((LEN, PAIR), bf16),
            vm((PAIR, LEN), bf16), vm((PAIR, LEN), f32), vm((8, LEN), f32),
            vm((3 * PAIR, LEN), bf16), vm((BLOCKS, BLOCK, 3 * PAIR), bf16), vm((MP, BLOCK, 3 * PAIR), bf16),
            vm((MP, width, 3 * PAIR), bf16), vm((DP, SHARE, WIDE), bf16),
            vm((4, 2, tokens, width), bf16),
            vm((DP, SHARE, WIDE), bf16), vm((3, SHARE, SLIM), bf16), vm((3, SHARE, WIDE), bf16),
            vm((SHARE, SLIM), bf16),
            vm((DP, SHARE, WIDE), bf16), vm((DP, SHARE, WIDE), bf16),
            vm((DP, SHARE, SLIM), bf16), vm((DP, SHARE, SLIM), bf16),
            vm((DP, 2, width), f32), vm((MP, 2, width), f32),
        ]
        + newton_scratch(WIDE)
        + newton_scratch(SLIM)
        + lands,
        name="back",
        compiler_params=pltpu.CompilerParams(
            collective_id=collective_id, has_side_effects=True, vmem_limit_bytes=60 * MEGA
        ),
    )(
        lens, q, k, v, heads_out, lse, grad_parts, normed, cos, sin, frequency_row(),
        *kept, all_rows, *landed, *momenta, stream, gain_two,
    )

STEP = 10
muon_rate = 1.0
out_rate = 4.0
adam_rate = 0.8
beta_first = 0.9
beta_second = 0.95
adam_epsilon = 1e-08


def final_kernel(
    values_grad, m_qkv, m_out, m_gate, m_up, m_down, o_q, o_k, o_v, o_out, o_gate, o_up, o_down,
    summed, gain_grad, stream, grad_residual, gains, moment1, moment2,
    qkv_weight, out_weight, gate_up_weight, down_weight,
    input_grad, values_out, qkv_new, qkv_moment, out_new, out_moment, gate_up_new, gate_up_moment,
    down_new, down_moment, moment1_new, moment2_new, gains_new,
):
    units = down_weight.shape[1]
    tall = muon_rate * (stream.shape[1] / SLIM) ** 0.5
    broad = muon_rate * (stream.shape[1] / units) ** 0.5
    for k, orth in enumerate((o_q, o_k, o_v)):
        qkv_moment[k] = m_qkv[:, k * SLIM : (k + 1) * SLIM]
        qkv_new[k] = qkv_weight[k] - tall * orth[...].astype(f32)
    out_moment[...] = m_out[...]
    out_new[...] = out_weight[...] - out_rate * o_out[...].astype(f32)
    for k, (moment, orth) in enumerate(((m_gate, o_gate), (m_up, o_up))):
        gate_up_moment[:, k, :] = moment[:, :units]
        gate_up_new[:, k, :] = gate_up_weight[:, k, :] - broad * orth[:, :units].astype(f32)
    down_moment[...] = m_down[:, :units]
    down_new[...] = down_weight[...] - muon_rate * o_down[:, :units].astype(f32)
    values_out[...] = values_grad[...]
    x = stream[...].astype(f32)
    inverse = lax.rsqrt(row_mean(x * x) + norm_epsilon)
    unit = x * inverse
    scaled = summed[...] * gains[0:1, :]
    input_grad[...] = grad_residual[...] + inverse * (scaled - unit * row_mean(scaled * unit))
    grad = gain_grad[...]
    first = beta_first * moment1[...] + (1.0 - beta_first) * grad
    second = beta_second * moment2[...] + (1.0 - beta_second) * grad * grad
    moment1_new[...] = first
    moment2_new[...] = second
    corrected1 = first / (1.0 - beta_first**STEP)
    corrected2 = second / (1.0 - beta_second**STEP)
    gains_new[...] = gains[...] - adam_rate * corrected1 / (jnp.sqrt(corrected2) + adam_epsilon)


def final_block(values_grad, *rest):
    args = (values_grad,) + rest
    stream, residual, gains = rest[14], rest[15], rest[16]
    weights = rest[19:]
    like = lambda x: jax.ShapeDtypeStruct(x.shape, f32)
    return pl.pallas_call(
        final_kernel,
        out_shape=[like(residual), like(values_grad)]
        + [like(w) for weight in weights for w in (weight, weight)]
        + [like(gains)] * 3,
        in_specs=[VMEM] * len(args),
        out_specs=[VMEM] * 13,
        name="final",
        compiler_params=pltpu.CompilerParams(vmem_limit_bytes=56 * MEGA),
    )(*args)
def on_device(
    block_input, first_values, out_cotangent, doc_lengths, norm_gains, gain_moment1, gain_moment2,
    qkv_weight, qkv_momentum, out_weight, out_momentum, gate_up_weight, gate_up_momentum,
    down_weight, down_momentum,
):
    tokens, width = block_input.shape
    qkv_weight, qkv_momentum = (a.transpose(1, 0, 2) for a in (qkv_weight, qkv_momentum))
    out_weight, out_momentum, down_weight, down_momentum = (
        a.T for a in (out_weight, out_momentum, down_weight, down_momentum)
    )
    *wholes, all_rows, normed, q, k, v, heads_out, lse, heads = front(
        doc_lengths, block_input, norm_gains,
        (gate_up_weight, down_weight, out_weight, qkv_weight), first_values, 0,
    )
    w_gate, w_up, w_down = (w.reshape(GROUPS, width, w.shape[-1]) for w in wholes)
    block_output, grad_residual, grad_heads, gain_two, *rest = token_block(
        heads, block_input, out_cotangent, norm_gains, w_gate, w_up, w_down, 1
    )
    kept, landed = rest[:4], rest[4:]
    done = back_block(
        doc_lengths, q, k, v, heads_out, lse, grad_heads, normed,
        [g.reshape(4, 2, 4, 2, SHARE, g.shape[-1]) for g in kept],
        all_rows.reshape(GROUPS, width, all_rows.shape[-1]),
        landed,
        (qkv_momentum, out_momentum, gate_up_momentum, down_momentum),
        block_input, gain_two, 2,
    )
    (
        input_grad, values_grad, qkv_new, qkv_moment, out_new, out_moment,
        gate_up_new, gate_up_moment, down_new, down_moment, *gains_out,
    ) = final_block(
        *done, block_input, grad_residual, norm_gains, gain_moment1, gain_moment2,
        qkv_weight, out_weight, gate_up_weight, down_weight,
    )
    return (
        block_output, input_grad, values_grad,
        qkv_new.transpose(1, 0, 2), qkv_moment.transpose(1, 0, 2), out_new.T, out_moment.T,
        gate_up_new, gate_up_moment, down_new.T, down_moment.T, *gains_out,
    )


def solution(mesh):
    placed = (
        P(("dp", "mp"), None), P("dp", "mp"), P(("dp", "mp"), None), P("dp", None),
        P(), P(), P(),
        P("dp", None, "mp"), P("dp", None, "mp"), P("mp", "dp"), P("mp", "dp"),
        P("dp", None, "mp"), P("dp", None, "mp"), P("mp", "dp"), P("mp", "dp"),
    )
    return jax.shard_map(
        on_device,
        mesh=mesh,
        in_specs=placed,
        out_specs=(P(("dp", "mp"), None), P(("dp", "mp"), None), P("dp", "mp")) + placed[7:] + (P(),) * 3,
        check_vma=False,
    )
```

```python
import functools

import jax
import jax.numpy as jnp
import numpy as np
from jax import lax
from jax.experimental import pallas as pl
from jax.experimental.pallas import tpu as pltpu
from jax.sharding import PartitionSpec as P

MEGA = 2**20
f32, bf16 = jnp.float32, jnp.bfloat16
VMEM = pl.BlockSpec(memory_space=pltpu.VMEM)
SMEM = pl.BlockSpec(memory_space=pltpu.SMEM)

HD = 64
LEN = 2048
PAIR = 2 * HD
BLOCK = 256
BLOCKS = LEN // BLOCK
LOG2E = 1.4426950408889634
SCORE_SCALE = HD**-0.5 * LOG2E
mask_fill = -1e30


def dot(a, b):
    return lax.dot_general(a, b, (((1,), (0,)), ((), ())), preferred_element_type=f32)


def dot_t(a, b):
    return lax.dot_general(a, b, (((1,), (1,)), ((), ())), preferred_element_type=f32)


def frequency():
    half = HD // 2
    return np.tile(np.exp(-np.log(10000.0) * np.arange(half) * 2.0 / HD), PAIR // half)


def angle_tables():
    angles = np.arange(BLOCK)[:, None] * frequency()[None, :]
    return np.cos(angles).astype(np.float32), np.sin(angles).astype(np.float32)


def frequency_row():
    return frequency()[None, :].astype(np.float32)


def doc_starts(lens):
    one = lens[0, 0]
    two = one + lens[0, 1]
    return one, two, two + lens[0, 2]


def pick_start(place, starts):
    zero = jnp.zeros_like(place)
    picked = jnp.where(place >= starts[0], starts[0], zero)
    picked = jnp.where(place >= starts[1], starts[1], picked)
    return jnp.where(place >= starts[2], starts[2], picked)


def turn_tables(starts, freq, turns):
    row = lax.broadcasted_iota(jnp.int32, (4 * BLOCKS, PAIR), 0)
    doc = row % 4
    start = jnp.where(doc == 1, starts[0], 0)
    start = jnp.where(doc == 2, starts[1], start)
    start = jnp.where(doc == 3, starts[2], start)
    angle = (row // 4 * BLOCK - start).astype(f32) * freq
    turns[0] = jnp.cos(angle)
    turns[1] = jnp.sin(angle)


def block_angles(block, starts, turns, cos_ref, sin_ref):
    place = block * BLOCK + lax.broadcasted_iota(jnp.int32, (BLOCK, PAIR), 0)

    def pick(table):
        picked = turns[table, pl.ds(4 * block, 1), :]
        for doc, start in enumerate(starts):
            picked = jnp.where(place >= start, turns[table, pl.ds(4 * block + doc + 1, 1), :], picked)
        return picked

    cos_b, sin_b = pick(0), pick(1)
    return cos_ref[...] * cos_b - sin_ref[...] * sin_b, sin_ref[...] * cos_b + cos_ref[...] * sin_b


def swap_halves(x):
    lane = lax.broadcasted_iota(jnp.int32, x.shape, 1)
    front = lane % HD < HD // 2
    return front, jnp.where(front, pltpu.roll(x, PAIR - HD // 2, 1), pltpu.roll(x, HD // 2, 1))


def rotate(x, cos, sin):
    front, other = swap_halves(x)
    return x * cos + jnp.where(front, -other, other) * sin


def rotate_back(x, cos, sin):
    front, other = swap_halves(x)
    return x * cos + jnp.where(front, other, -other) * sin


def head_only(x, head):
    lane = lax.broadcasted_iota(jnp.int32, x.shape, 1)
    return jnp.where(lane // HD == head, x, jnp.zeros_like(x))


def project_block(block, tokens, w_qkv, first_values, starts, turns, cos_ref, sin_ref, q_ref, k_ref, v_ref, vt):
    rows = slice(block * BLOCK, (block + 1) * BLOCK)
    proj = dot(tokens, w_qkv)
    cos, sin = block_angles(block, starts, turns, cos_ref, sin_ref)
    q_ref[rows, :] = rotate(proj[:, :PAIR], cos, sin).astype(bf16)
    k_ref[rows, :] = rotate(proj[:, PAIR : 2 * PAIR], cos, sin).astype(bf16)
    mix = 0.5 * proj[:, 2 * PAIR :] + 0.5 * first_values[rows, :].astype(f32)
    v_ref[rows, :] = mix.astype(bf16)
    vt[:PAIR, rows] = mix.T.astype(bf16)


def attend_block(block, starts, q_ref, k_ref, vt, out_ref, lse_ref):
    rows = slice(block * BLOCK, (block + 1) * BLOCK)
    span = (block + 1) * BLOCK
    row_at = rows.start + lax.broadcasted_iota(jnp.int32, (1, BLOCK), 1)
    start_row = pick_start(row_at, starts)
    key_at = lax.broadcasted_iota(jnp.int32, (span, BLOCK), 0)
    allowed = (key_at >= start_row) & (key_at <= row_at)
    outs = []
    for head in range(2):
        scores = dot_t(k_ref[:span, :], head_only(q_ref[rows, :], head))
        scores = jnp.where(allowed, scores, mask_fill)
        top = jnp.max(scores, axis=0, keepdims=True) * SCORE_SCALE
        weights = jnp.exp2(scores * SCORE_SCALE - top).astype(bf16)
        values = jnp.concatenate([vt[head * HD : (head + 1) * HD, :span], vt[PAIR:, :span]], axis=0)
        mixed = dot(values, weights)
        total = mixed[HD : HD + 1, :]
        outs.append(mixed[:HD, :] / total)
        lse_ref[head : head + 1, rows] = top + jnp.log2(total)
    out_ref[rows, :] = jnp.concatenate(outs, axis=0).T.astype(bf16)


def attend_back(
    starts, q_ref, k_ref, v_ref, heads_ref, grad_ref, lse_ref, normed, cos_ref, sin_ref, turns,
    values_grad_ref, w_grad_ref, dproj_ref, kt, dqt, delta, dproj_t,
):
    for block in range(BLOCKS):
        rows = slice(block * BLOCK, (block + 1) * BLOCK)
        kt[:, rows] = k_ref[rows, :].astype(f32).T.astype(bf16)
        both = (grad_ref[rows, :].astype(f32) * heads_ref[rows, :].astype(f32)).T
        for head in range(2):
            delta[head : head + 1, rows] = jnp.sum(
                both[head * HD : (head + 1) * HD, :], axis=0, keepdims=True
            )
    dqt[...] = jnp.zeros_like(dqt)
    yield
    chunk = 2 * BLOCK
    for block in range(BLOCKS):
        keys = slice(block * BLOCK, (block + 1) * BLOCK)
        dk = jnp.zeros((BLOCK, PAIR), f32)
        dv = jnp.zeros((BLOCK, PAIR), f32)
        at = block * BLOCK
        while at < LEN:
            width = chunk if at % chunk == 0 else BLOCK
            rows = slice(at, at + width)
            at += width
            row_at = rows.start + lax.broadcasted_iota(jnp.int32, (1, width), 1)
            start_row = pick_start(row_at, starts)
            key_at = keys.start + lax.broadcasted_iota(jnp.int32, (BLOCK, width), 0)
            allowed = key_at >= start_row
            if rows.start == keys.start:
                allowed = allowed & (key_at <= row_at)
            for head in range(2):
                q_h = head_only(q_ref[rows, :], head)
                g_h = head_only(grad_ref[rows, :], head)
                scores = dot_t(k_ref[keys, :], q_h)
                prob = jnp.exp2(scores * SCORE_SCALE - lse_ref[head : head + 1, rows])
                prob = jnp.where(allowed, prob, 0.0)
                grad_prob = dot_t(v_ref[keys, :], g_h)
                grad_scores = (prob * (grad_prob - delta[head : head + 1, rows])).astype(bf16)
                dv = dv + dot(prob.astype(bf16), g_h)
                dk = dk + dot(grad_scores, q_h)
                lanes = slice(head * HD, (head + 1) * HD)
                dqt[lanes, rows] += dot(kt[lanes, keys], grad_scores)
        half_dv = 0.5 * dv
        values_grad_ref[keys, :] = half_dv
        cos, sin = block_angles(block, starts, turns, cos_ref, sin_ref)
        dq = rotate_back(dqt[:, keys].T * HD**-0.5, cos, sin)
        dk = rotate_back(dk * HD**-0.5, cos, sin)
        dproj = jnp.concatenate([dq, dk, half_dv], axis=1)
        dproj_t[:, keys] = dproj.T.astype(bf16)
        dproj_ref[block] = dproj.astype(bf16)
        yield
    for part in range(4):
        cols = slice(part * BLOCK, (part + 1) * BLOCK)
        tokens = normed[:, :, :, cols].reshape(LEN, BLOCK)
        made = dot(dproj_t[...], tokens).T.astype(bf16)
        w_grad_ref[part * 4 : (part + 1) * 4] = made.reshape(4, BLOCK // 4, 3 * PAIR)


MESH = pl.DeviceIdType.MESH
ANY = pl.BlockSpec(memory_space=pl.ANY)
DMA = pltpu.SemaphoreType.DMA


def place():
    dp, mp = lax.axis_index("dp"), lax.axis_index("mp")
    return {"x": (dp // 2) % 2 * 2 + mp % 2, "y": dp // 4, "z": mp // 2, "core": dp % 2}


def device_at(at):
    return ((at["y"] * 2 + at["x"] // 2) * 2 + at["core"], at["z"] * 2 + at["x"] % 2)


def moved(at, axis, step):
    new = dict(at)
    if axis == "core":
        new[axis] = 1 - at[axis]
    elif axis == "pair":
        new["x"] = at["x"] + 1 - 2 * (at["x"] % 2)
    else:
        new[axis] = (at[axis] + step + 4) % 4
    return new


def greet(devices):
    barrier = pltpu.get_barrier_semaphore()
    for device in devices:
        pl.semaphore_signal(barrier, inc=1, device_id=device, device_id_type=MESH)
    pl.semaphore_wait(barrier, len(devices))


class Mover:
    def __init__(self, send_sems, recv_sems, local_sems=None):
        self.send_sems, self.recv_sems, self.local_sems = send_sems, recv_sems, local_sems
        self.used, self.locals, self.started = 0, 0, []

    def remote(self, src, dst, device, slot):
        return pltpu.make_async_remote_copy(
            src_ref=src,
            dst_ref=dst,
            send_sem=self.send_sems.at[slot],
            recv_sem=self.recv_sems.at[slot],
            device_id=device,
            device_id_type=MESH,
        )

    def send(self, src, dst, device):
        slot = self.used
        self.used += 1
        copy = self.remote(src, dst, device, slot)
        copy.start()
        self.started.append(copy)
        return slot

    def arrived(self, slot, region):
        self.remote(region, region, self.anyone, slot).wait_recv()

    def local(self, src, dst):
        copy = pltpu.make_async_copy(src, dst, self.local_sems.at[self.locals])
        self.locals += 1
        copy.start()
        return copy

    def finish(self):
        for copy in self.started:
            copy.wait_send()


def weave(*tasks):
    tasks = list(tasks)
    while tasks:
        for task in list(tasks):
            try:
                next(task)
            except StopIteration:
                tasks.remove(task)


def blocks_of(ref, at, whole, half=None, core=True):
    index = (
        slice(None) if "z" in whole else at["z"],
        slice(None) if "x" in whole else at["x"] % 2,
        slice(None) if "y" in whole else at["y"],
        slice(None) if "x" in whole else at["x"] // 2,
    )
    if core:
        index = index + (at["core"],)
    if half is not None:
        rows = ref.shape[-2] // 2
        index = index + (pl.ds(half * rows, rows),)
    return ref.at[index]


GATHER_ORDERS = (("z", "x", "y"), ("y", "z", "x"), ("y", "x", "z"))
ROW_ORDER = ("z", "x", "y")
ORDERS = (("x", "z", "y"), ("z", "x", "y"), ("y", "z", "x"), ("y", "x", "z"))
ORDERS = (("x", "y", "z"), ("y", "z", "x"), ("z", "x", "y"), ("y", "x", "z"))
RING = ("x", "y", "z")


def ring_ends(me):
    return [moved(me, axis, step) for axis in RING for step in (1, -1)] + [moved(me, "core", 1)]


def gather_part(mover, me, part, whole, order):
    sibling = moved(me, "core", 1)
    twin = device_at(sibling)
    mirrors = []
    one, two, three = order

    def pass_on(region, target):
        return mover.send(region, region, device_at(target))

    def four(at, half=None):
        return blocks_of(whole, at, (one,), half)

    def mirror(at):
        mine = four(at)
        slot = mover.send(mine, mine, twin)
        mirrors.append((slot, four(moved(at, "core", 1))))

    def ends(at, axis):
        return moved(at, axis, 1), moved(at, axis, -1), moved(at, axis, 2)

    def spread(at):
        plus, minus, _ = ends(me, three)
        slots = pass_on(four(at), plus), pass_on(four(at), minus)
        mirror(at)
        return at, slots

    def relay(sent):
        at, slots = sent
        plus, minus, across = ends(at, three)
        mover.arrived(slots[0], four(minus))
        up = pass_on(four(minus, 0), moved(me, three, 1))
        mover.arrived(slots[1], four(plus))
        down = pass_on(four(plus, 1), moved(me, three, -1))
        mirror(minus)
        mirror(plus)
        return across, (up, down)

    own = blocks_of(whole, me, ())
    mover.local(part, own).wait()
    plus, minus, across = ends(me, one)
    up, down = pass_on(own, plus), pass_on(own, minus)
    yield
    mover.arrived(up, blocks_of(whole, minus, ()))
    up = pass_on(blocks_of(whole, minus, (), 0), plus)
    mover.arrived(down, blocks_of(whole, plus, ()))
    down = pass_on(blocks_of(whole, plus, (), 1), minus)
    yield
    mover.arrived(up, blocks_of(whole, across, (), 0))
    mover.arrived(down, blocks_of(whole, across, (), 1))
    plus, minus, across = ends(me, two)
    up, down = pass_on(four(me), plus), pass_on(four(me), minus)
    sets = [spread(me)]
    yield
    mover.arrived(up, four(minus))
    up = pass_on(four(minus, 0), plus)
    mover.arrived(down, four(plus))
    down = pass_on(four(plus, 1), minus)
    sets += [spread(minus), spread(plus)]
    yield
    mover.arrived(up, four(across, 0))
    mover.arrived(down, four(across, 1))
    sets.append(spread(across))
    yield
    lasts = [relay(sets[0])]
    yield
    lasts += [relay(sets[1]), relay(sets[2])]
    yield
    lasts.append(relay(sets[3]))
    yield
    for at, slots in lasts:
        mover.arrived(slots[0], four(at, 0))
        mover.arrived(slots[1], four(at, 1))
        mirror(at)
    yield
    for slot, region in mirrors:
        mover.arrived(slot, region)


def gather_plain(mover, me, part, whole, order):
    twin = device_at(moved(me, "core", 1))
    mirrors = []

    def pass_on(region, target):
        return mover.send(region, region, device_at(target))

    def mirror(at, done):
        mine = blocks_of(whole, at, done)
        slot = mover.send(mine, mine, twin)
        mirrors.append((slot, blocks_of(whole, moved(at, "core", 1), done)))

    mover.local(part, blocks_of(whole, me, ())).wait()
    for phase, axis in enumerate(order):
        done = order[:phase]
        plus, minus, across = moved(me, axis, 1), moved(me, axis, -1), moved(me, axis, 2)
        mine = blocks_of(whole, me, done)
        up, down = pass_on(mine, plus), pass_on(mine, minus)
        if phase == 2:
            mirror(me, done)
        yield
        mover.arrived(up, blocks_of(whole, minus, done))
        up = pass_on(blocks_of(whole, minus, done, 0), plus)
        mover.arrived(down, blocks_of(whole, plus, done))
        down = pass_on(blocks_of(whole, plus, done, 1), minus)
        if phase == 2:
            mirror(minus, done)
            mirror(plus, done)
        yield
        mover.arrived(up, blocks_of(whole, across, done, 0))
        mover.arrived(down, blocks_of(whole, across, done, 1))
        if phase == 2:
            mirror(across, done)
    yield
    for slot, region in mirrors:
        mover.arrived(slot, region)


LEAD = 176


def gather_tokens_part(mover, me, whole):
    mate, plus, minus, across = (
        moved(me, "pair", 1),
        moved(me, "z", 1),
        moved(me, "z", -1),
        moved(me, "z", 2),
    )
    rows = whole.shape[-2]
    rest = rows - LEAD
    cut = (rest // 2 + 15) // 16 * 16
    lead, tail = pl.ds(0, LEAD), pl.ds(LEAD, rest)
    tails = (pl.ds(LEAD, cut), pl.ds(LEAD + cut, rest - cut))

    def at(place_, span):
        return whole.at[place_["z"], place_["x"] % 2, span]

    def both(place_, side=None):
        return whole.at[place_["z"], slice(None) if side is None else side, lead]

    def pass_on(region, target):
        return mover.send(region, region, device_at(target))

    pair = pass_on(at(me, lead), mate)
    ring = pass_on(at(me, tail), plus), pass_on(at(me, tail), minus)
    crossed = [(pass_on(at(me, tail), mate), at(moved(me, "pair", 1), tail))]
    yield
    mover.arrived(pair, at(mate, lead))
    wide = pass_on(both(me), plus), pass_on(both(me), minus)
    yield
    mover.arrived(ring[0], at(minus, tail))
    relay = [pass_on(at(minus, tails[0]), plus)]
    crossed.append((pass_on(at(minus, tail), mate), at(moved(minus, "pair", 1), tail)))
    mover.arrived(ring[1], at(plus, tail))
    relay.append(pass_on(at(plus, tails[1]), minus))
    crossed.append((pass_on(at(plus, tail), mate), at(moved(plus, "pair", 1), tail)))
    yield
    mover.arrived(relay[0], at(across, tails[0]))
    mover.arrived(relay[1], at(across, tails[1]))
    crossed.append((pass_on(at(across, tail), mate), at(moved(across, "pair", 1), tail)))
    yield
    mover.arrived(wide[0], both(minus))
    last = [pass_on(both(minus, 0), plus)]
    mover.arrived(wide[1], both(plus))
    last.append(pass_on(both(plus, 1), minus))
    yield
    for slot, region in crossed:
        mover.arrived(slot, region)
    mover.arrived(last[0], both(across, 0))
    mover.arrived(last[1], both(across, 1))


def load(ref):
    return ref[...].astype(f32)


def each_block(ref, body):
    lead = ref.shape[:-2]
    total = 1
    for size in lead:
        total *= size

    def step(flat, carry):
        index = []
        for size in reversed(lead):
            index.append(flat % size)
            flat = flat // size
        body(tuple(reversed(index)))
        return carry

    if total == 1:
        body((0,) * len(lead))
    else:
        lax.fori_loop(0, total, step, 0)


def add_into(target, *terms):
    def body(index):
        total = target[index].astype(f32)
        for term in terms:
            total = total + term[index].astype(f32)
        target[index] = total.astype(target.dtype)

    each_block(target, body)


def half_of(ref, half):
    rows = ref.shape[-2] // 2
    return ref.at[(slice(None),) * (len(ref.shape) - 2) + (pl.ds(half * rows, rows),)]


def scatter_part(mover, me, kept, lands, out, order, early=False):
    for phase, axis in enumerate(order):
        rest = order[phase + 1 :]
        plus, minus, across = moved(me, axis, 1), moved(me, axis, -1), moved(me, axis, 2)
        hop_up, hop_down, from_minus, from_plus = lands[phase]
        landed = early and phase == 0

        def part(at, half=None):
            return blocks_of(kept, at, rest, half, core=False)

        if not landed:
            up = mover.send(part(across, 0), hop_up, device_at(plus))
            down = mover.send(part(across, 1), hop_down, device_at(minus))
            plain_up = mover.send(part(plus, 1), half_of(from_minus, 1), device_at(plus))
            plain_down = mover.send(part(minus, 0), half_of(from_plus, 0), device_at(minus))
            yield
            mover.arrived(up, hop_up)
        add_into(part(plus, 0), hop_up)
        up = mover.send(part(plus, 0), half_of(from_minus, 0), device_at(plus))
        if not landed:
            mover.arrived(down, hop_down)
        add_into(part(minus, 1), hop_down)
        down = mover.send(part(minus, 1), half_of(from_plus, 1), device_at(minus))
        yield
        if not landed:
            mover.arrived(plain_up, half_of(from_minus, 1))
            mover.arrived(plain_down, half_of(from_plus, 0))
        mover.arrived(up, half_of(from_minus, 0))
        mover.arrived(down, half_of(from_plus, 1))
        if phase < 2:
            add_into(part(me), from_minus, from_plus)
        else:
            out[...] = load(part(me)) + load(from_minus) + load(from_plus)


def lead_shape(whole):
    shape = ()
    for axis, size in (("z", 4), ("x", 2), ("y", 4), ("x", 2)):
        if axis in whole:
            shape = shape + (size,)
    return shape

norm_epsilon = 1e-06
GROUPS = 8
DP, MP = 16, 8
SHARE = 64
WIDE, SLIM = 384, 128


def group_at(step):
    return step % 4 * 2 + step // 4


def row_mean(x):
    return jnp.mean(x, axis=-1, keepdims=True)


def token_kernel(
    heads, stream, cotangent, gains, w_gate, w_up, w_down, w_out,
    block_output, grad_residual, grad_heads, gain_part, k_gate, k_up, k_down, k_out, *rest,
):
    lands = [rest[4 * k : 4 * k + 4] for k in range(3)]
    (
        residual, normed, normed_t, cot_t, ffn, grad_normed,
        made, twin, made_out, twin_out, send_sems, recv_sems, out_sems,
        gate_send, gate_recv, up_send, up_recv, down_send, down_recv,
    ) = rest[12:]
    group = pl.program_id(0)
    gain = gains[1:2, :]
    me = place()
    ends = [device_at(end) for end in ring_ends(me)]

    sibling = device_at(moved(me, "core", 1))

    def pass_half(m):
        return [
            pltpu.make_async_remote_copy(
                src_ref=made.at[m % 2, k, :, :, 1 - me["core"]],
                dst_ref=twin.at[m, k],
                send_sem=send_sems.at[m, k],
                recv_sem=recv_sems.at[m, k],
                device_id=sibling,
                device_id_type=MESH,
            )
            for k in range(3)
        ]

    def pass_out():
        return pltpu.make_async_remote_copy(
            src_ref=made_out.at[:, :, 1 - me["core"]],
            dst_ref=twin_out,
            send_sem=out_sems.at[0],
            recv_sem=out_sems.at[1],
            device_id=sibling,
            device_id_type=MESH,
        )

    ahead = {axis: (device_at(moved(me, axis, 1)), device_at(moved(me, axis, -1))) for axis in RING}

    def hop(src, dst, sems, slot, device):
        return pltpu.make_async_remote_copy(
            src_ref=src, dst_ref=dst, send_sem=sems[0].at[slot], recv_sem=sems[1].at[slot],
            device_id=device, device_id_type=MESH,
        )

    def first_sends(piece, land, sems, index, where, axis):
        up, down, from_minus, from_plus = land
        plus, minus = ahead[axis]
        return {
            "far": (
                hop(half_of(piece, 0), up.at[where], sems, (0,) + index, plus),
                hop(half_of(piece, 1), down.at[where], sems, (1,) + index, minus),
            ),
            "plus": (hop(half_of(piece, 1), half_of(from_minus.at[where], 1), sems, (2,) + index, plus),),
            "minus": (hop(half_of(piece, 0), half_of(from_plus.at[where], 0), sems, (3,) + index, minus),),
        }

    def go(copies, delta):
        for name, value in (("plus", 1), ("far", 2), ("minus", 3)):

            @pl.when(delta == value)
            def start():
                for copy in copies[name]:
                    copy.start()

    gate_sems, up_sems, down_sems = (gate_send, gate_recv), (up_send, up_recv), (down_send, down_recv)

    def start_round(slot):
        m = group_at(slot)
        z, side = m // 2, m % 2
        for x_half in range(2):
            delta = (2 * x_half + side - me["x"] + 4) % 4
            piece = twin.at[slot, 0, :, x_half]
            go(first_sends(piece, lands[0], gate_sems, (z,), (z,), "x"), delta)
        for step, name in ((2, "far"), (1, "plus"), (3, "minus")):
            piece = twin.at[slot, 1, (me["y"] + step) % 4]
            for copy in first_sends(piece, lands[1], up_sems, (m,), (z, side), "y")[name]:
                copy.start()
        go(
            first_sends(twin.at[slot, 2], lands[2], down_sems, (side,), (side,), "z"),
            (z - me["z"] + 4) % 4,
        )

    def end_round():
        for land, sems, count, where in (
            (lands[0], gate_sems, 4, lambda i: (i,)),
            (lands[1], up_sems, 8, lambda i: (i // 2, i % 2)),
            (lands[2], down_sems, 2, lambda i: (i,)),
        ):
            for i in range(count):
                regions = (
                    land[0].at[where(i)], land[1].at[where(i)],
                    half_of(land[2].at[where(i)], 1), half_of(land[3].at[where(i)], 0),
                )
                for kind, region in enumerate(regions):
                    copy = hop(region, region, sems, (kind, i), sibling)
                    copy.wait_recv()
                    copy.wait_send()

    @pl.when(group == 0)
    def first():
        greet(ends)
        branch = jnp.zeros(residual.shape, f32)
        for m in range(GROUPS):
            branch = branch + dot_t(heads[m], w_out[m]).astype(bf16).astype(f32)
        total = stream[...].astype(f32) + branch
        residual[...] = total
        unit = total * lax.rsqrt(row_mean(total * total) + norm_epsilon)
        scaled = unit * gain
        normed[...] = scaled.astype(bf16)
        normed_t[...] = scaled.T.astype(bf16)
        cot_t[...] = cotangent[...].astype(f32).T.astype(bf16)
        ffn[...] = jnp.zeros_like(ffn)
        grad_normed[...] = jnp.zeros_like(grad_normed)

    @pl.when(group < GROUPS)
    def one():
        gate = dot(normed[...], w_gate[0, :, :WIDE])
        up = dot(normed[...], w_up[0])
        sigmoid = jax.nn.sigmoid(gate)
        silu = gate * sigmoid
        hidden = (silu * up).astype(bf16)
        ffn[...] += dot_t(hidden, w_down[0]).astype(bf16).astype(f32)
        grad_hidden = dot(cotangent[...], w_down[0])
        slope = sigmoid * (1.0 + gate * (1.0 - sigmoid))
        grad_gate = (grad_hidden * up * slope).astype(bf16)
        grad_up = (grad_hidden * silu).astype(bf16)
        grad_normed[...] += dot_t(grad_gate, w_gate[0, :, :WIDE]) + dot_t(grad_up, w_up[0])
        half = group % 2
        shape = made.shape[2:]
        grad_both = jnp.concatenate([grad_gate, grad_up], axis=1)
        grad_weight = dot(normed_t[...], grad_both).astype(bf16)
        made[half, 0] = grad_weight[:, :WIDE].reshape(shape)
        made[half, 1] = grad_weight[:, WIDE:].reshape(shape)
        made[half, 2] = dot(cot_t[...], hidden).astype(bf16).reshape(shape)
        for copy in pass_half(group):
            copy.start()

    @pl.when(group == GROUPS - 1)
    def last():
        total = residual[...]
        block_output[...] = (total + ffn[...]).astype(bf16)
        inverse = lax.rsqrt(row_mean(total * total) + norm_epsilon)
        unit = total * inverse
        grad = grad_normed[...]
        gain_part[...] = jnp.sum(grad * unit, axis=0, keepdims=True)
        scaled = grad * gain
        result = cotangent[...].astype(f32) + inverse * (scaled - unit * row_mean(scaled * unit))
        grad_residual[...] = result
        low = result.astype(bf16)
        low_t = result.T.astype(bf16)
        for m in range(GROUPS):
            made_out[m] = dot(low_t, heads[m]).astype(bf16).reshape(made_out.shape[1:])
        pass_out().start()
        for m in range(GROUPS):
            grad_heads[m] = dot(low, w_out[m]).astype(bf16)

    @pl.when(group > 0)
    def join():
        before = group - 1
        for k, (copy, kept) in enumerate(zip(pass_half(before), (k_gate, k_up, k_down))):
            copy.wait_recv()
            own = made[before % 2, k, :, :, me["core"]].astype(f32)
            both = (own + twin[before, k].astype(f32)).astype(bf16)
            twin[before, k] = both
            kept[0] = both.reshape(kept.shape[1:])
        start_round(before)
        for copy in pass_half(before):
            copy.wait_send()

    @pl.when(group == GROUPS)
    def join_out():
        copy = pass_out()
        copy.wait_recv()
        for m in range(GROUPS):
            own = made_out[m, :, me["core"]].astype(f32)
            k_out[m] = (own + twin_out[m].astype(f32)).astype(bf16)
        copy.wait_send()
        end_round()


def token_block(heads, stream, cotangent, gains, w_gate, w_up, w_down, collective_id):
    tokens, width = stream.shape
    hidden, slim = WIDE, SLIM
    pairs = width // SHARE // 2
    whole = lambda shape: pl.BlockSpec(shape, lambda m: (0,) * len(shape))
    each = lambda cols: pl.BlockSpec((1, width, cols), lambda m: (group_at(jnp.minimum(m, GROUPS - 1)), 0, 0))
    w_out = pl.BlockSpec((GROUPS, width, SLIM), lambda m: (0, 0, WIDE // SLIM))
    kept = pl.BlockSpec((1, pairs, SHARE, hidden), lambda m: (group_at(jnp.maximum(m - 1, 0)), 0, 0, 0))
    flat = (tokens, width)
    vm = pltpu.VMEM
    return pl.pallas_call(
        token_kernel,
        grid=(GROUPS + 1,),
        in_specs=[whole(heads.shape), whole(flat), whole(flat), whole(gains.shape)]
        + [each(WIDE + SLIM), each(WIDE), each(WIDE), w_out],
        out_specs=[whole(flat), whole(flat), whole(heads.shape), whole((1, width))]
        + [kept] * 3
        + [whole((GROUPS, pairs, SHARE, slim))]
        + [ANY] * 12,
        out_shape=[
            jax.ShapeDtypeStruct(flat, bf16),
            jax.ShapeDtypeStruct(flat, f32),
            jax.ShapeDtypeStruct(heads.shape, bf16),
            jax.ShapeDtypeStruct((1, width), f32),
        ]
        + [jax.ShapeDtypeStruct((GROUPS, pairs, SHARE, hidden), bf16)] * 3
        + [jax.ShapeDtypeStruct((GROUPS, pairs, SHARE, slim), bf16)]
        + [
            jax.ShapeDtypeStruct(lead_shape(order[1:]) + (rows, hidden), bf16)
            for order in ORDERS[:3]
            for rows in (SHARE // 2, SHARE // 2, SHARE, SHARE)
        ],
        scratch_shapes=[
            vm(flat, f32), vm(flat, bf16), vm((width, tokens), bf16), vm((width, tokens), bf16),
            vm(flat, f32), vm(flat, f32),
            vm((2, 3, 4, 2, 2, SHARE, hidden), bf16), vm((GROUPS, 3, 4, 2, SHARE, hidden), bf16),
            vm((GROUPS, pairs, 2, SHARE, slim), bf16), vm((GROUPS, pairs, SHARE, slim), bf16),
            DMA((GROUPS, 3)), DMA((GROUPS, 3)), DMA((2,)),
            DMA((4, 4)), DMA((4, 4)), DMA((4, 8)), DMA((4, 8)), DMA((4, 2)), DMA((4, 2)),
        ],
        name="token_block",
        compiler_params=pltpu.CompilerParams(
            collective_id=collective_id, has_side_effects=True, vmem_limit_bytes=58 * MEGA
        ),
    )(heads, stream, cotangent, gains, w_gate, w_up, w_down, w_gate)


def gather_row_part(mover, me, whole):
    plus, minus, across = moved(me, "y", 1), moved(me, "y", -1), moved(me, "y", 2)
    far, sibling = moved(me, "x", 2), moved(me, "core", 1)

    def one(at, half=None):
        region = whole.at[at["y"], at["x"] // 2, at["core"]]
        return region if half is None else region.at[pl.ds(half * (SHARE // 2), SHARE // 2)]

    def column(at):
        return whole.at[:, at["x"] // 2, at["core"]]

    def pass_on(region, target):
        return mover.send(region, region, device_at(target))

    ring = pass_on(one(me), plus), pass_on(one(me), minus)
    yield
    mover.arrived(ring[0], one(minus))
    relay = [pass_on(one(minus, 0), plus)]
    mover.arrived(ring[1], one(plus))
    relay.append(pass_on(one(plus, 1), minus))
    yield
    mover.arrived(relay[0], one(across, 0))
    mover.arrived(relay[1], one(across, 1))
    half = pass_on(column(me), far)
    mirrors = [(pass_on(column(me), sibling), column(sibling))]
    yield
    mover.arrived(half, column(far))
    mirrors.append((pass_on(column(far), sibling), column(moved(far, "core", 1))))
    yield
    for slot, region in mirrors:
        mover.arrived(slot, region)


def front_kernel(
    lens, stream, gains, gate_up_weight, down_weight, out_weight, qkv_weight, first_values,
    cos_ref, sin_ref, freq,
    w_gate, w_up, w_down, w_rows, normed, q_ref, k_ref, v_ref, out_ref, lse_ref, heads,
    send_sems, recv_sems, local_sems, head_send, head_recv, vt, turns, w_qkv, s_gate, s_up, s_down, s_qkv,
):
    me = place()
    dp, mp = lax.axis_index("dp"), lax.axis_index("mp")
    mover = Mover(send_sems, recv_sems, local_sems)
    mover.anyone = device_at(moved(me, "core", 1))
    cols_to = [(dp, (mp + k) % MP) for k in range(1, MP)]
    others = [moved(me, axis, step) for axis in ("x", "y") for step in (1, -1)]
    others += [moved(me, "core", 1), moved(me, "x", 2)]
    units = down_weight.shape[1]
    for share, weight in (
        (s_gate, gate_up_weight[:, 0, :]), (s_up, gate_up_weight[:, 1, :]), (s_down, down_weight[...])
    ):
        share[...] = jnp.zeros_like(share)
        share[:, :units] = weight.astype(bf16)
    s_gate[:, WIDE:] = out_weight[...].astype(bf16)
    for k in range(3):
        s_qkv[:, k * PAIR : (k + 1) * PAIR] = qkv_weight[k].astype(bf16)
    w_qkv[me["y"], me["x"] // 2, me["core"]] = s_qkv[...]
    x = stream[...].astype(f32)
    unit = x * lax.rsqrt(row_mean(x * x) + norm_epsilon)
    normed[me["z"], me["x"] % 2] = (unit * gains[0:1, :]).astype(bf16)
    greet(cols_to + [device_at(end) for end in others])

    tokens = gather_tokens_part(mover, me, normed)
    row = gather_row_part(mover, me, w_qkv)
    gate = gather_part(mover, me, s_gate, w_gate, GATHER_ORDERS[0])
    up = gather_plain(mover, me, s_up, w_up, GATHER_ORDERS[1])
    down = gather_plain(mover, me, s_down, w_down, GATHER_ORDERS[2])
    every = gather_plain(mover, me, s_qkv, w_rows, ROW_ORDER)
    starts = doc_starts(lens)

    def step(*tasks):
        for task in tasks:
            next(task, None)

    step(gate, row, tokens, up, down, every)
    turn_tables(starts, freq[...], turns)
    vt[PAIR:, :] = jnp.ones((16, LEN), bf16)
    lse_ref[...] = jnp.zeros_like(lse_ref)
    step(gate, row, up, down, every)
    step(gate, row)
    step(tokens)
    step(gate, row)
    step(tokens, up, down, every)
    step(gate)
    step(tokens)
    step(gate, up, down)
    step(tokens, row, every)
    step(gate)
    step(tokens, up, down, every)
    step(gate)
    weights = w_qkv[...].reshape(DP * SHARE, 3 * PAIR)
    for block in range(BLOCKS):
        project_block(
            block, normed[block // 2, block % 2], weights, first_values, starts, turns,
            cos_ref, sin_ref, q_ref, k_ref, v_ref, vt,
        )
    for block in range(BLOCKS):
        attend_block(block, starts, q_ref, k_ref, vt, out_ref, lse_ref)
    copies = []
    for k in (5, 3, 4, 2, 6, 7, 1):
        taker = (mp + k) % MP
        copy = pltpu.make_async_remote_copy(
            src_ref=out_ref.at[pl.ds(pl.multiple_of(taker * BLOCK, BLOCK), BLOCK)],
            dst_ref=heads.at[mp],
            send_sem=head_send.at[k],
            recv_sem=head_recv.at[k],
            device_id=(dp, taker),
            device_id_type=MESH,
        )
        copy.start()
        copies.append(copy)
    heads[mp] = out_ref[pl.ds(pl.multiple_of(mp * BLOCK, BLOCK), BLOCK), :]
    step(up, down, gate, every)
    for k in range(1, MP):
        giver = (mp + MP - k) % MP
        pltpu.make_async_remote_copy(
            src_ref=heads.at[giver],
            dst_ref=heads.at[giver],
            send_sem=head_send.at[k],
            recv_sem=head_recv.at[k],
            device_id=(dp, giver),
            device_id_type=MESH,
        ).wait_recv()
    step(up, down)
    step(gate, up, down, every)
    step(every)
    for copy in copies:
        copy.wait_send()
    mover.finish()


def front(lens, stream, gains, weights, first_values, collective_id):
    gate_up, down, out, qkv = weights
    cos, sin = angle_tables()
    flat = jax.ShapeDtypeStruct((LEN, PAIR), bf16)
    vm = pltpu.VMEM
    widths = (WIDE + SLIM, WIDE, WIDE)
    slots = 40 + 3 * 16 + 13 + 8
    return pl.pallas_call(
        front_kernel,
        out_shape=[jax.ShapeDtypeStruct((4, 2, 4, 2, 2, SHARE, w), bf16) for w in widths + (3 * PAIR,)]
        + [
            jax.ShapeDtypeStruct((4, 2) + stream.shape, bf16),
            flat, flat, flat, flat,
            jax.ShapeDtypeStruct((8, LEN), f32),
            jax.ShapeDtypeStruct((MP, BLOCK, PAIR), bf16),
        ],
        in_specs=[SMEM] + [VMEM] * 10,
        out_specs=[ANY] * 4 + [VMEM] * 7,
        scratch_shapes=[
            DMA((slots,)), DMA((slots,)), DMA((4,)), DMA((MP,)), DMA((MP,)),
            vm((PAIR + 16, LEN), bf16), vm((2, 4 * BLOCKS, PAIR), f32),
        ]
        + [vm((4, 2, 2, SHARE, 3 * PAIR), bf16)]
        + [vm((SHARE, w), bf16) for w in widths + (3 * PAIR,)],
        name="front",
        compiler_params=pltpu.CompilerParams(
            collective_id=collective_id, has_side_effects=True, vmem_limit_bytes=56 * MEGA
        ),
    )(lens, stream, gains, gate_up, down, out, qkv, first_values, cos, sin, frequency_row())

newton_a = 3.4445
newton_b = -4.775
newton_c = 2.0315
OWNERS = (12, 2, 6, 10, 0, 4, 8)
COLUMNS = (SLIM, SLIM, SLIM, SLIM, WIDE, WIDE, WIDE)
ASPECTS = (8.0, 8.0, 8.0, 1.0, 1024 / 352, 1024 / 352, 1.0)


def halves(x):
    high = x.astype(bf16)
    return high, (x - high.astype(f32)).astype(bf16)


def left_side(x):
    high, low = halves(x)
    return jnp.concatenate([high, high, low], axis=1)


def right_side(x):
    high, low = halves(x)
    return jnp.concatenate([high, low, high], axis=0)


def newton_steps(stacked, result, gram, poly, total, moving, norm, left, right, wide_left):
    size = stacked.shape[-1]
    rows = DP * SHARE

    def held():
        return stacked[...].reshape(rows, size)

    def polynomial():
        one = gram[...]
        rank = lax.broadcasted_iota(jnp.int32, (size, size), 0)
        file = lax.broadcasted_iota(jnp.int32, (size, size), 1)
        left[0] = left_side(one)
        right[0] = right_side(one)
        poly[...] = (
            jnp.where(rank == file, newton_a, 0.0) + newton_b * one + newton_c * dot(left[0], right[0])
        )
        right[1] = right_side(poly[...])

    def advance():
        half = dot(left[0], right[1])
        gram[...] = dot(left_side(half), right[1])

    def gather():
        total[...] = dot(left_side(total[...]), right[1])

    def begin():
        block = held()
        wide = block.astype(f32)
        length = jnp.sqrt(jnp.sum(wide * wide)) + 1e-07
        inverse = jnp.full((1, size), 1.0, f32) / length
        norm[0:1, :size] = inverse
        turned = wide.T.astype(bf16)
        gram[...] = dot(turned, block) * (inverse * inverse)

    def first():
        polynomial()
        total[...] = poly[...]

    def middle():
        high, low = halves(total[...])
        block = held()
        moving[...] = (dot(block, high) + dot(block, low)) * norm[0:1, :size]

    def regram():
        now = moving[...]
        high, low = halves(now)
        wide_left[...] = jnp.concatenate([high, high, low], axis=1)
        turned = now.T
        turned_high, turned_low = halves(turned)
        gram[...] = dot(turned_high, high) + (dot(turned_high, low) + dot(turned_low, high))

    def end():
        ending = dot(wide_left[...], right_side(total[...]))
        result[...] = ending.astype(bf16).reshape(DP, SHARE, size)

    return [
        begin, first, advance, polynomial, gather, middle, regram,
        first, advance, polynomial, gather, advance, polynomial, gather, end,
    ]


def newton_scratch(size):
    square = pltpu.VMEM((size, size), f32)
    return [
        square, square, square, pltpu.VMEM((DP * SHARE, size), f32), pltpu.VMEM((8, size), f32),
        pltpu.VMEM((1, size, 3 * size), bf16), pltpu.VMEM((2, 3 * size, size), bf16),
        pltpu.VMEM((DP * SHARE, 3 * size), bf16),
    ]


def link(src, dst, send, recv, device):
    return pltpu.make_async_remote_copy(
        src_ref=src, dst_ref=dst, send_sem=send, recv_sem=recv, device_id=device, device_id_type=MESH
    )


def back_kernel(
    lens, q_ref, k_ref, v_ref, heads_ref, lse_ref, grad_parts, all_normed, cos_ref, sin_ref, freq,
    k_gate, k_up, k_down, k_out, all_rows, *rest,
):
    landed, rest = [rest[4 * k : 4 * k + 4] for k in range(3)], rest[12:]
    (
        qkv_momentum,
    out_momentum, gate_up_momentum, down_momentum,
        stream, gain_two,
        values_grad, m_qkv, m_out, m_gate, m_up, m_down, o_q, o_k, o_v, o_out, o_gate, o_up, o_down,
        summed, gain_grad,
        send_sems, recv_sems, local_sems, head_send, head_recv, dp_send, dp_recv, own_send, own_recv,
        back_send, back_recv, all_send, all_recv, proj_send, proj_recv,
        turns, grad_heads, kt, dqt, delta, dproj_t, dproj, dproj_in, w_rows, g_qkv, normed,
        dp_land, qkv_share, wide_share, slim_share, wide_in, wide_out, slim_in, slim_out,
        gain_dp, gain_mp, *own_lands,
    ) = rest
    newton, own_lands = own_lands[:16], own_lands[16:]
    mover = Mover(send_sems, recv_sems, local_sems)
    me = place()
    dp, mp = lax.axis_index("dp"), lax.axis_index("mp")
    mover.anyone = device_at(moved(me, "core", 1))
    rows_to = [((dp + k) % DP, mp) for k in range(1, DP)]
    cols_to = [(dp, (mp + k) % MP) for k in range(1, MP)]
    kept_from = (k_gate, k_up, k_down, k_out)
    scratch = [own_lands[13 * index : 13 * (index + 1)] for index in range(4)]
    loads = [mover.local(source, own[0]) for source, own in zip(kept_from, scratch)]
    early = []
    for sources, own in zip(landed, scratch):
        up, down, from_minus, from_plus = own[1:5]
        early.append(
            [
                mover.local(source, target)
                for source, target in (
                    (sources[0], up), (sources[1], down),
                    (half_of(sources[2], 1), half_of(from_minus, 1)),
                    (half_of(sources[3], 0), half_of(from_plus, 0)),
                )
            ]
        )
    loads += [mover.local(all_rows, w_rows), mover.local(all_normed, normed)]
    greet(rows_to + cols_to + [device_at(moved(me, "x", step)) for step in (1, -1)])

    def rows_of(index):
        return pl.ds(pl.multiple_of(index * BLOCK, BLOCK), BLOCK)

    head_copies = []
    for k in (5, 3, 4, 2, 6, 7, 1):
        taker = (mp + k) % MP
        copy = link(
            grad_parts.at[taker], grad_heads.at[rows_of(mp)], head_send.at[k], head_recv.at[k], (dp, taker)
        )
        copy.start()
        head_copies.append(copy)
    grad_heads[rows_of(mp), :] = grad_parts[mp]

    sums = (m_gate, m_up, m_down, m_out)
    scatters = []
    for index in range(4):
        own = scratch[index]
        phases = [own[1 + 4 * phase : 5 + 4 * phase] for phase in range(3)]
        scatters.append(scatter_part(mover, me, own[0], phases, sums[index], ORDERS[index], index < 3))

    def step(*tasks):
        for task in tasks:
            next(task, None)

    for index in (3, 0, 1, 2):
        loads[index].wait()
        for copy in early[index] if index < 3 else ():
            copy.wait()
        step(scatters[index])
    starts = doc_starts(lens)
    turn_tables(starts, freq[...], turns)
    for k in range(1, MP):
        giver = (mp + MP - k) % MP
        region = grad_heads.at[rows_of(giver)]
        link(region, region, head_send.at[k], head_recv.at[k], (dp, giver)).wait_recv()
    attention = attend_back(
        starts, q_ref, k_ref, v_ref, heads_ref, grad_heads, lse_ref, normed, cos_ref, sin_ref,
        turns, values_grad, g_qkv, dproj, kt, dqt, delta, dproj_t,
    )

    def pass_rows(block):
        return link(
            dproj.at[block], dproj_in.at[mp], proj_send.at[block], proj_recv.at[mp], (dp, block)
        )

    step(attention)
    for block in range(BLOCKS):
        step(attention)

        @pl.when(mp != block)
        def away():
            pass_rows(block).start()

        @pl.when(mp == block)
        def here():
            dproj_in[mp] = dproj[block]

        if block in (0, 2, 4, 6, 7):
            step(*scatters)
    loads[5].wait()
    step(attention)
    dp_copies = []
    for k in range(1, DP):
        taker = (dp + k) % DP
        copy = link(g_qkv.at[taker], dp_land.at[dp], dp_send.at[k], dp_recv.at[k], (taker, mp))
        copy.start()
        dp_copies.append(copy)
    dp_land[dp] = g_qkv[dp]
    step(*scatters)
    step(*scatters)

    results = (o_q, o_k, o_v, o_out, o_gate, o_up, o_down)

    def give(index, share):
        owner = OWNERS[index]
        land = wide_in if COLUMNS[index] == WIDE else slim_in
        copy = link(share, land.at[dp], own_send.at[index], own_recv.at[dp], (owner, mp))

        @pl.when(dp != owner)
        def away():
            copy.start()

        @pl.when(dp == owner)
        def here():
            land[dp] = share[...]

        return owner, copy

    def settle(given):
        owner, copy = given

        @pl.when(dp != owner)
        def away():
            copy.wait_send()

    def take(index):
        land = wide_in if COLUMNS[index] == WIDE else slim_in
        for k in range(1, DP):
            giver = (dp + k) % DP
            region = land.at[giver]
            link(region, region, own_send.at[index], own_recv.at[giver], (giver, mp)).wait_recv()

    def returns(index, wait):
        made = wide_out if COLUMNS[index] == WIDE else slim_out
        for k in range(1, DP):
            taker = (dp + k) % DP
            copy = link(made.at[taker], results[index], back_send.at[taker], back_recv.at[index], (taker, mp))
            copy.wait_send() if wait else copy.start()

    def owned(columns):
        chosen = [i for i in range(len(OWNERS)) if COLUMNS[i] == columns]
        if columns == WIDE:
            steps = newton_steps(wide_in, wide_out, *newton[:8])
        else:
            steps = newton_steps(slim_in, slim_out, *newton[8:])
        mine = functools.reduce(jnp.logical_or, [dp == OWNERS[i] for i in chosen])
        for index in chosen:
            pl.when(dp == OWNERS[index])(functools.partial(take, index))
        for one in steps:
            pl.when(mine)(one)
            yield
        for index in chosen:
            pl.when(dp == OWNERS[index])(functools.partial(returns, index, False))

            @pl.when(dp == OWNERS[index])
            def keep():
                made = wide_out if COLUMNS[index] == WIDE else slim_out
                results[index][...] = made[dp]

    units = down_momentum.shape[1]
    m_out[...] += 0.5 * out_momentum[...]
    m_gate[:, :units] += 0.5 * gate_up_momentum[:, 0, :]
    m_up[:, :units] += 0.5 * gate_up_momentum[:, 1, :]
    m_down[:, :units] += 0.5 * down_momentum[...]
    slim_share[...] = m_out[...].astype(bf16)
    for k, moment in enumerate((m_gate, m_up, m_down)):
        wide_share[k] = moment[...].astype(bf16)
    given = [give(4 + k, wide_share.at[k]) for k in range(3)] + [give(3, slim_share)]

    def gains_task():
        loads[4].wait()
        for k in range(1, MP):
            giver = (mp + k) % MP
            region = dproj_in.at[giver]
            link(region, region, proj_send.at[0], proj_recv.at[giver], (dp, giver)).wait_recv()
        grad_normed = jnp.zeros(summed.shape, f32)
        for m in range(MP):
            grad_normed = grad_normed + dot_t(dproj_in[m], w_rows[m])
        summed[...] = grad_normed
        x = stream[...].astype(f32)
        unit = x * lax.rsqrt(row_mean(x * x) + norm_epsilon)
        gain_dp[dp] = jnp.concatenate(
            [jnp.sum(grad_normed * unit, axis=0, keepdims=True), gain_two[...]], axis=0
        )
        copies = []
        for k in range(1, DP):
            copy = link(
                gain_dp.at[dp], gain_dp.at[dp], all_send.at[k], all_recv.at[k], ((dp + k) % DP, mp)
            )
            copy.start()
            copies.append(copy)
        yield
        for k in range(1, DP):
            giver = (dp + DP - k) % DP
            region = gain_dp.at[giver]
            link(region, region, all_send.at[k], all_recv.at[k], (giver, mp)).wait_recv()
        total = gain_dp[0]
        for k in range(1, DP):
            total = total + gain_dp[k]
        gain_mp[mp] = total
        for k in range(1, MP):
            copy = link(
                gain_mp.at[mp], gain_mp.at[mp], all_send.at[DP + k], all_recv.at[DP + k], (dp, (mp + k) % MP)
            )
            copy.start()
            copies.append(copy)
        yield
        for k in range(1, MP):
            giver = (mp + MP - k) % MP
            region = gain_mp.at[giver]
            link(region, region, all_send.at[DP + k], all_recv.at[DP + k], (dp, giver)).wait_recv()
        total = gain_mp[0]
        for k in range(1, MP):
            total = total + gain_mp[k]
        gain_grad[...] = total
        for copy in copies:
            copy.wait_send()

    def qkv_task():
        for k in range(1, DP):
            giver = (dp + DP - k) % DP
            region = dp_land.at[giver]
            link(region, region, dp_send.at[k], dp_recv.at[k], (giver, mp)).wait_recv()
        total = jnp.zeros((SHARE, WIDE), f32)
        for k in range(DP):
            total = total + dp_land[k].astype(f32)
        for k in range(3):
            cols = slice(k * SLIM, (k + 1) * SLIM)
            moment = 0.5 * qkv_momentum[k] + total[:, cols]
            m_qkv[:, cols] = moment
            qkv_share[k] = moment.astype(bf16)
        given.extend(give(k, qkv_share.at[k]) for k in range(3))
        yield
        yield from owned(SLIM)

    gains, sums_task, wide_task = gains_task(), qkv_task(), owned(WIDE)
    step(gains)
    step(sums_task)
    for _ in range(8):
        step(wide_task)
    step(gains)
    for _ in range(8):
        step(wide_task)
    for _ in range(16):
        step(sums_task)
    step(gains)
    for index, owner in enumerate(OWNERS):

        @pl.when(dp != owner)
        def arrive():
            link(
                results[index], results[index], back_send.at[0], back_recv.at[index], (owner, mp)
            ).wait_recv()

        pl.when(dp == owner)(functools.partial(returns, index, True))
    for copy in head_copies + dp_copies:
        copy.wait_send()
    for block in range(BLOCKS):

        @pl.when(mp != block)
        def sent():
            pass_rows(block).wait_send()

    for one in given:
        settle(one)
    mover.finish()


def back_block(
    lens, q, k, v, heads_out, lse, grad_parts, normed, kept, all_rows, landed, momenta, stream, gain_two, collective_id,
):
    cos, sin = angle_tables()
    tokens, width = stream.shape
    vm = pltpu.VMEM
    slim, wide = (jax.ShapeDtypeStruct((SHARE, c), bf16) for c in (SLIM, WIDE))
    full = jax.ShapeDtypeStruct((SHARE, WIDE), f32)
    lands = []
    for index, source in enumerate(kept):
        rows, cols = source.shape[-2:]
        lands.append(vm(source.shape, bf16))
        for phase in range(3):
            lead = lead_shape(ORDERS[index][phase + 1 :])
            lands += [vm(lead + (rows // 2, cols), bf16)] * 2 + [vm(lead + (rows, cols), bf16)] * 2
    slots = 18 * len(kept)
    return pl.pallas_call(
        back_kernel,
        out_shape=[
            jax.ShapeDtypeStruct((LEN, PAIR), f32),
            full, jax.ShapeDtypeStruct((SHARE, SLIM), f32), full, full, full,
            slim, slim, slim, slim, wide, wide, wide,
            jax.ShapeDtypeStruct((tokens, width), f32),
            jax.ShapeDtypeStruct((2, width), f32),
        ],
        in_specs=[SMEM] + [VMEM] * 6 + [ANY] + [VMEM] * 3 + [ANY] * 17 + [VMEM] * 6,
        out_specs=[VMEM] * 15,
        scratch_shapes=[
            DMA((slots,)), DMA((slots,)), DMA((19,)), DMA((MP,)), DMA((MP,)),
            DMA((DP,)), DMA((DP,)), DMA((7,)), DMA((DP,)), DMA((DP,)), DMA((7,)),
            DMA((DP + MP,)), DMA((DP + MP,)), DMA((MP,)), DMA((MP,)),
            vm((2, 4 * BLOCKS, PAIR), f32), vm((LEN, PAIR), bf16),
            vm((PAIR, LEN), bf16), vm((PAIR, LEN), f32), vm((8, LEN), f32),
            vm((3 * PAIR, LEN), bf16), vm((BLOCKS, BLOCK, 3 * PAIR), bf16), vm((MP, BLOCK, 3 * PAIR), bf16),
            vm((MP, width, 3 * PAIR), bf16), vm((DP, SHARE, WIDE), bf16),
            vm((4, 2, tokens, width), bf16),
            vm((DP, SHARE, WIDE), bf16), vm((3, SHARE, SLIM), bf16), vm((3, SHARE, WIDE), bf16),
            vm((SHARE, SLIM), bf16),
            vm((DP, SHARE, WIDE), bf16), vm((DP, SHARE, WIDE), bf16),
            vm((DP, SHARE, SLIM), bf16), vm((DP, SHARE, SLIM), bf16),
            vm((DP, 2, width), f32), vm((MP, 2, width), f32),
        ]
        + newton_scratch(WIDE)
        + newton_scratch(SLIM)
        + lands,
        name="back",
        compiler_params=pltpu.CompilerParams(
            collective_id=collective_id, has_side_effects=True, vmem_limit_bytes=60 * MEGA
        ),
    )(
        lens, q, k, v, heads_out, lse, grad_parts, normed, cos, sin, frequency_row(),
        *kept, all_rows, *landed, *momenta, stream, gain_two,
    )

STEP = 10
muon_rate = 1.0
out_rate = 4.0
adam_rate = 0.8
beta_first = 0.9
beta_second = 0.95
adam_epsilon = 1e-08


def final_kernel(
    values_grad, m_qkv, m_out, m_gate, m_up, m_down, o_q, o_k, o_v, o_out, o_gate, o_up, o_down,
    summed, gain_grad, stream, grad_residual, gains, moment1, moment2,
    qkv_weight, out_weight, gate_up_weight, down_weight,
    input_grad, values_out, qkv_new, qkv_moment, out_new, out_moment, gate_up_new, gate_up_moment,
    down_new, down_moment, moment1_new, moment2_new, gains_new,
):
    units = down_weight.shape[1]
    tall = muon_rate * (stream.shape[1] / SLIM) ** 0.5
    broad = muon_rate * (stream.shape[1] / units) ** 0.5
    for k, orth in enumerate((o_q, o_k, o_v)):
        qkv_moment[k] = m_qkv[:, k * SLIM : (k + 1) * SLIM]
        qkv_new[k] = qkv_weight[k] - tall * orth[...].astype(f32)
    out_moment[...] = m_out[...]
    out_new[...] = out_weight[...] - out_rate * o_out[...].astype(f32)
    for k, (moment, orth) in enumerate(((m_gate, o_gate), (m_up, o_up))):
        gate_up_moment[:, k, :] = moment[:, :units]
        gate_up_new[:, k, :] = gate_up_weight[:, k, :] - broad * orth[:, :units].astype(f32)
    down_moment[...] = m_down[:, :units]
    down_new[...] = down_weight[...] - muon_rate * o_down[:, :units].astype(f32)
    values_out[...] = values_grad[...]
    x = stream[...].astype(f32)
    inverse = lax.rsqrt(row_mean(x * x) + norm_epsilon)
    unit = x * inverse
    scaled = summed[...] * gains[0:1, :]
    input_grad[...] = grad_residual[...] + inverse * (scaled - unit * row_mean(scaled * unit))
    grad = gain_grad[...]
    first = beta_first * moment1[...] + (1.0 - beta_first) * grad
    second = beta_second * moment2[...] + (1.0 - beta_second) * grad * grad
    moment1_new[...] = first
    moment2_new[...] = second
    corrected1 = first / (1.0 - beta_first**STEP)
    corrected2 = second / (1.0 - beta_second**STEP)
    gains_new[...] = gains[...] - adam_rate * corrected1 / (jnp.sqrt(corrected2) + adam_epsilon)


def final_block(values_grad, *rest):
    args = (values_grad,) + rest
    stream, residual, gains = rest[14], rest[15], rest[16]
    weights = rest[19:]
    like = lambda x: jax.ShapeDtypeStruct(x.shape, f32)
    return pl.pallas_call(
        final_kernel,
        out_shape=[like(residual), like(values_grad)]
        + [like(w) for weight in weights for w in (weight, weight)]
        + [like(gains)] * 3,
        in_specs=[VMEM] * len(args),
        out_specs=[VMEM] * 13,
        name="final",
        compiler_params=pltpu.CompilerParams(vmem_limit_bytes=56 * MEGA),
    )(*args)
def on_device(
    block_input, first_values, out_cotangent, doc_lengths, norm_gains, gain_moment1, gain_moment2,
    qkv_weight, qkv_momentum, out_weight, out_momentum, gate_up_weight, gate_up_momentum,
    down_weight, down_momentum,
):
    tokens, width = block_input.shape
    qkv_weight, qkv_momentum = (a.transpose(1, 0, 2) for a in (qkv_weight, qkv_momentum))
    out_weight, out_momentum, down_weight, down_momentum = (
        a.T for a in (out_weight, out_momentum, down_weight, down_momentum)
    )
    *wholes, all_rows, normed, q, k, v, heads_out, lse, heads = front(
        doc_lengths, block_input, norm_gains,
        (gate_up_weight, down_weight, out_weight, qkv_weight), first_values, 0,
    )
    w_gate, w_up, w_down = (w.reshape(GROUPS, width, w.shape[-1]) for w in wholes)
    block_output, grad_residual, grad_heads, gain_two, *rest = token_block(
        heads, block_input, out_cotangent, norm_gains, w_gate, w_up, w_down, 1
    )
    kept, landed = rest[:4], rest[4:]
    done = back_block(
        doc_lengths, q, k, v, heads_out, lse, grad_heads, normed,
        [g.reshape(4, 2, 4, 2, SHARE, g.shape[-1]) for g in kept],
        all_rows.reshape(GROUPS, width, all_rows.shape[-1]),
        landed,
        (qkv_momentum, out_momentum, gate_up_momentum, down_momentum),
        block_input, gain_two, 2,
    )
    (
        input_grad, values_grad, qkv_new, qkv_moment, out_new, out_moment,
        gate_up_new, gate_up_moment, down_new, down_moment, *gains_out,
    ) = final_block(
        *done, block_input, grad_residual, norm_gains, gain_moment1, gain_moment2,
        qkv_weight, out_weight, gate_up_weight, down_weight,
    )
    return (
        block_output, input_grad, values_grad,
        qkv_new.transpose(1, 0, 2), qkv_moment.transpose(1, 0, 2), out_new.T, out_moment.T,
        gate_up_new, gate_up_moment, down_new.T, down_moment.T, *gains_out,
    )


def solution(mesh):
    placed = (
        P(("dp", "mp"), None), P("dp", "mp"), P(("dp", "mp"), None), P("dp", None),
        P(), P(), P(),
        P("dp", None, "mp"), P("dp", None, "mp"), P("mp", "dp"), P("mp", "dp"),
        P("dp", None, "mp"), P("dp", None, "mp"), P("mp", "dp"), P("mp", "dp"),
    )
    return jax.shard_map(
        on_device,
        mesh=mesh,
        in_specs=placed,
        out_specs=(P(("dp", "mp"), None), P(("dp", "mp"), None), P("dp", "mp")) + placed[7:] + (P(),) * 3,
        check_vma=False,
    )
```
